128 devices in a mesh: slab: 8 (over x_hi, z), col: 16 (over x_lo, y, core).
Axes of the slice: x: 4 (x_hi: 2, x_lo: 2; x = x_hi * 2 + x_lo), y: 4, z: 4, core: 2. Of those that a mesh axis runs over, the one named last changes fastest.
Arguments:
- volume: bfloat16 [64, 2097152], P('slab', 'col'), may hold values from -6 to 6
- consensus: bfloat16 [64, 2097152], P('slab', 'col'), may hold values from -6 to 6
- templates: bfloat16 [128, 1024, 128], P('col'), may hold values from -0.015625 to 0.015625
- pattern: int32 [16, 256, 8, 8], P('col'), may hold values from 0 to 1023
- probe_wave: float32 [2, 64, 64], replicated, may hold values from -6 to 6
- measured: float32 [256, 128, 64, 64], P(('slab', 'col')), may hold values from 0.1 to 4
- scan_counts: int32 [256], replicated, may hold values from 1 to 128, as said below
- scan_positions: int32 [256, 128], replicated, may hold values from 0 to 960
Outputs:
- updated: float32 [64, 2097152], P('slab', 'col')
The draws below stay inside these ranges and needn't reach their ends.
Inputs may be any that keep to these rules, and one draw needn't show every extreme that they name: scan_counts[a] positions are used at angle a; 128 is reached by some angle in every draw. `scan_positions`: only the first scan_counts[a] entries of row a are used. `pattern`: entry t * 8 + k names template k of the column group applied to its volume tile t.
All inputs are finite; a program needn't handle non-finite values.
Results may differ from the reference program's by a relative error of at most 0.0044.
Values may be sent and summed in bfloat16 or wider, within the bound.
A program may use at most 128 MiB of HBM per device.

```python
import math
import jax
import jax.numpy as jnp
from jax import lax

PR = 64
NZ = 64
W = 1024
DT = 128
ND = 8
VT = 1024
VC = 131072
NT = 128
CELLS = 2097152
K = 8
S = 8
A = 256
PMAX = 128
N_COL = 16


def draw_scan_counts(key, part):
    key = jax.random.fold_in(key, 7)
    key_shift, key_jitter = jax.random.split(key)
    angle_index = jnp.arange(A, dtype=jnp.int32)
    phase_shift = jax.random.randint(key_shift, (), 0, A, dtype=jnp.int32)
    ramp_value = jnp.abs((angle_index + phase_shift) % A * 2 - A)
    floor_count = max(PMAX // 16, 1)
    base_count = floor_count + (PMAX - floor_count) * ramp_value * ramp_value // (A * A)
    jitter = jax.random.randint(key_jitter, (A,), 0, max(PMAX // 8, 1), dtype=jnp.int32)
    return jnp.minimum(base_count + jitter, PMAX)


def touch_ends(values, stream_key, low, top_value):
    index_at = [jax.random.randint(jax.random.fold_in(stream_key, axis), (), 0, length) for axis, length in enumerate(values.shape)]
    widest = values.shape.index(max(values.shape))
    neighbour = index_at[:widest] + [(index_at[widest] + 1) % values.shape[widest]] + index_at[widest + 1:]
    return values.at[tuple(index_at)].set(low).at[tuple(neighbour)].set(top_value)


def steps_of(rng, shape, pieces, smallest, top_value):
    def one(position, blocks):
        draws = jax.random.uniform(jax.random.fold_in(jax.random.fold_in(rng, 6), position), (blocks,), jnp.float32, smallest / len(pieces), top_value / len(pieces))
        return jnp.repeat(jnp.exp(draws), shape[position] // blocks).reshape((-1,) + (1,) * (len(shape) - position - 1))

    gain = one(*pieces[0])
    for cut in pieces[1:]:
        gain = gain * one(*cut)
    return gain


def centred(own_key, dims, scale, limit, pieces=(), kind=jnp.bfloat16):
    array = scale * jax.random.normal(own_key, dims, jnp.float32)
    if pieces:
        array = array * steps_of(own_key, dims, pieces, -0.22, 0.18)
    return jnp.clip(array, -limit, limit).astype(kind)


def setup_inputs(seed: int = 0) -> dict:
    splits = jax.random.split(jax.random.key(seed), 9)
    return {
        "volume": centred(splits[0], (NZ, CELLS), 1.0, 6.0, ((0, 8), (1, 16))),
        "consensus": centred(splits[1], (NZ, CELLS), 1.0, 6.0, ((0, 8), (1, 16))),
        "templates": centred(splits[2], (N_COL * K, VT, DT), (S * VT * N_COL) ** -0.5, 0.015625, ((0, 16),)),
        "pattern": touch_ends(jax.random.randint(splits[3], (N_COL, A, ND, S), 0, NT * K), jax.random.fold_in(splits[3], 1), 0, (NT * K) - 1).astype(jnp.int32),
        "probe_wave": centred(splits[4], (2, PR, PR), 1.0, 6.0, (), jnp.float32),
        "measured": jnp.clip(jnp.exp(math.log(4.0) - 3.6888794 * jax.random.uniform(splits[5], (A, PMAX, PR, PR), jnp.float32) ** steps_of(splits[5], (A, PMAX, PR, PR), ((0, 128),), -0.2, 0.2)), 0.1, 4.0),
        "scan_counts": draw_scan_counts(jax.random.fold_in(splits[8], 71), 0),
        "scan_positions": touch_ends(jax.random.randint(splits[7], (A, PMAX), 0, W - PR + 1), jax.random.fold_in(splits[7], 1), 0, W - PR).astype(jnp.int32),
    }


step_size = 0.1
penalty = 1.0

def reference(volume, consensus, templates, pattern, probe_wave, measured, scan_counts, scan_positions):
    volume_tiles = volume.reshape(NZ, N_COL, NT, VT).transpose(1, 0, 2, 3)
    group_tables = templates.reshape(N_COL, K, VT, DT)

    def project(carry, inputs):
        tiles_here, tables_here, layout = inputs
        tile_table = jnp.einsum('ztv,kvd->ztkd', tiles_here.astype(jnp.float32), tables_here.astype(jnp.float32))
        tile_table = tile_table.astype(jnp.bfloat16).reshape(NZ, NT * K, DT)
        for member in range(S):
            carry = carry + jnp.take(tile_table, layout[:, :, member].reshape(-1), axis=1).astype(jnp.float32)
        return (carry, None)
    phase, _ = lax.scan(project, jnp.zeros((NZ, A * ND, DT), jnp.float32), (volume_tiles, group_tables, pattern))
    phase = phase.reshape(NZ, A, W).transpose(1, 0, 2)
    wave = lax.complex(probe_wave[0], probe_wave[1])
    offsets = jnp.arange(PR, dtype=jnp.int32)
    slot_range = jnp.arange(PMAX, dtype=jnp.int32)

    def angle_grad(inputs):
        image, observed, live_count, starts = inputs
        columns = (starts[:, None] + offsets[None, :]).reshape(-1)
        patch_phase = jnp.take(image, columns, axis=1).reshape(NZ, PMAX, PR).transpose(1, 0, 2)
        exit_wave = wave * lax.complex(jnp.cos(patch_phase), jnp.sin(patch_phase))
        spectrum = jnp.fft.fft2(exit_wave, norm='ortho')
        residual = jnp.real(spectrum) * jnp.real(spectrum) + jnp.imag(spectrum) * jnp.imag(spectrum) - observed
        back_wave = jnp.fft.ifft2(residual * spectrum, norm='ortho')
        patch_grad = 2.0 * jnp.imag(jnp.conj(exit_wave) * back_wave)
        patch_grad = jnp.where((slot_range < live_count)[:, None, None], patch_grad, 0.0)
        gradient = jnp.zeros((NZ, W), jnp.float32).at[:, columns].add(patch_grad.transpose(1, 0, 2).reshape(NZ, PMAX * PR))
        return gradient.astype(jnp.bfloat16)
    angle_grads = lax.map(angle_grad, (phase, measured, scan_counts, scan_positions))
    rows_data = angle_grads.reshape(A, NZ, ND, DT).transpose(0, 2, 1, 3).reshape(A * ND, NZ * DT).astype(jnp.float32)

    def backproject(inputs):
        tables_here, layout = inputs
        summed = jnp.zeros((NT * K, NZ * DT), jnp.float32)
        for member in range(S):
            summed = summed + jax.ops.segment_sum(rows_data, layout[:, :, member].reshape(-1), num_segments=NT * K)
        rounded = summed.astype(jnp.bfloat16).reshape(NT, K, NZ, DT)
        result = jnp.einsum('tkzd,kvd->ztv', rounded.astype(jnp.float32), tables_here.astype(jnp.float32))
        return result.reshape(NZ, VC)
    spread_back = lax.map(backproject, (group_tables, pattern))
    backproj = spread_back.transpose(1, 0, 2).reshape(NZ, CELLS)
    volume_f32 = volume.astype(jnp.float32)
    return volume_f32 - step_size * (backproj + penalty * (volume_f32 - consensus.astype(jnp.float32)))
```

```python
import functools
import math

import jax
import jax.numpy as jnp
import numpy as np
from jax import lax
from jax.experimental import pallas as pl
from jax.experimental.pallas import tpu as pltpu
from jax.sharding import PartitionSpec as P

BF16 = jnp.bfloat16
F32 = jnp.float32
GROUP = 8
step_size = 0.1
penalty = 1.0


def trig_coefficients():
    grid = (np.cos(np.pi * (np.arange(400) + 0.5) / 400) + 1.0) * (np.pi * np.pi * 0.5005)
    root = np.sqrt(grid)
    sine = np.polynomial.Polynomial.fit(grid, np.sin(root) / root, 6).convert().coef
    cosine = np.polynomial.Polynomial.fit(grid, np.cos(root), 7).convert().coef
    return [float(v) for v in sine], [float(v) for v in cosine]


def sine_cosine(angle):
    sine, cosine = trig_coefficients()
    square = angle * angle
    sine_value = jnp.full_like(square, sine[-1])
    for value in sine[-2::-1]:
        sine_value = sine_value * square + value
    cosine_value = jnp.full_like(square, cosine[-1])
    for value in cosine[-2::-1]:
        cosine_value = cosine_value * square + value
    return sine_value * angle, cosine_value


def split_bf16(table):
    high = table.astype(np.float32).astype(BF16)
    low = (table - high.astype(np.float64)).astype(np.float32).astype(BF16)
    return high, low


def transform_tables(size):
    index = np.arange(size)
    radians = 2.0 * np.pi / size * (index[:, None] * index[None, :] % size)
    cosine = np.cos(radians) / math.sqrt(size)
    sine = np.sin(radians) / math.sqrt(size)
    zero = np.zeros_like(cosine)
    forward = np.block([[cosine, -sine], [sine, cosine]])
    pair = np.block([[cosine, zero, sine, zero], [zero, cosine, zero, sine]])
    back = np.block([[2 * sine, -2 * cosine], [2 * cosine, 2 * sine]])
    f_high, f_low = split_bf16(forward)
    p_high, p_low = split_bf16(pair)
    b_high, b_low = split_bf16(back)
    lanes = np.concatenate([f_high, f_low], 1)
    return (
        np.concatenate([lanes, lanes], 0),
        np.concatenate([p_high, p_high], 0),
        p_low,
        np.concatenate([b_high, b_low], 1),
    )


def halves(value):
    high = value.astype(BF16)
    low = (value - high.astype(F32)).astype(BF16)
    return high, low


def dot(left, right):
    return jnp.dot(left, right, preferred_element_type=F32)


def ptycho_kernel(
    counts, starts, image, probe_a, probe_b, t_first, t_pair, t_pair_low, t_back, measured,
    out, waves, total, staged, observed,
):
    slots, size, _, limit = measured.shape
    width = waves.shape[0]
    tile = image.shape[1]
    rows = width // tile * slots
    chunk_count = limit // GROUP

    def used_chunks(slot):
        return jnp.clip(lax.div(counts[slot] + (GROUP - 1), GROUP), 0, chunk_count)

    half = size // 2

    @pl.loop(0, slots)
    def _(slot):
        for row in range(half):
            both = jnp.concatenate([measured[slot, row], measured[slot, row + half]], 0)
            observed[slot, pl.ds(row, limit, half), :] = both.T

    staged[...] = image[...].astype(jnp.int32).astype(F32) * (2 * math.pi / 65536)
    lane = lax.broadcasted_iota(jnp.int32, (size, 2 * size), 1)

    @pl.loop(0, slots)
    def _(slot):
        for part in range(width // tile):
            sine, cosine = sine_cosine(staged[pl.ds(slot * (width // tile) + part, size, rows), :])
            waves[part * tile : (part + 1) * tile, :] = jnp.concatenate([cosine, sine], 0).T
        total[...] = jnp.zeros_like(total)
        count = counts[slot]

        @pl.loop(0, used_chunks(slot))
        def _(chunk):
            begin = chunk * GROUP
            at = [starts[slot, begin + member] for member in range(GROUP)]
            exits = []
            for member in range(GROUP):
                patch = waves[pl.ds(at[member], size), :]
                exits.append(probe_a[...] * patch + probe_b[...] * pltpu.roll(patch, size, 1))
            exit_wave = jnp.concatenate(exits, 0)
            high, low = halves(exit_wave)
            first = dot(jnp.concatenate([high, low], 1), t_first[...])
            first = first[:, : 2 * size] + first[:, 2 * size :]
            turned = jnp.concatenate(
                [first[pair * 2 * size : (pair + 1) * 2 * size].T for pair in range(GROUP // 2)], 0
            )
            high, low = halves(turned)
            second = dot(jnp.concatenate([high, low], 1), t_pair[...])
            second = second + dot(high, t_pair_low[...])
            scaled = []
            for pair in range(GROUP // 2):
                block = second[pair * 2 * size : (pair + 1) * 2 * size]
                real = block[:size, : 2 * size] + block[size:, 2 * size :]
                imag = block[size:, : 2 * size] - block[:size, 2 * size :]
                member = begin + 2 * pair
                seen = [
                    observed[slot, pl.ds(pl.multiple_of((member + m) * half, half), half), :]
                    for m in range(2)
                ]
                seen = jnp.concatenate(
                    [
                        jnp.concatenate([seen[0][:, :size], seen[1][:, :size]], 1),
                        jnp.concatenate([seen[0][:, size:], seen[1][:, size:]], 1),
                    ],
                    0,
                )
                residual = real * real + imag * imag - seen
                live = member + jnp.where(lane >= size, 1, 0) < count
                residual = jnp.where(live, residual, 0.0)
                scaled += [residual * real, residual * imag]
            third = dot(jnp.concatenate(scaled, 0).astype(BF16), t_pair[: 2 * size, :])
            turned = []
            for pair in range(GROUP // 2):
                block = third[pair * 2 * size : (pair + 1) * 2 * size]
                real = block[:size, : 2 * size] - block[size:, 2 * size :]
                imag = block[size:, : 2 * size] + block[:size, 2 * size :]
                turned.append(jnp.concatenate([real, imag], 0).T)
            back = dot(jnp.concatenate(turned, 0).astype(BF16), t_back[...])
            gradient = exit_wave * (back[:, : 2 * size] + back[:, 2 * size :])
            for member in range(GROUP):
                span = pl.ds(at[member], size)
                total[span, :] = total[span, :] + gradient[member * size : (member + 1) * size]

        for part in range(width // tile):
            flat = total[part * tile : (part + 1) * tile, :].T
            staged[pl.ds(slot * (width // tile) + part, size, rows), :] = flat[:size] + flat[size:]

    out[...] = staged[...].astype(BF16)


def ptycho(image, probe_wave, measured, counts, starts):
    slots, size, _, limit = measured.shape
    height, tile = image.shape
    width = height // size // slots * tile
    tables = [jnp.asarray(table) for table in transform_tables(size)]
    turned = jnp.swapaxes(probe_wave, 1, 2)
    probe_a = jnp.concatenate([turned[0], turned[0]], 1)
    probe_b = jnp.concatenate([-turned[1], turned[1]], 1)
    scalar = pl.BlockSpec(memory_space=pltpu.SMEM)
    vector = pl.BlockSpec(memory_space=pltpu.VMEM)
    return pl.pallas_call(
        ptycho_kernel,
        out_shape=jax.ShapeDtypeStruct((height, tile), BF16),
        in_specs=[scalar, scalar] + [vector] * 8,
        out_specs=vector,
        scratch_shapes=[
            pltpu.VMEM((width, 2 * size), F32),
            pltpu.VMEM((width, 2 * size), F32),
            pltpu.VMEM((height, tile), F32),
            pltpu.VMEM((slots, limit * size // 2, 2 * size), F32),
        ],
        compiler_params=pltpu.CompilerParams(vmem_limit_bytes=48 * 2**20),
        cost_estimate=pl.CostEstimate(
            flops=2**34, bytes_accessed=2**23, transcendentals=0
        ),
    )(counts, starts, image, probe_a, probe_b, *tables, measured)


TURN = 65536 / (2 * math.pi)


def project_kernel(volume, templates, pattern, out, flat, table, counts, index):
    slab_rows, cells = volume.shape
    group, tile_cells, tile = templates.shape
    tiles = cells // tile_cells
    spread = pattern.shape[1]
    columns, _, slabs = out.shape[:3]
    step = 32
    for base in range(0, tiles, step):
        left = jnp.concatenate(
            [
                volume[:, t * tile_cells : (t + 1) * tile_cells].astype(F32)
                for t in range(base, base + step)
            ],
            0,
        ).astype(BF16)
        for k in range(0, group, 2):
            right = jnp.concatenate([templates[k], templates[k + 1]], 1)
            result = dot(left, right)
            span = slice(base * slab_rows, (base + step) * slab_rows)
            flat[k, span, :] = result[:, :tile]
            flat[k + 1, span, :] = result[:, tile:]
    for k in range(group):
        for z in range(slab_rows):
            block = flat[k, pl.ds(z, tiles, slab_rows), :]
            table[k * tiles : (k + 1) * tiles, z * tile : (z + 1) * tile] = block.astype(BF16)

    angles = pattern.shape[2]
    own = angles * pattern.shape[0] // (columns * slabs)
    turned = jnp.concatenate(
        [
            pattern[:, :, base : base + tile].reshape(-1, tile).T
            for base in range(0, angles, tile)
        ],
        0,
    )
    turned = (turned & (group - 1)) * tiles + lax.shift_right_logical(turned, 3)
    for d in range(pattern.shape[0]):
        index[pl.ds(d, angles, pattern.shape[0]), :spread] = turned[:, d * spread : (d + 1) * spread]

    lane = lax.broadcasted_iota(jnp.int32, (2 * slabs * own, tiles), 1)

    @pl.loop(0, columns // 2)
    def _(chip):
        wanted = jnp.concatenate(
            [
                index[pl.ds(pl.multiple_of((s * columns + 2 * chip + core) * own, own), own), :]
                for core in range(2)
                for s in range(slabs)
            ],
            0,
        )
        for k in range(group):
            held = jnp.zeros(lane.shape, F32)
            for member in range(spread):
                held = held + jnp.where(wanted[:, member : member + 1] == lane + k * tiles, 1.0, 0.0)
            counts[:, k * tiles : (k + 1) * tiles] = held.astype(BF16)
        for z in range(0, slab_rows, 2):
            result = dot(counts[...], table[:, z * tile : (z + 2) * tile])
            result = jnp.floor(result * TURN + 0.5).astype(jnp.int32).astype(jnp.int16)
            for core in range(2):
                for more in range(2):
                    block = result[
                        core * slabs * own : (core + 1) * slabs * own,
                        more * tile : (more + 1) * tile,
                    ]
                    out[2 * chip + core, z + more] = block.reshape(slabs, own, tile)


def project(volume, templates, pattern, columns, slabs):
    slab_rows, cells = volume.shape
    group, tile_cells, tile = templates.shape
    tiles = cells // tile_cells
    tile_rows, spread, angles = pattern.shape
    rows = angles * tile_rows
    own = rows // (columns * slabs)
    vector = pl.BlockSpec(memory_space=pltpu.VMEM)
    return pl.pallas_call(
        project_kernel,
        out_shape=jax.ShapeDtypeStruct((columns, slab_rows, slabs, own, tile), jnp.int16),
        in_specs=[vector] * 3,
        out_specs=vector,
        scratch_shapes=[
            pltpu.VMEM((group, tiles * slab_rows, tile), F32),
            pltpu.VMEM((group * tiles, slab_rows * tile), BF16),
            pltpu.VMEM((2 * slabs * own, group * tiles), BF16),
            pltpu.VMEM((rows, tile), jnp.int32),
        ],
        compiler_params=pltpu.CompilerParams(vmem_limit_bytes=48 * 2**20),
    )(volume, templates, pattern)


def spread_kernel(
    step_size, penalty,
    gathered, pattern, templates, volume, consensus, out, grads, counts, flat,
):
    columns, slabs, slab_rows, own, tile = gathered.shape
    spread, rows = pattern.shape
    group, tile_cells, _ = templates.shape
    tiles = flat.shape[1] // slab_rows
    here = volume.shape[1] // tile_cells

    @pl.when(pl.program_id(0) == 0)
    def _():
        for z in range(slab_rows):
            grads[:, z * tile : (z + 1) * tile] = gathered[:, :, z].reshape(rows, tile)

        chunk = tiles
        row = lax.broadcasted_iota(jnp.int32, (chunk, 256), 0)

        @pl.loop(0, group)
        def _(k):
            for base in range(0, rows, 256):
                entry = pattern[:, base : base + 256]
                wanted = (entry & (group - 1)) * tiles + lax.shift_right_logical(entry, 3)
                held = jnp.zeros((chunk, 256), F32)
                for member in range(spread):
                    held = held + jnp.where(
                        wanted[member : member + 1, :] == row + k * tiles, 1.0, 0.0
                    )
                counts[pl.ds(pl.multiple_of(k * tiles, tiles), tiles), base : base + 256] = (
                    held.astype(BF16)
                )

        for base in range(0, group, 2):
            for z in range(0, slab_rows, 2):
                result = dot(
                    counts[base * tiles : (base + 2) * tiles, :],
                    grads[:, z * tile : (z + 2) * tile],
                )
                result = result.astype(BF16).astype(F32)
                for k in range(2):
                    for more in range(2):
                        flat[base + k, pl.ds(z + more, tiles, slab_rows), :] = (
                            result[k * tiles : (k + 1) * tiles, more * tile : (more + 1) * tile]
                        )

    size = here * slab_rows
    mine = pl.ds(pl.multiple_of(pl.program_id(0) * size, size), size)
    left = jnp.concatenate([flat[k, mine, :] for k in range(group)], 1).astype(BF16)
    for part in range(0, tile_cells, 256):
        total = jnp.zeros((size, 256), F32)
        for k in range(0, group, 2):
            right = jnp.concatenate(
                [templates[k, part : part + 256, :], templates[k + 1, part : part + 256, :]], 1
            )
            total = total + lax.dot_general(
                left[:, k * tile : (k + 2) * tile],
                right,
                (((1,), (1,)), ((), ())),
                preferred_element_type=F32,
            )
        for t in range(here):
            span = slice(t * tile_cells + part, t * tile_cells + part + 256)
            own_volume = volume[:, span].astype(F32)
            wanted = consensus[:, span].astype(F32)
            moved = total[t * slab_rows : (t + 1) * slab_rows]
            out[:, span] = own_volume - step_size * (moved + penalty * (own_volume - wanted))


def spread_back(gathered, pattern_columns, templates, volume, consensus, step_size, penalty):
    slab_rows, cells = volume.shape
    group, tile_cells, tile = templates.shape
    tiles = cells // tile_cells
    rows = pattern_columns.shape[1]
    vector = pl.BlockSpec(memory_space=pltpu.VMEM)
    steps = 4
    block = pl.BlockSpec((slab_rows, cells // steps), lambda i: (0, i))
    return pl.pallas_call(
        functools.partial(spread_kernel, step_size, penalty),
        grid=(steps,),
        out_shape=jax.ShapeDtypeStruct((slab_rows, cells), F32),
        in_specs=[vector] * 3 + [block, block],
        out_specs=block,
        scratch_shapes=[
            pltpu.VMEM((rows, slab_rows * tile), BF16),
            pltpu.VMEM((group * tiles, rows), BF16),
            pltpu.VMEM((group, tiles * slab_rows, tile), F32),
        ],
        compiler_params=pltpu.CompilerParams(vmem_limit_bytes=48 * 2**20),
    )(gathered, pattern_columns, templates, volume, consensus)


def steps_over():
    return [(dx, dy) for dx in range(2) for dy in range(4)]


def moved(index, step):
    high, low = lax.div(index, 4), lax.rem(index, 4)
    return lax.rem(high + step[0], 2) * 4 + lax.rem(low + step[1], 4)


def greet(slab, chip, core):
    barrier = pltpu.get_barrier_semaphore()
    here = slab, 2 * chip + core
    others = [(slab, 2 * chip + 1 - core)]
    others += [(slab, 2 * moved(chip, step) + core) for step in steps_over()[1:]]
    others += [(moved(slab, step), here[1]) for step in steps_over()[1:]]
    for other in others:
        pl.semaphore_signal(barrier, inc=1, device_id=other, device_id_type=pl.DeviceIdType.MESH)
    pl.semaphore_wait(barrier, len(others))


def remote(source, target, send, receive, device):
    return pltpu.make_async_remote_copy(
        src_ref=source,
        dst_ref=target,
        send_sem=send,
        recv_sem=receive,
        device_id=device,
        device_id_type=pl.DeviceIdType.MESH,
    )


def reduce_kernel(
    partial, out, own, pair, sent, arrived, total,
    own_sem, pair_send, pair_recv, chip_send, chip_recv, slab_send, slab_recv,
):
    slab, column = lax.axis_index("slab"), lax.axis_index("col")
    chip, core = lax.div(column, 2), lax.rem(column, 2)
    slabs, slab_rows = out.shape[:2]
    steps = steps_over()
    order = list(range(1, 8)) + [0]
    greet(slab, chip, core)

    locals_, pairs, chips, slabs_ = {}, {}, {}, {}
    for d in order:
        target = 2 * moved(chip, steps[d])
        pairs[d] = remote(
            partial.at[target + 1 - core], pair.at[d], pair_send.at[d], pair_recv.at[d],
            (slab, 2 * chip + 1 - core),
        )
        pairs[d].start()
        locals_[d] = pltpu.make_async_copy(partial.at[target + core], own.at[d], own_sem.at[d])
        locals_[d].start()
    for d in order:
        locals_[d].wait()
        pairs[d].wait_recv()
        if d:

            @pl.loop(0, slab_rows)
            def _(z):
                sent[d, z] = own[d, z] + pair[d, z]

            chips[d] = remote(
                sent.at[d], arrived.at[d], chip_send.at[d], chip_recv.at[d],
                (slab, 2 * moved(chip, steps[d]) + core),
            )
            chips[d].start()
    for d in order[:-1]:
        chips[d].wait_recv()

    @pl.loop(0, slab_rows)
    def _(z):
        value = own[0, z] + pair[0, z]
        for d in range(1, 8):
            value = value + arrived[d, z]
        total[:, z] = value

    for d in order[:-1]:
        other = moved(slab, steps[d])
        slabs_[d] = remote(
            total.at[other], out.at[slab], slab_send.at[d], slab_recv.at[d], (other, column)
        )
        slabs_[d].start()
    out[slab] = total[slab]
    for d in order:
        pairs[d].wait_send()
    for d in order[:-1]:
        chips[d].wait_send()
        slabs_[d].wait()


def reduce_images(partial):
    columns, slab_rows, slabs, own, tile = partial.shape
    block = (8, slab_rows, slabs, own, tile)
    sem = pltpu.SemaphoreType.DMA((8,))
    return pl.pallas_call(
        reduce_kernel,
        out_shape=jax.ShapeDtypeStruct((slabs, slab_rows, own, tile), jnp.int16),
        in_specs=[pl.BlockSpec(memory_space=pl.ANY)],
        out_specs=pl.BlockSpec(memory_space=pltpu.VMEM),
        scratch_shapes=[pltpu.VMEM(block, jnp.int16)] * 4
        + [pltpu.VMEM((slabs, slab_rows, own, tile), jnp.int16)]
        + [sem] * 7,
        compiler_params=pltpu.CompilerParams(
            collective_id=1, has_side_effects=True, vmem_limit_bytes=32 * 2**20
        ),
    )(partial)


def gather_kernel(
    grads, out, mine, held, slab_send, slab_recv, chip_send, chip_recv, pair_send, pair_recv,
    out_sem,
):
    slab, column = lax.axis_index("slab"), lax.axis_index("col")
    chip, core = lax.div(column, 2), lax.rem(column, 2)
    sibling = (slab, 2 * chip + 1 - core)
    steps = steps_over()
    greet(slab, chip, core)

    slabs_, chips, pairs, locals_ = {}, {}, {}, {}
    for d in range(1, 8):
        other = moved(slab, steps[d])
        slabs_[d] = remote(
            grads.at[other], mine.at[slab], slab_send.at[d], slab_recv.at[d], (other, column)
        )
        slabs_[d].start()
    mine[slab] = grads[slab]
    for d in range(1, 8):
        slabs_[d].wait_recv()
    for d in range(1, 8):
        target = moved(chip, steps[d])
        chips[d] = remote(
            mine, held.at[d], chip_send.at[d], chip_recv.at[d], (slab, 2 * target + core)
        )
        chips[d].start()
    for d in range(8):
        if d:
            chips[d].wait_recv()
        source = mine if d == 0 else held.at[d]
        origin = moved(chip, ((2 - steps[d][0]) % 2, (4 - steps[d][1]) % 4))
        place = out.at[2 * origin + core]
        pairs[d] = remote(source, place, pair_send.at[d], pair_recv.at[d], sibling)
        pairs[d].start()
        locals_[d] = pltpu.make_async_copy(source, place, out_sem.at[d])
        locals_[d].start()
    for d in range(8):
        locals_[d].wait()
        pairs[d].wait()
        if d:
            chips[d].wait_send()
            slabs_[d].wait_send()


def gather_grads(grads):
    slabs, slab_rows, own, tile = grads.shape
    sem = pltpu.SemaphoreType.DMA((8,))
    return pl.pallas_call(
        gather_kernel,
        out_shape=jax.ShapeDtypeStruct((16, slabs, slab_rows, own, tile), BF16),
        in_specs=[pl.BlockSpec(memory_space=pltpu.VMEM)],
        out_specs=pl.BlockSpec(memory_space=pl.ANY),
        scratch_shapes=[pltpu.VMEM(grads.shape, BF16), pltpu.VMEM((8,) + grads.shape, BF16)]
        + [sem] * 7,
        compiler_params=pltpu.CompilerParams(
            collective_id=2, has_side_effects=True, vmem_limit_bytes=32 * 2**20
        ),
    )(grads)


def on_device(
    volume, consensus, templates, pattern, probe_wave, measured, scan_counts, scan_positions
):
    slab_rows = volume.shape[0]
    tile = templates.shape[2]
    slab_count = lax.axis_size("slab")
    column_count = lax.axis_size("col")
    angle_count, tile_rows, spread = pattern.shape[1:]
    per_owner = angle_count // (slab_count * column_count)
    own = per_owner * tile_rows
    rows = angle_count * tile_rows
    owner = lax.axis_index("slab") * column_count + lax.axis_index("col")
    counts = lax.dynamic_slice_in_dim(scan_counts, owner * per_owner, per_owner)
    starts = lax.dynamic_slice_in_dim(scan_positions, owner * per_owner, per_owner)

    partial = project(
        volume, templates, pattern[0].transpose(1, 2, 0), column_count, slab_count
    )
    image = reduce_images(partial).reshape(slab_count * slab_rows * own, tile)

    gradients = ptycho(image, probe_wave, measured.transpose(0, 2, 3, 1), counts, starts)

    gathered = gather_grads(gradients.reshape(slab_count, slab_rows, own, tile))
    pattern_columns = pattern.reshape(slab_count, column_count, own, spread)
    pattern_columns = pattern_columns.transpose(3, 1, 0, 2).reshape(spread, rows)
    return spread_back(
        gathered, pattern_columns, templates, volume, consensus, step_size, penalty
    )


def solution(mesh):
    return jax.shard_map(
        on_device,
        mesh=mesh,
        in_specs=(
            P("slab", "col"),
            P("slab", "col"),
            P("col", None, None),
            P("col", None, None, None),
            P(),
            P(("slab", "col"), None, None, None),
            P(),
            P(),
        ),
        out_specs=P("slab", "col"),
        check_vma=False,
    )
```

```python
import functools
import math

import jax
import jax.numpy as jnp
import numpy as np
from jax import lax
from jax.experimental import pallas as pl
from jax.experimental.pallas import tpu as pltpu
from jax.sharding import PartitionSpec as P

BF16 = jnp.bfloat16
F32 = jnp.float32
GROUP = 8
step_size = 0.1
penalty = 1.0
I16 = jnp.int16
TURN = 65536 / (2 * math.pi)

def dot(left, right):
    return jnp.dot(left, right, preferred_element_type=F32)


def steps_over():
    return [(dx, dy) for dx in range(2) for dy in range(4)]


def moved(index, step):
    high, low = lax.div(index, 4), lax.rem(index, 4)
    return lax.rem(high + step[0], 2) * 4 + lax.rem(low + step[1], 4)


def greet_all(slab, chip, core):
    barrier = pltpu.get_barrier_semaphore()
    here = slab, 2 * chip + core
    others = [(slab, 2 * chip + 1 - core)]
    others += [(slab, 2 * moved(chip, step) + core) for step in steps_over()[1:]]
    others += [(moved(slab, step), here[1]) for step in steps_over()[1:]]
    for other in others:
        pl.semaphore_signal(barrier, inc=1, device_id=other, device_id_type=pl.DeviceIdType.MESH)


def greeted(number):
    pl.semaphore_wait(pltpu.get_barrier_semaphore(), number)


def remote(source, target, send, receive, device):
    return pltpu.make_async_remote_copy(
        src_ref=source,
        dst_ref=target,
        send_sem=send,
        recv_sem=receive,
        device_id=device,
        device_id_type=pl.DeviceIdType.MESH,
    )


def gather_kernel(
    grads, out, mine, held, slab_send, slab_recv, chip_send, chip_recv, pair_send, pair_recv,
    out_sem,
):
    slab, column = lax.axis_index("slab"), lax.axis_index("col")
    chip, core = lax.div(column, 2), lax.rem(column, 2)
    sibling = (slab, 2 * chip + 1 - core)
    steps = steps_over()
    greet_all(slab, chip, core)
    greeted(15)

    slabs_, chips, pairs, locals_ = {}, {}, {}, {}
    for d in range(1, 8):
        other = moved(slab, steps[d])
        slabs_[d] = remote(
            grads.at[other], mine.at[slab], slab_send.at[d], slab_recv.at[d], (other, column)
        )
        slabs_[d].start()
    mine[slab] = grads[slab]
    for d in range(1, 8):
        slabs_[d].wait_recv()
    for d in range(1, 8):
        target = moved(chip, steps[d])
        chips[d] = remote(
            mine, held.at[d], chip_send.at[d], chip_recv.at[d], (slab, 2 * target + core)
        )
        chips[d].start()
    for d in range(8):
        if d:
            chips[d].wait_recv()
        source = mine if d == 0 else held.at[d]
        origin = moved(chip, ((2 - steps[d][0]) % 2, (4 - steps[d][1]) % 4))
        place = out.at[2 * origin + core]
        pairs[d] = remote(source, place, pair_send.at[d], pair_recv.at[d], sibling)
        pairs[d].start()
        locals_[d] = pltpu.make_async_copy(source, place, out_sem.at[d])
        locals_[d].start()
    for d in range(8):
        locals_[d].wait()
        pairs[d].wait()
        if d:
            chips[d].wait_send()
            slabs_[d].wait_send()


def gather_grads(grads):
    slabs, slab_rows, own, tile = grads.shape
    sem = pltpu.SemaphoreType.DMA((8,))
    return pl.pallas_call(
        gather_kernel,
        out_shape=jax.ShapeDtypeStruct((16, slabs, slab_rows, own, tile), BF16),
        in_specs=[pl.BlockSpec(memory_space=pltpu.VMEM)],
        out_specs=pl.BlockSpec(memory_space=pl.ANY),
        scratch_shapes=[pltpu.VMEM(grads.shape, BF16), pltpu.VMEM((8,) + grads.shape, BF16)]
        + [sem] * 7,
        compiler_params=pltpu.CompilerParams(
            collective_id=2, has_side_effects=True, vmem_limit_bytes=32 * 2**20
        ),
    )(grads)


def segment_of(entry, group, tiles):
    return (entry & (group - 1)) * tiles + lax.div(entry, group)


def forward_kernel(
    volume_in, templates_in, pattern, measured_in, image, observed,
    volume, templates, measured, flat, table, counts, index, own, outgoing, pair, arrived, total,
    load_sem, pair_send, pair_recv, chip_send, chip_recv, slab_send, slab_recv,
):
    slab, column = lax.axis_index("slab"), lax.axis_index("col")
    chip, core = lax.div(column, 2), lax.rem(column, 2)
    slabs, slab_rows, share, tile = image.shape
    columns = 2 * own.shape[0]
    group, tile_cells, _ = templates.shape
    tiles = table.shape[0] // group
    tile_rows, spread, angles = pattern.shape
    half = measured.shape[1] // 2
    limit = measured.shape[3]
    quarter = volume.shape[1] // 4
    greet_all(slab, chip, core)

    loads = [pltpu.make_async_copy(templates_in, templates, load_sem.at[0])]
    for part in range(4):
        span = pl.ds(part * quarter, quarter)
        loads.append(
            pltpu.make_async_copy(volume_in.at[:, span], volume.at[:, span], load_sem.at[1 + part])
        )
    loads.append(pltpu.make_async_copy(measured_in, measured, load_sem.at[5]))
    for load in loads:
        load.start()

    turned = jnp.concatenate(
        [
            pattern[:, :, base : base + tile].reshape(-1, tile).T
            for base in range(0, angles, tile)
        ],
        0,
    )
    turned = segment_of(turned, group, tiles)
    for d in range(tile_rows):
        index[pl.ds(d, angles, tile_rows), :spread] = turned[:, d * spread : (d + 1) * spread]

    loads[0].wait()
    step = tiles // 4
    for part in range(4):
        loads[1 + part].wait()
        left = jnp.concatenate(
            [
                volume[:, t * tile_cells : (t + 1) * tile_cells].astype(F32)
                for t in range(part * step, (part + 1) * step)
            ],
            0,
        ).astype(BF16)
        span = slice(part * step * slab_rows, (part + 1) * step * slab_rows)
        for k in range(0, group, 2):
            result = dot(left, jnp.concatenate([templates[k], templates[k + 1]], 1))
            flat[k, span, :] = result[:, :tile]
            flat[k + 1, span, :] = result[:, tile:]
    for k in range(group):
        for z in range(slab_rows):
            block = flat[k, pl.ds(z, tiles, slab_rows), :]
            table[k * tiles : (k + 1) * tiles, z * tile : (z + 1) * tile] = block.astype(BF16)

    greeted(15)
    lane = lax.broadcasted_iota(jnp.int32, (2 * slabs * share, tiles), 1)

    def at_step(i):
        d = lax.rem(5 * i + 5, 8)
        high = lax.rem(lax.div(chip, 4) + lax.div(d, 4), 2)
        return d, 4 * high + lax.rem(chip + d, 4)

    def to_pair(d):
        return remote(
            outgoing.at[d], pair.at[d], pair_send.at[d], pair_recv.at[d],
            (slab, 2 * chip + 1 - core),
        )

    def to_chip(d, target):
        return remote(
            own.at[d], arrived.at[d], chip_send.at[d], chip_recv.at[d], (slab, 2 * target + core)
        )

    def compute(i):
        d, target = at_step(i)
        wanted = jnp.concatenate(
            [
                index[pl.ds(pl.multiple_of((s * columns + 2 * target + c) * share, share), share), :]
                for c in (core, 1 - core)
                for s in range(slabs)
            ],
            0,
        )
        for k in range(group):
            held = jnp.zeros(lane.shape, F32)
            for member in range(spread):
                held = held + jnp.where(wanted[:, member : member + 1] == lane + k * tiles, 1.0, 0.0)
            counts[:, k * tiles : (k + 1) * tiles] = held.astype(BF16)
        for z in range(0, slab_rows, 2):
            result = dot(counts[...], table[:, z * tile : (z + 2) * tile])
            result = jnp.floor(result * TURN + 0.5).astype(jnp.int32).astype(I16)
            for more in range(2):
                part = result[:, more * tile : (more + 1) * tile]
                own[d, z + more] = part[: slabs * share].reshape(slabs, share, tile)
                outgoing[d, z + more] = part[slabs * share :].reshape(slabs, share, tile)
        to_pair(d).start()

    def combine(i):
        d, target = at_step(i)
        to_pair(d).wait_recv()

        @pl.loop(0, slab_rows)
        def _(z):
            own[d, z] = own[d, z] + pair[d, z]

        @pl.when(i < 7)
        def _():
            to_chip(d, target).start()

    @pl.loop(0, 9)
    def _(i):
        @pl.when(i < 8)
        def _():
            compute(i)

        @pl.when(i > 0)
        def _():
            combine(i - 1)

    loads[5].wait()
    for slot in range(measured.shape[0]):

        @pl.loop(0, half)
        def _(row):
            both = jnp.concatenate([measured[slot, row], measured[slot, row + half]], 0)
            observed[slot, pl.ds(row, limit, half), :] = both.T

    for i in range(7):
        d, target = at_step(i)
        to_chip(d, target).wait_recv()

    @pl.loop(0, slab_rows)
    def _(z):
        value = own[0, z]
        for d in range(1, 8):
            value = value + arrived[d, z]
        total[:, z] = value

    slabs_ = []
    for d in range(1, 8):
        other = moved(slab, steps_over()[d])
        slabs_.append(
            remote(total.at[other], image.at[slab], slab_send.at[d], slab_recv.at[d], (other, column))
        )
        slabs_[-1].start()
    image[slab] = total[slab]
    for i in range(8):
        d, target = at_step(i)
        to_pair(d).wait_send()
        if i < 7:
            to_chip(d, target).wait_send()
    for copy in slabs_:
        copy.wait()


def forward(volume, templates, pattern, measured, columns, slabs):
    slab_rows, cells = volume.shape
    group, tile_cells, tile = templates.shape
    tiles = cells // tile_cells
    tile_rows, spread, angles = pattern.shape
    slots, size, _, limit = measured.shape
    rows = angles * tile_rows
    share = rows // (columns * slabs)
    block = (columns // 2, slab_rows, slabs, share, tile)
    vector = pl.BlockSpec(memory_space=pltpu.VMEM)
    anywhere = pl.BlockSpec(memory_space=pl.ANY)
    sem = pltpu.SemaphoreType.DMA((8,))
    return pl.pallas_call(
        forward_kernel,
        out_shape=(
            jax.ShapeDtypeStruct((slabs, slab_rows, share, tile), I16),
            jax.ShapeDtypeStruct((slots, limit * size // 2, 2 * size), F32),
        ),
        in_specs=[anywhere, anywhere, vector, anywhere],
        out_specs=(vector, vector),
        scratch_shapes=[
            pltpu.VMEM(volume.shape, BF16),
            pltpu.VMEM(templates.shape, BF16),
            pltpu.VMEM(measured.shape, F32),
            pltpu.VMEM((group, tiles * slab_rows, tile), F32),
            pltpu.VMEM((group * tiles, slab_rows * tile), BF16),
            pltpu.VMEM((2 * slabs * share, group * tiles), BF16),
            pltpu.VMEM((rows, tile), jnp.int32),
        ]
        + [pltpu.VMEM(block, I16)] * 4
        + [pltpu.VMEM((slabs, slab_rows, share, tile), I16)]
        + [sem] * 7,
        compiler_params=pltpu.CompilerParams(
            collective_id=1, has_side_effects=True, vmem_limit_bytes=48 * 2**20
        ),
    )(volume, templates, pattern, measured)


def trig_coefficients():
    grid = (np.cos(np.pi * (np.arange(400) + 0.5) / 400) + 1.0) * (np.pi * np.pi * 0.5005)
    root = np.sqrt(grid)
    sine = np.polynomial.Polynomial.fit(grid, np.sin(root) / root, 6).convert().coef
    cosine = np.polynomial.Polynomial.fit(grid, np.cos(root), 7).convert().coef
    return [float(v) for v in sine], [float(v) for v in cosine]


def sine_cosine(angle):
    sine, cosine = trig_coefficients()
    square = angle * angle
    sine_value = jnp.full_like(square, sine[-1])
    for value in sine[-2::-1]:
        sine_value = sine_value * square + value
    cosine_value = jnp.full_like(square, cosine[-1])
    for value in cosine[-2::-1]:
        cosine_value = cosine_value * square + value
    return sine_value * angle, cosine_value


def split_bf16(table):
    high = table.astype(np.float32).astype(BF16)
    low = (table - high.astype(np.float64)).astype(np.float32).astype(BF16)
    return high, low


def transform_tables(size):
    index = np.arange(size)
    radians = 2.0 * np.pi / size * (index[:, None] * index[None, :] % size)
    cosine = np.cos(radians) / math.sqrt(size)
    sine = np.sin(radians) / math.sqrt(size)
    zero = np.zeros_like(cosine)
    forward = np.block([[cosine, -sine], [sine, cosine]])
    pair = np.block([[cosine, zero, sine, zero], [zero, cosine, zero, sine]])
    back = np.block([[2 * sine, -2 * cosine], [2 * cosine, 2 * sine]])
    f_high, f_low = split_bf16(forward)
    p_high, p_low = split_bf16(pair)
    b_high, b_low = split_bf16(back)
    lanes = np.concatenate([f_high, f_low], 1)
    back = np.concatenate([b_high, b_low], 1)
    return (
        np.concatenate([lanes, lanes], 0),
        np.concatenate([p_high, p_high], 0),
        np.concatenate([p_high, p_low], 0),
        np.concatenate([back, back], 0),
    )


def halves(value):
    high = value.astype(BF16)
    low = (value - high.astype(F32)).astype(BF16)
    return high, low


def ptycho_kernel(
    counts, starts_in, image, probe_wave, t_first, t_pair, t_pair_both, t_back, observed,
    out, waves, total, staged, probe_a, probe_b, starts, landed,
):
    slots = observed.shape[0]
    size = probe_wave.shape[1]
    limit = starts.shape[1]
    owner = lax.axis_index("slab") * lax.axis_size("col") + lax.axis_index("col")
    first_angle = owner * slots
    first_row = lax.div(first_angle, 8) * 8
    load = pltpu.make_async_copy(starts_in.at[pl.ds(pl.multiple_of(first_row, 8), 8)], starts, landed)
    load.start()
    both = jnp.concatenate([probe_wave[0], probe_wave[0]], 0)
    probe_a[...] = both.T
    both = jnp.concatenate([-probe_wave[1], probe_wave[1]], 0)
    probe_b[...] = both.T
    width = waves.shape[0]
    tile = image.shape[1]
    rows = width // tile * slots
    chunk_count = limit // GROUP

    def used_chunks(slot):
        return jnp.clip(lax.div(counts[first_angle + slot] + (GROUP - 1), GROUP), 0, chunk_count)

    half = size // 2

    staged[...] = image[...].astype(jnp.int32).astype(F32) * (2 * math.pi / 65536)
    load.wait()
    lane = lax.broadcasted_iota(jnp.int32, (size, 2 * size), 1)

    @pl.loop(0, slots)
    def _(slot):
        for part in range(width // tile):
            sine, cosine = sine_cosine(staged[pl.ds(slot * (width // tile) + part, size, rows), :])
            waves[part * tile : (part + 1) * tile, :] = jnp.concatenate([cosine, sine], 0).T
        total[...] = jnp.zeros_like(total)
        count = counts[first_angle + slot]

        @pl.loop(0, used_chunks(slot))
        def _(chunk):
            begin = chunk * GROUP
            at = [starts[first_angle - first_row + slot, begin + member] for member in range(GROUP)]
            exits = []
            for member in range(GROUP):
                patch = waves[pl.ds(at[member], size), :]
                exits.append(probe_a[...] * patch + probe_b[...] * pltpu.roll(patch, size, 1))
            exit_wave = jnp.concatenate(exits, 0)
            high, low = halves(exit_wave)
            first = dot(jnp.concatenate([high, low], 1), t_first[...])
            first = first[:, : 2 * size] + first[:, 2 * size :]
            turned = jnp.concatenate(
                [first[pair * 2 * size : (pair + 1) * 2 * size].T for pair in range(GROUP // 2)], 0
            )
            high, low = halves(turned)
            second = dot(jnp.concatenate([high, low], 1), t_pair[...])
            second = second + dot(high, t_pair_both[2 * size :, :])
            scaled = []
            for pair in range(GROUP // 2):
                block = second[pair * 2 * size : (pair + 1) * 2 * size]
                real = block[:size, : 2 * size] + block[size:, 2 * size :]
                imag = block[size:, : 2 * size] - block[:size, 2 * size :]
                member = begin + 2 * pair
                seen = [
                    observed[slot, pl.ds(pl.multiple_of((member + m) * half, half), half), :]
                    for m in range(2)
                ]
                seen = jnp.concatenate(
                    [
                        jnp.concatenate([seen[0][:, :size], seen[1][:, :size]], 1),
                        jnp.concatenate([seen[0][:, size:], seen[1][:, size:]], 1),
                    ],
                    0,
                )
                residual = real * real + imag * imag - seen
                live = member + jnp.where(lane >= size, 1, 0) < count
                residual = jnp.where(live, residual, 0.0)
                scaled += [residual * real, residual * imag]
            scaled = jnp.concatenate(scaled, 0).astype(BF16)
            third = dot(jnp.concatenate([scaled, scaled], 1), t_pair_both[...])
            turned = []
            for pair in range(GROUP // 2):
                block = third[pair * 2 * size : (pair + 1) * 2 * size]
                real = block[:size, : 2 * size] - block[size:, 2 * size :]
                imag = block[size:, : 2 * size] + block[:size, 2 * size :]
                turned.append(jnp.concatenate([real, imag], 0).T)
            high, low = halves(jnp.concatenate(turned, 0))
            back = dot(jnp.concatenate([high, low], 1), t_back[...])
            gradient = exit_wave * (back[:, : 2 * size] + back[:, 2 * size :])
            for member in range(GROUP):
                span = pl.ds(at[member], size)
                total[span, :] = total[span, :] + gradient[member * size : (member + 1) * size]

        for part in range(width // tile):
            flat = total[part * tile : (part + 1) * tile, :].T
            staged[pl.ds(slot * (width // tile) + part, size, rows), :] = flat[:size] + flat[size:]

    out[...] = staged[...].astype(BF16)


def ptycho(image, probe_wave, observed, counts, starts):
    slots = observed.shape[0]
    size = probe_wave.shape[1]
    height, tile = image.shape
    width = height // size // slots * tile
    tables = [jnp.asarray(table) for table in transform_tables(size)]
    vector = pl.BlockSpec(memory_space=pltpu.VMEM)
    return pl.pallas_call(
        ptycho_kernel,
        out_shape=jax.ShapeDtypeStruct((height, tile), BF16),
        in_specs=[pl.BlockSpec(memory_space=pltpu.SMEM), pl.BlockSpec(memory_space=pl.ANY)]
        + [vector] * 7,
        out_specs=vector,
        scratch_shapes=[
            pltpu.VMEM((width, 2 * size), F32),
            pltpu.VMEM((width, 2 * size), F32),
            pltpu.VMEM((height, tile), F32),
            pltpu.VMEM((size, 2 * size), F32),
            pltpu.VMEM((size, 2 * size), F32),
            pltpu.SMEM((8, starts.shape[1]), jnp.int32),
            pltpu.SemaphoreType.DMA,
        ],
        compiler_params=pltpu.CompilerParams(vmem_limit_bytes=48 * 2**20),
    )(counts, starts, image, probe_wave, *tables, observed)


def spread_kernel(
    step_size, penalty,
    gathered, pattern, templates, volume, consensus, out, grads, counts, flat,
):
    columns, slabs, slab_rows, own, tile = gathered.shape
    spread, rows = pattern.shape
    group, tile_cells, _ = templates.shape
    tiles = flat.shape[1] // slab_rows
    here = volume.shape[1] // tile_cells

    @pl.when(pl.program_id(0) == 0)
    def _():
        for z in range(slab_rows):
            grads[:, z * tile : (z + 1) * tile] = gathered[:, :, z].reshape(rows, tile)

        chunk = tiles
        row = lax.broadcasted_iota(jnp.int32, (chunk, 256), 0)

        @pl.loop(0, group)
        def _(k):
            for base in range(0, rows, 256):
                entry = pattern[:, base : base + 256]
                wanted = (entry & (group - 1)) * tiles + lax.shift_right_logical(entry, 3)
                held = jnp.zeros((chunk, 256), F32)
                for member in range(spread):
                    held = held + jnp.where(
                        wanted[member : member + 1, :] == row + k * tiles, 1.0, 0.0
                    )
                counts[pl.ds(pl.multiple_of(k * tiles, tiles), tiles), base : base + 256] = (
                    held.astype(BF16)
                )

        for base in range(0, group, 2):
            for z in range(0, slab_rows, 2):
                result = dot(
                    counts[base * tiles : (base + 2) * tiles, :],
                    grads[:, z * tile : (z + 2) * tile],
                )
                result = result.astype(BF16).astype(F32)
                for k in range(2):
                    for more in range(2):
                        flat[base + k, pl.ds(z + more, tiles, slab_rows), :] = (
                            result[k * tiles : (k + 1) * tiles, more * tile : (more + 1) * tile]
                        )

    size = here * slab_rows
    mine = pl.ds(pl.multiple_of(pl.program_id(0) * size, size), size)
    left = jnp.concatenate([flat[k, mine, :] for k in range(group)], 1).astype(BF16)
    for part in range(0, tile_cells, 256):
        total = jnp.zeros((size, 256), F32)
        for k in range(0, group, 2):
            right = jnp.concatenate(
                [templates[k, part : part + 256, :], templates[k + 1, part : part + 256, :]], 1
            )
            total = total + lax.dot_general(
                left[:, k * tile : (k + 2) * tile],
                right,
                (((1,), (1,)), ((), ())),
                preferred_element_type=F32,
            )
        for t in range(here):
            span = slice(t * tile_cells + part, t * tile_cells + part + 256)
            own_volume = volume[:, span].astype(F32)
            wanted = consensus[:, span].astype(F32)
            moved = total[t * slab_rows : (t + 1) * slab_rows]
            out[:, span] = own_volume - step_size * (moved + penalty * (own_volume - wanted))


def spread_back(gathered, pattern_columns, templates, volume, consensus, step_size, penalty):
    slab_rows, cells = volume.shape
    group, tile_cells, tile = templates.shape
    tiles = cells // tile_cells
    rows = pattern_columns.shape[1]
    vector = pl.BlockSpec(memory_space=pltpu.VMEM)
    steps = 4
    block = pl.BlockSpec((slab_rows, cells // steps), lambda i: (0, i))
    return pl.pallas_call(
        functools.partial(spread_kernel, step_size, penalty),
        grid=(steps,),
        out_shape=jax.ShapeDtypeStruct((slab_rows, cells), F32),
        in_specs=[vector] * 3 + [block, block],
        out_specs=block,
        scratch_shapes=[
            pltpu.VMEM((rows, slab_rows * tile), BF16),
            pltpu.VMEM((group * tiles, rows), BF16),
            pltpu.VMEM((group, tiles * slab_rows, tile), F32),
        ],
        compiler_params=pltpu.CompilerParams(vmem_limit_bytes=48 * 2**20),
    )(gathered, pattern_columns, templates, volume, consensus)


def on_device(
    volume, consensus, templates, pattern, probe_wave, measured, scan_counts, scan_positions
):
    slab_rows = volume.shape[0]
    tile = templates.shape[2]
    slab_count = lax.axis_size("slab")
    column_count = lax.axis_size("col")
    angle_count, tile_rows, spread = pattern.shape[1:]
    per_owner = angle_count // (slab_count * column_count)
    own = per_owner * tile_rows
    rows = angle_count * tile_rows

    image, observed = forward(
        volume,
        templates,
        pattern[0].transpose(1, 2, 0),
        measured.transpose(0, 2, 3, 1),
        column_count,
        slab_count,
    )
    image = image.reshape(slab_count * slab_rows * own, tile)
    gradients = ptycho(image, probe_wave, observed, scan_counts, scan_positions)
    gathered = gather_grads(gradients.reshape(slab_count, slab_rows, own, tile))
    pattern_columns = pattern.reshape(slab_count, column_count, own, spread)
    pattern_columns = pattern_columns.transpose(3, 1, 0, 2).reshape(spread, rows)
    return spread_back(
        gathered, pattern_columns, templates, volume, consensus, step_size, penalty
    )


def solution(mesh):
    return jax.shard_map(
        on_device,
        mesh=mesh,
        in_specs=(
            P("slab", "col"),
            P("slab", "col"),
            P("col", None, None),
            P("col", None, None, None),
            P(),
            P(("slab", "col"), None, None, None),
            P(),
            P(),
        ),
        out_specs=P("slab", "col"),
        check_vma=False,
    )
```

```python
import functools
import math

import jax
import jax.numpy as jnp
import numpy as np
from jax import lax
from jax.experimental import pallas as pl
from jax.experimental.pallas import tpu as pltpu
from jax.sharding import PartitionSpec as P

BF16 = jnp.bfloat16
F32 = jnp.float32
GROUP = 8
step_size = 0.1
penalty = 1.0
I16 = jnp.int16
TURN = 65536 / (2 * math.pi)

def dot(left, right):
    return jnp.dot(left, right, preferred_element_type=F32)


def steps_over():
    return [(dx, dy) for dx in range(2) for dy in range(4)]


def moved(index, step):
    high, low = lax.div(index, 4), lax.rem(index, 4)
    return lax.rem(high + step[0], 2) * 4 + lax.rem(low + step[1], 4)


def greet_all(slab, chip, core):
    barrier = pltpu.get_barrier_semaphore()
    here = slab, 2 * chip + core
    others = [(slab, 2 * chip + 1 - core)]
    others += [(slab, 2 * moved(chip, step) + core) for step in steps_over()[1:]]
    others += [(moved(slab, step), here[1]) for step in steps_over()[1:]]
    for other in others:
        pl.semaphore_signal(barrier, inc=1, device_id=other, device_id_type=pl.DeviceIdType.MESH)


def greeted(number):
    pl.semaphore_wait(pltpu.get_barrier_semaphore(), number)


def remote(source, target, send, receive, device):
    return pltpu.make_async_remote_copy(
        src_ref=source,
        dst_ref=target,
        send_sem=send,
        recv_sem=receive,
        device_id=device,
        device_id_type=pl.DeviceIdType.MESH,
    )


def segment_of(entry, group, tiles):
    return (entry & (group - 1)) * tiles + lax.div(entry, group)


def forward_kernel(
    volume_in, templates_in, pattern, measured_in, image, observed,
    volume, templates, measured, flat, table, counts, index, own, outgoing, pair, arrived, total,
    load_sem, pair_send, pair_recv, chip_send, chip_recv, slab_send, slab_recv,
):
    slab, column = lax.axis_index("slab"), lax.axis_index("col")
    chip, core = lax.div(column, 2), lax.rem(column, 2)
    slabs, slab_rows, share, tile = image.shape
    columns = 2 * own.shape[0]
    group, tile_cells, _ = templates.shape
    tiles = table.shape[0] // group
    tile_rows, spread, angles = pattern.shape
    half = measured.shape[1] // 2
    limit = measured.shape[3]
    quarter = volume.shape[1] // 4
    greet_all(slab, chip, core)

    loads = [pltpu.make_async_copy(templates_in, templates, load_sem.at[0])]
    for part in range(4):
        span = pl.ds(part * quarter, quarter)
        loads.append(
            pltpu.make_async_copy(volume_in.at[:, span], volume.at[:, span], load_sem.at[1 + part])
        )
    loads.append(pltpu.make_async_copy(measured_in, measured, load_sem.at[5]))
    for load in loads:
        load.start()

    turned = jnp.concatenate(
        [
            pattern[:, :, base : base + tile].reshape(-1, tile).T
            for base in range(0, angles, tile)
        ],
        0,
    )
    turned = segment_of(turned, group, tiles)
    for d in range(tile_rows):
        index[pl.ds(d, angles, tile_rows), :spread] = turned[:, d * spread : (d + 1) * spread]

    loads[0].wait()
    step = tiles // 4
    for part in range(4):
        loads[1 + part].wait()
        left = jnp.concatenate(
            [
                volume[:, t * tile_cells : (t + 1) * tile_cells].astype(F32)
                for t in range(part * step, (part + 1) * step)
            ],
            0,
        ).astype(BF16)
        span = slice(part * step * slab_rows, (part + 1) * step * slab_rows)
        for k in range(0, group, 2):
            result = dot(left, jnp.concatenate([templates[k], templates[k + 1]], 1))
            flat[k, span, :] = result[:, :tile]
            flat[k + 1, span, :] = result[:, tile:]
    for k in range(group):
        for z in range(slab_rows):
            block = flat[k, pl.ds(z, tiles, slab_rows), :]
            table[k * tiles : (k + 1) * tiles, z * tile : (z + 1) * tile] = block.astype(BF16)

    greeted(15)
    lane = lax.broadcasted_iota(jnp.int32, (2 * slabs * share, tiles), 1)

    def at_step(i):
        d = lax.rem(5 * i + 5, 8)
        high = lax.rem(lax.div(chip, 4) + lax.div(d, 4), 2)
        return d, 4 * high + lax.rem(chip + d, 4)

    def to_pair(d):
        return remote(
            outgoing.at[d], pair.at[d], pair_send.at[d], pair_recv.at[d],
            (slab, 2 * chip + 1 - core),
        )

    def to_chip(d, target):
        return remote(
            own.at[d], arrived.at[d], chip_send.at[d], chip_recv.at[d], (slab, 2 * target + core)
        )

    def compute(i):
        d, target = at_step(i)
        wanted = jnp.concatenate(
            [
                index[pl.ds(pl.multiple_of((s * columns + 2 * target + c) * share, share), share), :]
                for c in (core, 1 - core)
                for s in range(slabs)
            ],
            0,
        )
        for k in range(group):
            held = jnp.zeros(lane.shape, F32)
            for member in range(spread):
                held = held + jnp.where(wanted[:, member : member + 1] == lane + k * tiles, 1.0, 0.0)
            counts[:, k * tiles : (k + 1) * tiles] = held.astype(BF16)
        for z in range(0, slab_rows, 2):
            result = dot(counts[...], table[:, z * tile : (z + 2) * tile])
            result = jnp.floor(result * TURN + 0.5).astype(jnp.int32).astype(I16)
            for more in range(2):
                part = result[:, more * tile : (more + 1) * tile]
                own[d, z + more] = part[: slabs * share].reshape(slabs, share, tile)
                outgoing[d, z + more] = part[slabs * share :].reshape(slabs, share, tile)
        to_pair(d).start()

    def combine(i):
        d, target = at_step(i)
        to_pair(d).wait_recv()

        @pl.loop(0, slab_rows)
        def _(z):
            own[d, z] = own[d, z] + pair[d, z]

        @pl.when(i < 7)
        def _():
            to_chip(d, target).start()

    @pl.loop(0, 9)
    def _(i):
        @pl.when(i < 8)
        def _():
            compute(i)

        @pl.when(i > 0)
        def _():
            combine(i - 1)

    loads[5].wait()
    for slot in range(measured.shape[0]):

        @pl.loop(0, half)
        def _(row):
            both = jnp.concatenate([measured[slot, row], measured[slot, row + half]], 0)
            observed[slot, pl.ds(row, limit, half), :] = both.T

    for i in range(7):
        d, target = at_step(i)
        to_chip(d, target).wait_recv()

    @pl.loop(0, slab_rows)
    def _(z):
        value = own[0, z]
        for d in range(1, 8):
            value = value + arrived[d, z]
        total[:, z] = value

    slabs_ = []
    for d in range(1, 8):
        other = moved(slab, steps_over()[d])
        slabs_.append(
            remote(total.at[other], image.at[slab], slab_send.at[d], slab_recv.at[d], (other, column))
        )
        slabs_[-1].start()
    image[slab] = total[slab]
    for i in range(8):
        d, target = at_step(i)
        to_pair(d).wait_send()
        if i < 7:
            to_chip(d, target).wait_send()
    for copy in slabs_:
        copy.wait()


def forward(volume, templates, pattern, measured, columns, slabs):
    slab_rows, cells = volume.shape
    group, tile_cells, tile = templates.shape
    tiles = cells // tile_cells
    tile_rows, spread, angles = pattern.shape
    slots, size, _, limit = measured.shape
    rows = angles * tile_rows
    share = rows // (columns * slabs)
    block = (columns // 2, slab_rows, slabs, share, tile)
    vector = pl.BlockSpec(memory_space=pltpu.VMEM)
    anywhere = pl.BlockSpec(memory_space=pl.ANY)
    sem = pltpu.SemaphoreType.DMA((8,))
    return pl.pallas_call(
        forward_kernel,
        out_shape=(
            jax.ShapeDtypeStruct((slabs, slab_rows, share, tile), I16),
            jax.ShapeDtypeStruct((slots, limit * size // 2, 2 * size), F32),
        ),
        in_specs=[anywhere, anywhere, vector, anywhere],
        out_specs=(vector, vector),
        scratch_shapes=[
            pltpu.VMEM(volume.shape, BF16),
            pltpu.VMEM(templates.shape, BF16),
            pltpu.VMEM(measured.shape, F32),
            pltpu.VMEM((group, tiles * slab_rows, tile), F32),
            pltpu.VMEM((group * tiles, slab_rows * tile), BF16),
            pltpu.VMEM((2 * slabs * share, group * tiles), BF16),
            pltpu.VMEM((rows, tile), jnp.int32),
        ]
        + [pltpu.VMEM(block, I16)] * 4
        + [pltpu.VMEM((slabs, slab_rows, share, tile), I16)]
        + [sem] * 7,
        compiler_params=pltpu.CompilerParams(
            collective_id=1, has_side_effects=True, vmem_limit_bytes=48 * 2**20
        ),
    )(volume, templates, pattern, measured)


def trig_coefficients():
    grid = (np.cos(np.pi * (np.arange(400) + 0.5) / 400) + 1.0) * (np.pi * np.pi * 0.5005)
    root = np.sqrt(grid)
    sine = np.polynomial.Polynomial.fit(grid, np.sin(root) / root, 6).convert().coef
    cosine = np.polynomial.Polynomial.fit(grid, np.cos(root), 7).convert().coef
    return [float(v) for v in sine], [float(v) for v in cosine]


def sine_cosine(angle):
    sine, cosine = trig_coefficients()
    square = angle * angle
    sine_value = jnp.full_like(square, sine[-1])
    for value in sine[-2::-1]:
        sine_value = sine_value * square + value
    cosine_value = jnp.full_like(square, cosine[-1])
    for value in cosine[-2::-1]:
        cosine_value = cosine_value * square + value
    return sine_value * angle, cosine_value


def split_bf16(table):
    high = table.astype(np.float32).astype(BF16)
    low = (table - high.astype(np.float64)).astype(np.float32).astype(BF16)
    return high, low


def transform_tables(size):
    index = np.arange(size)
    radians = 2.0 * np.pi / size * (index[:, None] * index[None, :] % size)
    cosine = np.cos(radians) / math.sqrt(size)
    sine = np.sin(radians) / math.sqrt(size)
    zero = np.zeros_like(cosine)
    forward = np.block([[cosine, -sine], [sine, cosine]])
    pair = np.block([[cosine, zero, sine, zero], [zero, cosine, zero, sine]])
    back = np.block([[2 * sine, -2 * cosine], [2 * cosine, 2 * sine]])
    f_high, f_low = split_bf16(forward)
    p_high, p_low = split_bf16(pair)
    b_high, b_low = split_bf16(back)
    lanes = np.concatenate([f_high, f_low], 1)
    back = np.concatenate([b_high, b_low], 1)
    return (
        np.concatenate([lanes, lanes], 0),
        np.concatenate([p_high, p_high], 0),
        np.concatenate([p_high, p_low], 0),
        np.concatenate([back, back], 0),
    )


def halves(value):
    high = value.astype(BF16)
    low = (value - high.astype(F32)).astype(BF16)
    return high, low


def ptycho_kernel(
    counts, starts_in, image, probe_wave, t_first, t_pair, t_pair_both, t_back, observed,
    out, waves, total, staged, probe_a, probe_b, starts, landed,
):
    slots = observed.shape[0]
    size = probe_wave.shape[1]
    limit = starts.shape[1]
    owner = lax.axis_index("slab") * lax.axis_size("col") + lax.axis_index("col")
    first_angle = owner * slots
    first_row = lax.div(first_angle, 8) * 8
    load = pltpu.make_async_copy(starts_in.at[pl.ds(pl.multiple_of(first_row, 8), 8)], starts, landed)
    load.start()
    both = jnp.concatenate([probe_wave[0], probe_wave[0]], 0)
    probe_a[...] = both.T
    both = jnp.concatenate([-probe_wave[1], probe_wave[1]], 0)
    probe_b[...] = both.T
    width = waves.shape[0]
    tile = image.shape[1]
    rows = width // tile * slots
    chunk_count = limit // GROUP

    def used_chunks(slot):
        return jnp.clip(lax.div(counts[first_angle + slot] + (GROUP - 1), GROUP), 0, chunk_count)

    half = size // 2

    staged[...] = image[...].astype(jnp.int32).astype(F32) * (2 * math.pi / 65536)
    load.wait()
    lane = lax.broadcasted_iota(jnp.int32, (size, 2 * size), 1)

    @pl.loop(0, slots)
    def _(slot):
        for part in range(width // tile):
            sine, cosine = sine_cosine(staged[pl.ds(slot * (width // tile) + part, size, rows), :])
            waves[part * tile : (part + 1) * tile, :] = jnp.concatenate([cosine, sine], 0).T
        total[...] = jnp.zeros_like(total)
        count = counts[first_angle + slot]

        @pl.loop(0, used_chunks(slot))
        def _(chunk):
            begin = chunk * GROUP
            at = [starts[first_angle - first_row + slot, begin + member] for member in range(GROUP)]
            exits = []
            for member in range(GROUP):
                patch = waves[pl.ds(at[member], size), :]
                exits.append(probe_a[...] * patch + probe_b[...] * pltpu.roll(patch, size, 1))
            exit_wave = jnp.concatenate(exits, 0)
            high, low = halves(exit_wave)
            first = dot(jnp.concatenate([high, low], 1), t_first[...])
            first = first[:, : 2 * size] + first[:, 2 * size :]
            turned = jnp.concatenate(
                [first[pair * 2 * size : (pair + 1) * 2 * size].T for pair in range(GROUP // 2)], 0
            )
            high, low = halves(turned)
            second = dot(jnp.concatenate([high, low], 1), t_pair[...])
            second = second + dot(high, t_pair_both[2 * size :, :])
            scaled = []
            for pair in range(GROUP // 2):
                block = second[pair * 2 * size : (pair + 1) * 2 * size]
                real = block[:size, : 2 * size] + block[size:, 2 * size :]
                imag = block[size:, : 2 * size] - block[:size, 2 * size :]
                member = begin + 2 * pair
                seen = [
                    observed[slot, pl.ds(pl.multiple_of((member + m) * half, half), half), :]
                    for m in range(2)
                ]
                seen = jnp.concatenate(
                    [
                        jnp.concatenate([seen[0][:, :size], seen[1][:, :size]], 1),
                        jnp.concatenate([seen[0][:, size:], seen[1][:, size:]], 1),
                    ],
                    0,
                )
                residual = real * real + imag * imag - seen
                live = member + jnp.where(lane >= size, 1, 0) < count
                residual = jnp.where(live, residual, 0.0)
                scaled += [residual * real, residual * imag]
            scaled = jnp.concatenate(scaled, 0).astype(BF16)
            third = dot(jnp.concatenate([scaled, scaled], 1), t_pair_both[...])
            turned = []
            for pair in range(GROUP // 2):
                block = third[pair * 2 * size : (pair + 1) * 2 * size]
                real = block[:size, : 2 * size] - block[size:, 2 * size :]
                imag = block[size:, : 2 * size] + block[:size, 2 * size :]
                turned.append(jnp.concatenate([real, imag], 0).T)
            high, low = halves(jnp.concatenate(turned, 0))
            back = dot(jnp.concatenate([high, low], 1), t_back[...])
            gradient = exit_wave * (back[:, : 2 * size] + back[:, 2 * size :])
            for member in range(GROUP):
                span = pl.ds(at[member], size)
                total[span, :] = total[span, :] + gradient[member * size : (member + 1) * size]

        for part in range(width // tile):
            flat = total[part * tile : (part + 1) * tile, :].T
            staged[pl.ds(slot * (width // tile) + part, size, rows), :] = flat[:size] + flat[size:]

    out[...] = staged[...].astype(BF16)


def ptycho(image, probe_wave, observed, counts, starts):
    slots = observed.shape[0]
    size = probe_wave.shape[1]
    height, tile = image.shape
    width = height // size // slots * tile
    tables = [jnp.asarray(table) for table in transform_tables(size)]
    vector = pl.BlockSpec(memory_space=pltpu.VMEM)
    return pl.pallas_call(
        ptycho_kernel,
        out_shape=jax.ShapeDtypeStruct((height, tile), BF16),
        in_specs=[pl.BlockSpec(memory_space=pltpu.SMEM), pl.BlockSpec(memory_space=pl.ANY)]
        + [vector] * 7,
        out_specs=vector,
        scratch_shapes=[
            pltpu.VMEM((width, 2 * size), F32),
            pltpu.VMEM((width, 2 * size), F32),
            pltpu.VMEM((height, tile), F32),
            pltpu.VMEM((size, 2 * size), F32),
            pltpu.VMEM((size, 2 * size), F32),
            pltpu.SMEM((8, starts.shape[1]), jnp.int32),
            pltpu.SemaphoreType.DMA,
        ],
        compiler_params=pltpu.CompilerParams(vmem_limit_bytes=48 * 2**20),
    )(counts, starts, image, probe_wave, *tables, observed)


def collect_kernel(
    grads, pattern, out, mine, held, twin, counts, index, total, flat,
    slab_send, slab_recv, chip_send, chip_recv, pair_send, pair_recv,
):
    slab, column = lax.axis_index("slab"), lax.axis_index("col")
    chip, core = lax.div(column, 2), lax.rem(column, 2)
    sibling = (slab, 2 * chip + 1 - core)
    steps = steps_over()
    slabs, slab_rows, share, tile = grads.shape
    tile_rows, spread, angles = pattern.shape
    group, _, _ = out.shape
    tiles = out.shape[1] // slab_rows
    columns = angles * tile_rows // (slabs * share)
    greet_all(slab, chip, core)
    greeted(15)

    order = [1, 3, 4, 2, 5, 7, 6]
    slabs_, chips, pairs = {}, {}, {}
    for d in order:
        other = moved(slab, steps[d])
        slabs_[d] = remote(
            grads.at[other], mine.at[slab], slab_send.at[d], slab_recv.at[d], (other, column)
        )
        slabs_[d].start()
    mine[slab] = grads[slab]

    turned = jnp.concatenate(
        [
            pattern[:, :, base : base + tile].reshape(-1, tile).T
            for base in range(0, angles, tile)
        ],
        0,
    )
    turned = segment_of(turned, group, tiles)
    for d in range(tile_rows):
        index[pl.ds(d, angles, tile_rows), :spread] = turned[:, d * spread : (d + 1) * spread]

    for d in order:
        slabs_[d].wait_recv()
    for d in order:
        chips[d] = remote(
            mine, held.at[d], chip_send.at[d], chip_recv.at[d],
            (slab, 2 * moved(chip, steps[d]) + core),
        )
        chips[d].start()
    pairs[0] = remote(mine, twin.at[0], pair_send.at[0], pair_recv.at[0], sibling)
    pairs[0].start()

    row = lax.broadcasted_iota(jnp.int32, (tiles, 2 * slabs * share), 0)

    @pl.loop(0, columns // 2)
    def _(origin):
        wanted = jnp.concatenate(
            [
                index[pl.ds(pl.multiple_of((s * columns + 2 * origin + c) * share, share), share), :]
                for c in range(2)
                for s in range(slabs)
            ],
            0,
        ).T
        for k in range(group):
            held_here = jnp.zeros(row.shape, F32)
            for member in range(spread):
                held_here = held_here + jnp.where(
                    wanted[member : member + 1, :] == row + k * tiles, 1.0, 0.0
                )
            counts[origin, k * tiles : (k + 1) * tiles, :] = held_here.astype(BF16)

    def add(d, near, far):
        if d:
            origin = moved(chip, ((2 - steps[d][0]) % 2, (4 - steps[d][1]) % 4))
        else:
            origin = chip
        swapped = core == 1
        for z in range(0, slab_rows, 2):
            parts = []
            for more in range(2):
                a = near[:, z + more].reshape(slabs * share, tile)
                b = far[:, z + more].reshape(slabs * share, tile)
                parts.append(
                    jnp.concatenate([jnp.where(swapped, b, a), jnp.where(swapped, a, b)], 0)
                )
            right = jnp.concatenate(parts, 1)
            for base in range(0, group * tiles, 256):
                result = dot(counts[origin, base : base + 256, :], right)
                span = slice(base, base + 256)
                lanes = slice(z * tile, (z + 2) * tile)
                if d:
                    result = result + total[span, lanes]
                total[span, lanes] = result

    pending = 0
    for d in order + [None]:
        if d is not None:
            chips[d].wait_recv()
            pairs[d] = remote(held.at[d], twin.at[d], pair_send.at[d], pair_recv.at[d], sibling)
            pairs[d].start()
        pairs[pending].wait_recv()
        add(pending, held.at[pending] if pending else mine, twin.at[pending])
        pending = d

    for k in range(group):
        for z in range(slab_rows):
            block = total[k * tiles : (k + 1) * tiles, z * tile : (z + 1) * tile]
            flat[pl.ds(z, tiles, slab_rows), :] = block
        out[k] = flat[...].astype(BF16)

    for d in order:
        slabs_[d].wait_send()
        chips[d].wait_send()
    for d in [0] + order:
        pairs[d].wait_send()


def collect(grads, pattern, templates, tiles):
    slabs, slab_rows, share, tile = grads.shape
    group, tile_cells, _ = templates.shape
    tile_rows, spread, angles = pattern.shape
    columns = angles * tile_rows // (slabs * share)
    vector = pl.BlockSpec(memory_space=pltpu.VMEM)
    sem = pltpu.SemaphoreType.DMA((8,))
    return pl.pallas_call(
        collect_kernel,
        out_shape=jax.ShapeDtypeStruct((group, tiles * slab_rows, tile), BF16),
        in_specs=[vector, vector],
        out_specs=vector,
        scratch_shapes=[
            pltpu.VMEM(grads.shape, BF16),
            pltpu.VMEM((8,) + grads.shape, BF16),
            pltpu.VMEM((8,) + grads.shape, BF16),
            pltpu.VMEM((columns // 2, group * tiles, 2 * slabs * share), BF16),
            pltpu.VMEM((angles * tile_rows, tile), jnp.int32),
            pltpu.VMEM((group * tiles, slab_rows * tile), F32),
            pltpu.VMEM((tiles * slab_rows, tile), F32),
        ]
        + [sem] * 6,
        compiler_params=pltpu.CompilerParams(
            collective_id=2, has_side_effects=True, vmem_limit_bytes=48 * 2**20
        ),
    )(grads, pattern)


def update_kernel(sums, templates, volume, consensus, out):
    group, size, tile = sums.shape
    tile_cells = templates.shape[1]
    slab_rows = volume.shape[0]
    left = jnp.concatenate([sums[k] for k in range(group)], 1)
    for part in range(0, tile_cells, 256):
        total = jnp.zeros((size, 256), F32)
        for k in range(0, group, 2):
            right = jnp.concatenate(
                [templates[k, part : part + 256, :], templates[k + 1, part : part + 256, :]], 1
            )
            total = total + lax.dot_general(
                left[:, k * tile : (k + 2) * tile],
                right,
                (((1,), (1,)), ((), ())),
                preferred_element_type=F32,
            )
        for t in range(size // slab_rows):
            span = slice(t * tile_cells + part, t * tile_cells + part + 256)
            own_volume = volume[:, span].astype(F32)
            wanted = consensus[:, span].astype(F32)
            moved_by = total[t * slab_rows : (t + 1) * slab_rows]
            out[:, span] = own_volume - step_size * (moved_by + penalty * (own_volume - wanted))


def update(sums, templates, volume, consensus):
    slab_rows, cells = volume.shape
    group, height, tile = sums.shape
    steps = 4
    block = pl.BlockSpec((slab_rows, cells // steps), lambda i: (0, i))
    return pl.pallas_call(
        update_kernel,
        grid=(steps,),
        out_shape=jax.ShapeDtypeStruct((slab_rows, cells), F32),
        in_specs=[
            pl.BlockSpec((group, height // steps, tile), lambda i: (0, i, 0)),
            pl.BlockSpec(templates.shape, lambda i: (0, 0, 0)),
            block,
            block,
        ],
        out_specs=block,
        compiler_params=pltpu.CompilerParams(vmem_limit_bytes=48 * 2**20),
    )(sums, templates, volume, consensus)


def on_device(
    volume, consensus, templates, pattern, probe_wave, measured, scan_counts, scan_positions
):
    slab_rows = volume.shape[0]
    tile = templates.shape[2]
    slab_count = lax.axis_size("slab")
    column_count = lax.axis_size("col")
    angle_count, tile_rows, spread = pattern.shape[1:]
    per_owner = angle_count // (slab_count * column_count)
    own = per_owner * tile_rows
    rows = angle_count * tile_rows

    image, observed = forward(
        volume,
        templates,
        pattern[0].transpose(1, 2, 0),
        measured.transpose(0, 2, 3, 1),
        column_count,
        slab_count,
    )
    image = image.reshape(slab_count * slab_rows * own, tile)
    gradients = ptycho(image, probe_wave, observed, scan_counts, scan_positions)
    sums = collect(
        gradients.reshape(slab_count, slab_rows, own, tile),
        pattern[0].transpose(1, 2, 0),
        templates,
        volume.shape[1] // templates.shape[1],
    )
    return update(sums, templates, volume, consensus)


def solution(mesh):
    return jax.shard_map(
        on_device,
        mesh=mesh,
        in_specs=(
            P("slab", "col"),
            P("slab", "col"),
            P("col", None, None),
            P("col", None, None, None),
            P(),
            P(("slab", "col"), None, None, None),
            P(),
            P(),
        ),
        out_specs=P("slab", "col"),
        check_vma=False,
    )
```

```python
import functools
import math

import jax
import jax.numpy as jnp
import numpy as np
from jax import lax
from jax.experimental import pallas as pl
from jax.experimental.pallas import tpu as pltpu
from jax.sharding import PartitionSpec as P

BF16 = jnp.bfloat16
F32 = jnp.float32
GROUP = 64
step_size = 0.1
penalty = 1.0
I16 = jnp.int16
TURN = 65536 / (2 * math.pi)

def dot(left, right):
    return jnp.dot(left, right, preferred_element_type=F32)


def steps_over():
    return [(dx, dy) for dx in range(2) for dy in range(4)]


def moved(index, step):
    high, low = lax.div(index, 4), lax.rem(index, 4)
    return lax.rem(high + step[0], 2) * 4 + lax.rem(low + step[1], 4)


def greet_all(slab, chip, core):
    barrier = pltpu.get_barrier_semaphore()
    here = slab, 2 * chip + core
    others = [(slab, 2 * chip + 1 - core)]
    others += [(slab, 2 * moved(chip, step) + core) for step in steps_over()[1:]]
    others += [(moved(slab, step), here[1]) for step in steps_over()[1:]]
    for other in others:
        pl.semaphore_signal(barrier, inc=1, device_id=other, device_id_type=pl.DeviceIdType.MESH)


def greeted(number):
    pl.semaphore_wait(pltpu.get_barrier_semaphore(), number)


def remote(source, target, send, receive, device):
    return pltpu.make_async_remote_copy(
        src_ref=source,
        dst_ref=target,
        send_sem=send,
        recv_sem=receive,
        device_id=device,
        device_id_type=pl.DeviceIdType.MESH,
    )


def segment_of(entry, group, tiles):
    return (entry & (group - 1)) * tiles + lax.div(entry, group)


def forward_kernel(
    volume_in, templates_in, pattern, measured_in, image, observed,
    volume, templates, measured, turned_over, flat, table, counts, index, own, outgoing, pair, arrived, total,
    load_sem, pair_send, pair_recv, chip_send, chip_recv, slab_send, slab_recv,
):
    slab, column = lax.axis_index("slab"), lax.axis_index("col")
    chip, core = lax.div(column, 2), lax.rem(column, 2)
    slabs, slab_rows, share, tile = image.shape
    columns = 2 * own.shape[0]
    group, tile_cells, _ = templates.shape
    tiles = table.shape[0] // group
    tile_rows, spread, angles = pattern.shape
    half = measured.shape[1] // 2
    limit = measured.shape[3]
    quarter = volume.shape[1] // 4
    greet_all(slab, chip, core)

    loads = [pltpu.make_async_copy(templates_in, templates, load_sem.at[0])]
    for part in range(4):
        span = pl.ds(part * quarter, quarter)
        loads.append(
            pltpu.make_async_copy(volume_in.at[:, span], volume.at[:, span], load_sem.at[1 + part])
        )
    loads.append(pltpu.make_async_copy(measured_in, measured, load_sem.at[5]))
    for load in loads:
        load.start()

    turned = jnp.concatenate(
        [
            pattern[:, :, base : base + tile].reshape(-1, tile).T
            for base in range(0, angles, tile)
        ],
        0,
    )
    turned = segment_of(turned, group, tiles)
    for d in range(tile_rows):
        index[pl.ds(d, angles, tile_rows), :spread] = turned[:, d * spread : (d + 1) * spread]

    loads[0].wait()
    step = tiles // 4
    for part in range(4):
        loads[1 + part].wait()
        left = jnp.concatenate(
            [
                volume[:, t * tile_cells : (t + 1) * tile_cells].astype(F32)
                for t in range(part * step, (part + 1) * step)
            ],
            0,
        ).astype(BF16)
        span = slice(part * step * slab_rows, (part + 1) * step * slab_rows)
        for k in range(0, group, 2):
            result = dot(left, jnp.concatenate([templates[k], templates[k + 1]], 1))
            flat[k, span, :] = result[:, :tile]
            flat[k + 1, span, :] = result[:, tile:]
    for k in range(group):
        for z in range(slab_rows):
            block = flat[k, pl.ds(z, tiles, slab_rows), :]
            table[k * tiles : (k + 1) * tiles, z * tile : (z + 1) * tile] = block.astype(BF16)

    greeted(15)
    lane = lax.broadcasted_iota(jnp.int32, (2 * slabs * share, tiles), 1).astype(I16)
    one, zero = jnp.ones(lane.shape, BF16), jnp.zeros(lane.shape, BF16)

    def at_step(i):
        d = lax.rem(5 * i + 5, 8)
        high = lax.rem(lax.div(chip, 4) + lax.div(d, 4), 2)
        return d, 4 * high + lax.rem(chip + d, 4)

    def to_pair(d):
        return remote(
            outgoing.at[d], pair.at[d], pair_send.at[d], pair_recv.at[d],
            (slab, 2 * chip + 1 - core),
        )

    def to_chip(d, target):
        return remote(
            own.at[d], arrived.at[d], chip_send.at[d], chip_recv.at[d], (slab, 2 * target + core)
        )

    def compute(i):
        d, target = at_step(i)
        wanted = jnp.concatenate(
            [
                index[pl.ds(pl.multiple_of((s * columns + 2 * target + c) * share, share), share), :]
                for c in (core, 1 - core)
                for s in range(slabs)
            ],
            0,
        )
        wide = [
            jnp.broadcast_to(wanted[:, member : member + 1], lane.shape).astype(I16)
            for member in range(spread)
        ]
        for k in range(group):
            held = zero
            for member in range(spread):
                held = held + jnp.where(wide[member] == lane + I16(k * tiles), one, zero)
            counts[:, k * tiles : (k + 1) * tiles] = held
        for z in range(0, slab_rows, 2):
            result = dot(counts[...], table[:, z * tile : (z + 2) * tile])
            result = jnp.floor(result * TURN + 0.5).astype(jnp.int32).astype(I16)
            for more in range(2):
                part = result[:, more * tile : (more + 1) * tile]
                own[d, z + more] = part[: slabs * share].reshape(slabs, share, tile)
                outgoing[d, z + more] = part[slabs * share :].reshape(slabs, share, tile)
        to_pair(d).start()

    def combine(i):
        d, target = at_step(i)
        to_pair(d).wait_recv()

        @pl.loop(0, slab_rows)
        def _(z):
            own[d, z] = own[d, z] + pair[d, z]

        @pl.when(i < 7)
        def _():
            to_chip(d, target).start()

    @pl.loop(0, 9)
    def _(i):
        @pl.when(i < 8)
        def _():
            compute(i)

        @pl.when(i > 0)
        def _():
            combine(i - 1)

    loads[5].wait()
    stores = []
    for slot in range(measured.shape[0]):

        @pl.loop(0, half)
        def _(row):
            both = jnp.concatenate([measured[slot, row], measured[slot, row + half]], 0)
            turned_over[slot, pl.ds(row, limit, half), :] = both.T

        stores.append(
            pltpu.make_async_copy(turned_over.at[slot], observed.at[slot], load_sem.at[6 + slot])
        )
        stores[-1].start()

    for i in range(7):
        d, target = at_step(i)
        to_chip(d, target).wait_recv()

    @pl.loop(0, slab_rows)
    def _(z):
        value = own[0, z]
        for d in range(1, 8):
            value = value + arrived[d, z]
        total[:, z] = value

    slabs_ = []
    for d in range(1, 8):
        other = moved(slab, steps_over()[d])
        slabs_.append(
            remote(total.at[other], image.at[slab], slab_send.at[d], slab_recv.at[d], (other, column))
        )
        slabs_[-1].start()
    image[slab] = total[slab]
    for i in range(8):
        d, target = at_step(i)
        to_pair(d).wait_send()
        if i < 7:
            to_chip(d, target).wait_send()
    for copy in slabs_ + stores:
        copy.wait()


def forward(volume, templates, pattern, measured, columns, slabs):
    slab_rows, cells = volume.shape
    group, tile_cells, tile = templates.shape
    tiles = cells // tile_cells
    tile_rows, spread, angles = pattern.shape
    slots, size, _, limit = measured.shape
    rows = angles * tile_rows
    share = rows // (columns * slabs)
    block = (columns // 2, slab_rows, slabs, share, tile)
    vector = pl.BlockSpec(memory_space=pltpu.VMEM)
    anywhere = pl.BlockSpec(memory_space=pl.ANY)
    sem = pltpu.SemaphoreType.DMA((8,))
    return pl.pallas_call(
        forward_kernel,
        out_shape=(
            jax.ShapeDtypeStruct((slabs, slab_rows, share, tile), I16),
            jax.ShapeDtypeStruct((slots, limit * size // 2, 2 * size), F32),
        ),
        in_specs=[anywhere, anywhere, vector, anywhere],
        out_specs=(vector, anywhere),
        scratch_shapes=[
            pltpu.VMEM(volume.shape, BF16),
            pltpu.VMEM(templates.shape, BF16),
            pltpu.VMEM(measured.shape, F32),
            pltpu.VMEM((slots, limit * size // 2, 2 * size), F32),
            pltpu.VMEM((group, tiles * slab_rows, tile), F32),
            pltpu.VMEM((group * tiles, slab_rows * tile), BF16),
            pltpu.VMEM((2 * slabs * share, group * tiles), BF16),
            pltpu.VMEM((rows, tile), jnp.int32),
        ]
        + [pltpu.VMEM(block, I16)] * 4
        + [pltpu.VMEM((slabs, slab_rows, share, tile), I16)]
        + [sem] * 7,
        compiler_params=pltpu.CompilerParams(
            collective_id=1, has_side_effects=True, vmem_limit_bytes=56 * 2**20
        ),
    )(volume, templates, pattern, measured)


def trig_coefficients():
    grid = (np.cos(np.pi * (np.arange(400) + 0.5) / 400) + 1.0) * (np.pi * np.pi * 0.5005)
    root = np.sqrt(grid)
    sine = np.polynomial.Polynomial.fit(grid, np.sin(root) / root, 6).convert().coef
    cosine = np.polynomial.Polynomial.fit(grid, np.cos(root), 7).convert().coef
    return [float(v) for v in sine], [float(v) for v in cosine]


def sine_cosine(angle):
    sine, cosine = trig_coefficients()
    square = angle * angle
    sine_value = jnp.full_like(square, sine[-1])
    for value in sine[-2::-1]:
        sine_value = sine_value * square + value
    cosine_value = jnp.full_like(square, cosine[-1])
    for value in cosine[-2::-1]:
        cosine_value = cosine_value * square + value
    return sine_value * angle, cosine_value


def split_bf16(table):
    high = table.astype(np.float32).astype(BF16)
    low = (table - high.astype(np.float64)).astype(np.float32).astype(BF16)
    return high, low


def transform_tables(size):
    index = np.arange(size)
    radians = 2.0 * np.pi / size * (index[:, None] * index[None, :] % size)
    cosine = np.cos(radians) / math.sqrt(size)
    sine = np.sin(radians) / math.sqrt(size)
    zero = np.zeros_like(cosine)
    forward = np.block([[cosine, -sine], [sine, cosine]])
    pair = np.block([[cosine, zero, sine, zero], [zero, cosine, zero, sine]])
    back = np.block([[2 * sine, -2 * cosine], [2 * cosine, 2 * sine]])
    f_high, f_low = split_bf16(forward)
    p_high, p_low = split_bf16(pair)
    b_high, b_low = split_bf16(back)
    lanes = np.concatenate([f_high, f_low], 1)
    back = np.concatenate([b_high, b_low], 1)
    return (
        np.concatenate([lanes, lanes], 0),
        np.concatenate([p_high, p_high], 0),
        np.concatenate([p_high, p_low], 0),
        np.concatenate([back, back], 0),
    )


def halves(value):
    high = value.astype(BF16)
    low = (value - high.astype(F32)).astype(BF16)
    return high, low


def ptycho_kernel(
    counts, starts_in, image, probe_wave, t_first, t_pair, t_pair_both, t_back, observed_in,
    out, waves, total, staged, probe_a, probe_b, observed, starts, landed, here,
):
    slots = observed.shape[0]
    size = probe_wave.shape[1]
    limit = starts.shape[1]
    owner = lax.axis_index("slab") * lax.axis_size("col") + lax.axis_index("col")
    first_angle = owner * slots
    first_row = lax.div(first_angle, 8) * 8
    load = pltpu.make_async_copy(starts_in.at[pl.ds(pl.multiple_of(first_row, 8), 8)], starts, landed)
    load.start()
    fetches = [
        pltpu.make_async_copy(observed_in.at[slot], observed.at[slot], here.at[slot])
        for slot in range(slots)
    ]
    for fetch in fetches:
        fetch.start()
    both = jnp.concatenate([probe_wave[0], probe_wave[0]], 0)
    probe_a[...] = both.T
    both = jnp.concatenate([-probe_wave[1], probe_wave[1]], 0)
    probe_b[...] = both.T
    width = waves.shape[0]
    tile = image.shape[1]
    rows = width // tile * slots
    chunk_count = limit // GROUP

    def used_chunks(slot):
        return jnp.clip(lax.div(counts[first_angle + slot] + (GROUP - 1), GROUP), 0, chunk_count)

    half = size // 2

    staged[...] = image[...].astype(jnp.int32).astype(F32) * (2 * math.pi / 65536)
    load.wait()
    lane = lax.broadcasted_iota(jnp.int32, (size, 2 * size), 1)

    @pl.loop(0, slots)
    def _(slot):
        pltpu.make_async_copy(observed_in.at[slot], observed.at[slot], here.at[slot]).wait()
        for part in range(width // tile):
            sine, cosine = sine_cosine(staged[pl.ds(slot * (width // tile) + part, size, rows), :])
            waves[part * tile : (part + 1) * tile, :] = jnp.concatenate([cosine, sine], 0).T
        total[...] = jnp.zeros_like(total)
        count = counts[first_angle + slot]

        @pl.loop(0, used_chunks(slot))
        def _(chunk):
            begin = chunk * GROUP
            at = [starts[first_angle - first_row + slot, begin + member] for member in range(GROUP)]
            exits = []
            for member in range(GROUP):
                patch = waves[pl.ds(at[member], size), :]
                exits.append(probe_a[...] * patch + probe_b[...] * pltpu.roll(patch, size, 1))
            exit_wave = jnp.concatenate(exits, 0)
            high, low = halves(exit_wave)
            first = dot(jnp.concatenate([high, low], 1), t_first[...])
            first = first[:, : 2 * size] + first[:, 2 * size :]
            turned = jnp.concatenate(
                [first[pair * 2 * size : (pair + 1) * 2 * size].T for pair in range(GROUP // 2)], 0
            )
            high, low = halves(turned)
            second = dot(jnp.concatenate([high, low], 1), t_pair[...])
            second = second + dot(high, t_pair_both[2 * size :, :])
            scaled = []
            for pair in range(GROUP // 2):
                block = second[pair * 2 * size : (pair + 1) * 2 * size]
                real = block[:size, : 2 * size] + block[size:, 2 * size :]
                imag = block[size:, : 2 * size] - block[:size, 2 * size :]
                member = begin + 2 * pair
                seen = [
                    observed[slot, pl.ds(pl.multiple_of((member + m) * half, half), half), :]
                    for m in range(2)
                ]
                seen = jnp.concatenate(
                    [
                        jnp.concatenate([seen[0][:, :size], seen[1][:, :size]], 1),
                        jnp.concatenate([seen[0][:, size:], seen[1][:, size:]], 1),
                    ],
                    0,
                )
                residual = real * real + imag * imag - seen
                live = member + jnp.where(lane >= size, 1, 0) < count
                residual = jnp.where(live, residual, 0.0)
                scaled += [residual * real, residual * imag]
            scaled = jnp.concatenate(scaled, 0).astype(BF16)
            third = dot(jnp.concatenate([scaled, scaled], 1), t_pair_both[...])
            turned = []
            for pair in range(GROUP // 2):
                block = third[pair * 2 * size : (pair + 1) * 2 * size]
                real = block[:size, : 2 * size] - block[size:, 2 * size :]
                imag = block[size:, : 2 * size] + block[:size, 2 * size :]
                turned.append(jnp.concatenate([real, imag], 0).T)
            high, low = halves(jnp.concatenate(turned, 0))
            back = dot(jnp.concatenate([high, low], 1), t_back[...])
            gradient = exit_wave * (back[:, : 2 * size] + back[:, 2 * size :])
            for member in range(GROUP):
                span = pl.ds(at[member], size)
                total[span, :] = total[span, :] + gradient[member * size : (member + 1) * size]

        for part in range(width // tile):
            flat = total[part * tile : (part + 1) * tile, :].T
            staged[pl.ds(slot * (width // tile) + part, size, rows), :] = flat[:size] + flat[size:]

    out[...] = staged[...].astype(BF16)


def ptycho(image, probe_wave, observed, counts, starts):
    slots = observed.shape[0]
    size = probe_wave.shape[1]
    height, tile = image.shape
    width = height // size // slots * tile
    tables = [jnp.asarray(table) for table in transform_tables(size)]
    vector = pl.BlockSpec(memory_space=pltpu.VMEM)
    return pl.pallas_call(
        ptycho_kernel,
        out_shape=jax.ShapeDtypeStruct((height, tile), BF16),
        in_specs=[pl.BlockSpec(memory_space=pltpu.SMEM), pl.BlockSpec(memory_space=pl.ANY)]
        + [vector] * 6
        + [pl.BlockSpec(memory_space=pl.ANY)],
        out_specs=vector,
        scratch_shapes=[
            pltpu.VMEM((width, 2 * size), F32),
            pltpu.VMEM((width, 2 * size), F32),
            pltpu.VMEM((height, tile), F32),
            pltpu.VMEM((size, 2 * size), F32),
            pltpu.VMEM((size, 2 * size), F32),
            pltpu.VMEM(observed.shape, F32),
            pltpu.SMEM((8, starts.shape[1]), jnp.int32),
            pltpu.SemaphoreType.DMA,
            pltpu.SemaphoreType.DMA((slots,)),
        ],
        compiler_params=pltpu.CompilerParams(vmem_limit_bytes=56 * 2**20),
    )(counts, starts, image, probe_wave, *tables, observed)


def collect_kernel(
    grads, pattern, out, mine, held, twin, counts, index, total, flat,
    slab_send, slab_recv, chip_send, chip_recv, pair_send, pair_recv,
):
    slab, column = lax.axis_index("slab"), lax.axis_index("col")
    chip, core = lax.div(column, 2), lax.rem(column, 2)
    sibling = (slab, 2 * chip + 1 - core)
    steps = steps_over()
    slabs, slab_rows, share, tile = grads.shape
    tile_rows, spread, angles = pattern.shape
    group, _, _ = out.shape
    tiles = out.shape[1] // slab_rows
    columns = angles * tile_rows // (slabs * share)
    greet_all(slab, chip, core)
    greeted(15)

    order = [1, 3, 4, 2, 5, 7, 6]
    slabs_, chips, pairs = {}, {}, {}
    for d in order:
        other = moved(slab, steps[d])
        slabs_[d] = remote(
            grads.at[other], mine.at[slab], slab_send.at[d], slab_recv.at[d], (other, column)
        )
        slabs_[d].start()
    mine[slab] = grads[slab]

    turned = jnp.concatenate(
        [
            pattern[:, :, base : base + tile].reshape(-1, tile).T
            for base in range(0, angles, tile)
        ],
        0,
    )
    turned = segment_of(turned, group, tiles)
    for d in range(tile_rows):
        index[pl.ds(d, angles, tile_rows), :spread] = turned[:, d * spread : (d + 1) * spread]

    for d in order:
        slabs_[d].wait_recv()
    for d in order:
        chips[d] = remote(
            mine, held.at[d], chip_send.at[d], chip_recv.at[d],
            (slab, 2 * moved(chip, steps[d]) + core),
        )
        chips[d].start()
    pairs[0] = remote(mine, twin.at[0], pair_send.at[0], pair_recv.at[0], sibling)
    pairs[0].start()

    row = lax.broadcasted_iota(jnp.int32, (tiles, 2 * slabs * share), 0).astype(I16)
    one, zero = jnp.ones(row.shape, BF16), jnp.zeros(row.shape, BF16)

    @pl.loop(0, columns // 2)
    def _(origin):
        wanted = jnp.concatenate(
            [
                index[pl.ds(pl.multiple_of((s * columns + 2 * origin + c) * share, share), share), :]
                for c in range(2)
                for s in range(slabs)
            ],
            0,
        ).T
        wide = [
            jnp.broadcast_to(wanted[member : member + 1, :], row.shape).astype(I16)
            for member in range(spread)
        ]
        for k in range(group):
            held_here = zero
            for member in range(spread):
                held_here = held_here + jnp.where(wide[member] == row + I16(k * tiles), one, zero)
            counts[origin, k * tiles : (k + 1) * tiles, :] = held_here

    def add(d, near, far):
        if d:
            origin = moved(chip, ((2 - steps[d][0]) % 2, (4 - steps[d][1]) % 4))
        else:
            origin = chip
        swapped = core == 1
        for z in range(0, slab_rows, 2):
            parts = []
            for more in range(2):
                a = near[:, z + more].reshape(slabs * share, tile)
                b = far[:, z + more].reshape(slabs * share, tile)
                parts.append(
                    jnp.concatenate([jnp.where(swapped, b, a), jnp.where(swapped, a, b)], 0)
                )
            right = jnp.concatenate(parts, 1)
            for base in range(0, group * tiles, 256):
                result = dot(counts[origin, base : base + 256, :], right)
                span = slice(base, base + 256)
                lanes = slice(z * tile, (z + 2) * tile)
                if d:
                    result = result + total[span, lanes]
                total[span, lanes] = result

    pending = 0
    for d in order + [None]:
        if d is not None:
            chips[d].wait_recv()
            pairs[d] = remote(held.at[d], twin.at[d], pair_send.at[d], pair_recv.at[d], sibling)
            pairs[d].start()
        pairs[pending].wait_recv()
        add(pending, held.at[pending] if pending else mine, twin.at[pending])
        pending = d

    for k in range(group):
        for z in range(slab_rows):
            block = total[k * tiles : (k + 1) * tiles, z * tile : (z + 1) * tile]
            flat[pl.ds(z, tiles, slab_rows), :] = block
        out[k] = flat[...].astype(BF16)

    for d in order:
        slabs_[d].wait_send()
        chips[d].wait_send()
    for d in [0] + order:
        pairs[d].wait_send()


def collect(grads, pattern, templates, tiles):
    slabs, slab_rows, share, tile = grads.shape
    group, tile_cells, _ = templates.shape
    tile_rows, spread, angles = pattern.shape
    columns = angles * tile_rows // (slabs * share)
    vector = pl.BlockSpec(memory_space=pltpu.VMEM)
    sem = pltpu.SemaphoreType.DMA((8,))
    return pl.pallas_call(
        collect_kernel,
        out_shape=jax.ShapeDtypeStruct((group, tiles * slab_rows, tile), BF16),
        in_specs=[vector, vector],
        out_specs=vector,
        scratch_shapes=[
            pltpu.VMEM(grads.shape, BF16),
            pltpu.VMEM((8,) + grads.shape, BF16),
            pltpu.VMEM((8,) + grads.shape, BF16),
            pltpu.VMEM((columns // 2, group * tiles, 2 * slabs * share), BF16),
            pltpu.VMEM((angles * tile_rows, tile), jnp.int32),
            pltpu.VMEM((group * tiles, slab_rows * tile), F32),
            pltpu.VMEM((tiles * slab_rows, tile), F32),
        ]
        + [sem] * 6,
        compiler_params=pltpu.CompilerParams(
            collective_id=2, has_side_effects=True, vmem_limit_bytes=56 * 2**20
        ),
    )(grads, pattern)


def update_kernel(sums, templates, volume, consensus, out):
    group, size, tile = sums.shape
    tile_cells = templates.shape[1]
    slab_rows = volume.shape[0]
    left = jnp.concatenate([sums[k] for k in range(group)], 1)
    for part in range(0, tile_cells, 256):
        total = jnp.zeros((size, 256), F32)
        for k in range(0, group, 2):
            right = jnp.concatenate(
                [templates[k, part : part + 256, :], templates[k + 1, part : part + 256, :]], 1
            )
            total = total + lax.dot_general(
                left[:, k * tile : (k + 2) * tile],
                right,
                (((1,), (1,)), ((), ())),
                preferred_element_type=F32,
            )
        for t in range(size // slab_rows):
            span = slice(t * tile_cells + part, t * tile_cells + part + 256)
            own_volume = volume[:, span].astype(F32)
            wanted = consensus[:, span].astype(F32)
            moved_by = total[t * slab_rows : (t + 1) * slab_rows]
            out[:, span] = own_volume - step_size * (moved_by + penalty * (own_volume - wanted))


def update(sums, templates, volume, consensus):
    slab_rows, cells = volume.shape
    group, height, tile = sums.shape
    steps = 4
    block = pl.BlockSpec((slab_rows, cells // steps), lambda i: (0, i))
    return pl.pallas_call(
        update_kernel,
        grid=(steps,),
        out_shape=jax.ShapeDtypeStruct((slab_rows, cells), F32),
        in_specs=[
            pl.BlockSpec((group, height // steps, tile), lambda i: (0, i, 0)),
            pl.BlockSpec(templates.shape, lambda i: (0, 0, 0)),
            block,
            block,
        ],
        out_specs=block,
        compiler_params=pltpu.CompilerParams(vmem_limit_bytes=56 * 2**20),
    )(sums, templates, volume, consensus)


def on_device(
    volume, consensus, templates, pattern, probe_wave, measured, scan_counts, scan_positions
):
    slab_rows = volume.shape[0]
    tile = templates.shape[2]
    slab_count = lax.axis_size("slab")
    column_count = lax.axis_size("col")
    angle_count, tile_rows, spread = pattern.shape[1:]
    per_owner = angle_count // (slab_count * column_count)
    own = per_owner * tile_rows
    rows = angle_count * tile_rows

    image, observed = forward(
        volume,
        templates,
        pattern[0].transpose(1, 2, 0),
        measured.transpose(0, 2, 3, 1),
        column_count,
        slab_count,
    )
    image = image.reshape(slab_count * slab_rows * own, tile)
    gradients = ptycho(image, probe_wave, observed, scan_counts, scan_positions)
    sums = collect(
        gradients.reshape(slab_count, slab_rows, own, tile),
        pattern[0].transpose(1, 2, 0),
        templates,
        volume.shape[1] // templates.shape[1],
    )
    return update(sums, templates, volume, consensus)


def solution(mesh):
    return jax.shard_map(
        on_device,
        mesh=mesh,
        in_specs=(
            P("slab", "col"),
            P("slab", "col"),
            P("col", None, None),
            P("col", None, None, None),
            P(),
            P(("slab", "col"), None, None, None),
            P(),
            P(),
        ),
        out_specs=P("slab", "col"),
        check_vma=False,
    )
```

```python
import functools
import math

import jax
import jax.numpy as jnp
import numpy as np
from jax import lax
from jax.experimental import pallas as pl
from jax.experimental.pallas import tpu as pltpu
from jax.sharding import PartitionSpec as P

BF16 = jnp.bfloat16
F32 = jnp.float32
GROUP = 64
step_size = 0.1
penalty = 1.0
I16 = jnp.int16
TURN = 65536 / (2 * math.pi)

def dot(left, right):
    return jnp.dot(left, right, preferred_element_type=F32)


def steps_over():
    return [(dx, dy) for dx in range(2) for dy in range(4)]


def moved(index, step):
    high, low = lax.div(index, 4), lax.rem(index, 4)
    return lax.rem(high + step[0], 2) * 4 + lax.rem(low + step[1], 4)


def greet_near(slab, chip, core):
    barrier = pltpu.get_barrier_semaphore()
    column = 2 * chip + core
    others = [(slab, 2 * chip + 1 - core)]
    others += [(slab, 2 * moved(chip, step) + core) for step in steps_over()[1:5]]
    others += [(moved(slab, step), column) for step in steps_over()[1:]]
    for other in others:
        pl.semaphore_signal(barrier, inc=1, device_id=other, device_id_type=pl.DeviceIdType.MESH)


def greeted(number):
    pl.semaphore_wait(pltpu.get_barrier_semaphore(), number)


def remote(source, target, send, receive, device):
    return pltpu.make_async_remote_copy(
        src_ref=source,
        dst_ref=target,
        send_sem=send,
        recv_sem=receive,
        device_id=device,
        device_id_type=pl.DeviceIdType.MESH,
    )


def segment_of(entry, group, tiles):
    return (entry & (group - 1)) * tiles + lax.div(entry, group)


def forward_kernel(
    volume_in, templates_in, pattern, measured_in, image, observed,
    volume, templates, measured, turned_over, flat, table, counts, index, own, outgoing, pair, from_y, from_x, total,
    load_sem, pair_send, pair_recv, x_send, x_recv, y_send, y_recv, slab_send, slab_recv,
):
    slab, column = lax.axis_index("slab"), lax.axis_index("col")
    chip, core = lax.div(column, 2), lax.rem(column, 2)
    slabs, slab_rows, share, tile = image.shape
    columns = 2 * own.shape[0]
    group, tile_cells, _ = templates.shape
    tiles = table.shape[0] // group
    tile_rows, spread, angles = pattern.shape
    half = measured.shape[1] // 2
    limit = measured.shape[3]
    quarter = volume.shape[1] // 4
    greet_near(slab, chip, core)

    loads = [pltpu.make_async_copy(templates_in, templates, load_sem.at[0])]
    for part in range(4):
        span = pl.ds(part * quarter, quarter)
        loads.append(
            pltpu.make_async_copy(volume_in.at[:, span], volume.at[:, span], load_sem.at[1 + part])
        )
    loads.append(pltpu.make_async_copy(measured_in, measured, load_sem.at[5]))
    for load in loads:
        load.start()

    turned = jnp.concatenate(
        [
            pattern[:, :, base : base + tile].reshape(-1, tile).T
            for base in range(0, angles, tile)
        ],
        0,
    )
    turned = segment_of(turned, group, tiles)
    for d in range(tile_rows):
        index[pl.ds(d, angles, tile_rows), :spread] = turned[:, d * spread : (d + 1) * spread]

    loads[0].wait()
    step = tiles // 4
    for part in range(4):
        loads[1 + part].wait()
        left = jnp.concatenate(
            [
                volume[:, t * tile_cells : (t + 1) * tile_cells].astype(F32)
                for t in range(part * step, (part + 1) * step)
            ],
            0,
        ).astype(BF16)
        span = slice(part * step * slab_rows, (part + 1) * step * slab_rows)
        for k in range(0, group, 2):
            result = dot(left, jnp.concatenate([templates[k], templates[k + 1]], 1))
            flat[k, span, :] = result[:, :tile]
            flat[k + 1, span, :] = result[:, tile:]
    for k in range(group):
        for z in range(slab_rows):
            block = flat[k, pl.ds(z, tiles, slab_rows), :]
            table[k * tiles : (k + 1) * tiles, z * tile : (z + 1) * tile] = block.astype(BF16)

    greeted(12)
    lane = lax.broadcasted_iota(jnp.int32, (2 * slabs * share, tiles), 1).astype(I16)
    one, zero = jnp.ones(lane.shape, BF16), jnp.zeros(lane.shape, BF16)

    low, high = slice(0, slab_rows // 2), slice(slab_rows // 2, slab_rows)
    across = (slab, 2 * moved(chip, (1, 0)) + core)

    def at_step(i):
        dy = lax.rem(i + 1, 4)
        far = 1 - lax.div(i, 4)
        ahead = lax.rem(lax.div(chip, 4) + far, 2)
        return 4 * far + dy, dy, 4 * ahead + lax.rem(chip + dy, 4)

    def along(dy):
        return (slab, 2 * (4 * lax.div(chip, 4) + lax.rem(chip + dy, 4)) + core)

    def to_pair(d):
        return remote(
            outgoing.at[d], pair.at[d], pair_send.at[d], pair_recv.at[d],
            (slab, 2 * chip + 1 - core),
        )

    def low_across(dy):
        return remote(
            own.at[4 + dy, low], from_x.at[dy, low], x_send.at[dy], x_recv.at[dy], across
        )

    def low_along(dy):
        return remote(own.at[dy, low], from_y.at[dy, low], y_send.at[dy], y_recv.at[dy], along(dy))

    def high_along(d, dy):
        return remote(
            own.at[d, high], from_y.at[d, high], y_send.at[8 + d], y_recv.at[8 + d], along(dy)
        )

    def high_across():
        return remote(own.at[4, high], from_x.at[0, high], x_send.at[4], x_recv.at[4], across)

    def compute(i):
        d, _, target = at_step(i)
        wanted = jnp.concatenate(
            [
                index[pl.ds(pl.multiple_of((s * columns + 2 * target + c) * share, share), share), :]
                for c in (core, 1 - core)
                for s in range(slabs)
            ],
            0,
        )
        wide = [
            jnp.broadcast_to(wanted[:, member : member + 1], lane.shape).astype(I16)
            for member in range(spread)
        ]
        for k in range(group):
            held = zero
            for member in range(spread):
                held = held + jnp.where(wide[member] == lane + I16(k * tiles), one, zero)
            counts[:, k * tiles : (k + 1) * tiles] = held
        for z in range(0, slab_rows, 2):
            result = dot(counts[...], table[:, z * tile : (z + 2) * tile])
            result = jnp.floor(result * TURN + 0.5).astype(jnp.int32).astype(I16)
            for more in range(2):
                part = result[:, more * tile : (more + 1) * tile]
                own[d, z + more] = part[: slabs * share].reshape(slabs, share, tile)
                outgoing[d, z + more] = part[slabs * share :].reshape(slabs, share, tile)
        to_pair(d).start()

    def combine(i):
        d, dy, _ = at_step(i)
        to_pair(d).wait_recv()

        @pl.loop(0, slab_rows)
        def _(z):
            own[d, z] = own[d, z] + pair[d, z]

        @pl.when(lax.rem(i, 4) < 3)
        def _():
            high_along(d, dy).start()

        @pl.when(i < 4)
        def _():
            low_across(dy).start()

        @pl.when(i > 3)
        def _():
            low_across(dy).wait_recv()

            @pl.loop(0, slab_rows // 2)
            def _(z):
                own[dy, z] = own[dy, z] + from_x[dy, z]

        @pl.when((i > 3) & (i < 7))
        def _():
            low_along(dy).start()

    @pl.loop(0, 9)
    def _(i):
        @pl.when(i < 8)
        def _():
            compute(i)

        @pl.when(i > 0)
        def _():
            combine(i - 1)

    for dy in range(1, 4):
        high_along(4 + dy, dy).wait_recv()

    @pl.loop(slab_rows // 2, slab_rows)
    def _(z):
        value = own[4, z]
        for dy in range(1, 4):
            value = value + from_y[4 + dy, z]
        own[4, z] = value

    high_across().start()

    loads[5].wait()
    stores = []
    for slot in range(measured.shape[0]):

        @pl.loop(0, half)
        def _(row):
            both = jnp.concatenate([measured[slot, row], measured[slot, row + half]], 0)
            turned_over[slot, pl.ds(row, limit, half), :] = both.T

        stores.append(
            pltpu.make_async_copy(turned_over.at[slot], observed.at[slot], load_sem.at[6 + slot])
        )
        stores[-1].start()

    def to_slab(d, part):
        other = moved(slab, steps_over()[d])
        side = (low, high)[part]
        number = 8 * part + d
        return remote(
            total.at[other, side], image.at[slab, side], slab_send.at[number], slab_recv.at[number],
            (other, column),
        )

    for part in range(2):
        for dy in range(1, 4):
            if part:
                high_along(dy, dy).wait_recv()
            else:
                low_along(dy).wait_recv()
        if part:
            high_across().wait_recv()

        @pl.loop(part * slab_rows // 2, (part + 1) * slab_rows // 2)
        def _(z):
            value = own[0, z]
            for dy in range(1, 4):
                value = value + from_y[dy, z]
            if part:
                value = value + from_x[0, z]
            total[:, z] = value

        for d in range(1, 8):
            to_slab(d, part).start()

    image[slab] = total[slab]
    for d in range(8):
        to_pair(d).wait_send()
    for dy in range(4):
        low_across(dy).wait_send()
        if dy:
            low_along(dy).wait_send()
            high_along(dy, dy).wait_send()
            high_along(4 + dy, dy).wait_send()
    high_across().wait_send()
    for part in range(2):
        for d in range(1, 8):
            to_slab(d, part).wait()
    for copy in stores:
        copy.wait()


def forward(volume, templates, pattern, measured, columns, slabs):
    slab_rows, cells = volume.shape
    group, tile_cells, tile = templates.shape
    tiles = cells // tile_cells
    tile_rows, spread, angles = pattern.shape
    slots, size, _, limit = measured.shape
    rows = angles * tile_rows
    share = rows // (columns * slabs)
    block = (columns // 2, slab_rows, slabs, share, tile)
    vector = pl.BlockSpec(memory_space=pltpu.VMEM)
    anywhere = pl.BlockSpec(memory_space=pl.ANY)
    sem = pltpu.SemaphoreType.DMA((8,))
    return pl.pallas_call(
        forward_kernel,
        out_shape=(
            jax.ShapeDtypeStruct((slabs, slab_rows, share, tile), I16),
            jax.ShapeDtypeStruct((slots, limit * size // 2, 2 * size), F32),
        ),
        in_specs=[anywhere, anywhere, vector, anywhere],
        out_specs=(vector, anywhere),
        scratch_shapes=[
            pltpu.VMEM(volume.shape, BF16),
            pltpu.VMEM(templates.shape, BF16),
            pltpu.VMEM(measured.shape, F32),
            pltpu.VMEM((slots, limit * size // 2, 2 * size), F32),
            pltpu.VMEM((group, tiles * slab_rows, tile), F32),
            pltpu.VMEM((group * tiles, slab_rows * tile), BF16),
            pltpu.VMEM((2 * slabs * share, group * tiles), BF16),
            pltpu.VMEM((rows, tile), jnp.int32),
        ]
        + [pltpu.VMEM(block, I16)] * 4
        + [pltpu.VMEM((4,) + block[1:], I16)]
        + [pltpu.VMEM((slabs, slab_rows, share, tile), I16)]
        + [sem] * 5
        + [pltpu.SemaphoreType.DMA((16,))] * 4,
        compiler_params=pltpu.CompilerParams(
            collective_id=1, has_side_effects=True, vmem_limit_bytes=56 * 2**20
        ),
    )(volume, templates, pattern, measured)


def trig_coefficients():
    grid = (np.cos(np.pi * (np.arange(400) + 0.5) / 400) + 1.0) * (np.pi * np.pi * 0.5005)
    root = np.sqrt(grid)
    sine = np.polynomial.Polynomial.fit(grid, np.sin(root) / root, 6).convert().coef
    cosine = np.polynomial.Polynomial.fit(grid, np.cos(root), 7).convert().coef
    return [float(v) for v in sine], [float(v) for v in cosine]


def sine_cosine(angle):
    sine, cosine = trig_coefficients()
    square = angle * angle
    sine_value = jnp.full_like(square, sine[-1])
    for value in sine[-2::-1]:
        sine_value = sine_value * square + value
    cosine_value = jnp.full_like(square, cosine[-1])
    for value in cosine[-2::-1]:
        cosine_value = cosine_value * square + value
    return sine_value * angle, cosine_value


def split_bf16(table):
    high = table.astype(np.float32).astype(BF16)
    low = (table - high.astype(np.float64)).astype(np.float32).astype(BF16)
    return high, low


def transform_tables(size):
    index = np.arange(size)
    radians = 2.0 * np.pi / size * (index[:, None] * index[None, :] % size)
    cosine = np.cos(radians) / math.sqrt(size)
    sine = np.sin(radians) / math.sqrt(size)
    zero = np.zeros_like(cosine)
    forward = np.block([[cosine, -sine], [sine, cosine]])
    pair = np.block([[cosine, zero, sine, zero], [zero, cosine, zero, sine]])
    back = np.block([[2 * sine, -2 * cosine], [2 * cosine, 2 * sine]])
    f_high, f_low = split_bf16(forward)
    p_high, p_low = split_bf16(pair)
    b_high, b_low = split_bf16(back)
    lanes = np.concatenate([f_high, f_low], 1)
    back = np.concatenate([b_high, b_low], 1)
    return (
        np.concatenate([lanes, lanes], 0),
        np.concatenate([p_high, p_high], 0),
        np.concatenate([p_high, p_low], 0),
        np.concatenate([back, back], 0),
    )


def halves(value):
    high = value.astype(BF16)
    low = (value - high.astype(F32)).astype(BF16)
    return high, low


def ptycho_kernel(
    counts, starts_in, image, probe_wave, t_first, t_pair, t_pair_both, t_back, observed_in,
    out, waves, total, staged, probe_a, probe_b, observed, starts, landed, here,
):
    slots = observed.shape[0]
    size = probe_wave.shape[1]
    limit = starts.shape[1]
    owner = lax.axis_index("slab") * lax.axis_size("col") + lax.axis_index("col")
    first_angle = owner * slots
    first_row = lax.div(first_angle, 8) * 8
    load = pltpu.make_async_copy(starts_in.at[pl.ds(pl.multiple_of(first_row, 8), 8)], starts, landed)
    load.start()
    fetches = [
        pltpu.make_async_copy(observed_in.at[slot], observed.at[slot], here.at[slot])
        for slot in range(slots)
    ]
    for fetch in fetches:
        fetch.start()
    both = jnp.concatenate([probe_wave[0], probe_wave[0]], 0)
    probe_a[...] = both.T
    both = jnp.concatenate([-probe_wave[1], probe_wave[1]], 0)
    probe_b[...] = both.T
    width = waves.shape[0]
    tile = image.shape[1]
    rows = width // tile * slots
    chunk_count = limit // GROUP

    def used_chunks(slot):
        return jnp.clip(lax.div(counts[first_angle + slot] + (GROUP - 1), GROUP), 0, chunk_count)

    half = size // 2

    staged[...] = image[...].astype(jnp.int32).astype(F32) * (2 * math.pi / 65536)
    load.wait()
    lane = lax.broadcasted_iota(jnp.int32, (size, 2 * size), 1)

    @pl.loop(0, slots)
    def _(slot):
        pltpu.make_async_copy(observed_in.at[slot], observed.at[slot], here.at[slot]).wait()
        for part in range(width // tile):
            sine, cosine = sine_cosine(staged[pl.ds(slot * (width // tile) + part, size, rows), :])
            waves[part * tile : (part + 1) * tile, :] = jnp.concatenate([cosine, sine], 0).T
        total[...] = jnp.zeros_like(total)
        count = counts[first_angle + slot]

        @pl.loop(0, used_chunks(slot))
        def _(chunk):
            begin = chunk * GROUP
            at = [starts[first_angle - first_row + slot, begin + member] for member in range(GROUP)]
            exits = []
            for member in range(GROUP):
                patch = waves[pl.ds(at[member], size), :]
                exits.append(probe_a[...] * patch + probe_b[...] * pltpu.roll(patch, size, 1))
            exit_wave = jnp.concatenate(exits, 0)
            high, low = halves(exit_wave)
            first = dot(jnp.concatenate([high, low], 1), t_first[...])
            first = first[:, : 2 * size] + first[:, 2 * size :]
            turned = jnp.concatenate(
                [first[pair * 2 * size : (pair + 1) * 2 * size].T for pair in range(GROUP // 2)], 0
            )
            high, low = halves(turned)
            second = dot(jnp.concatenate([high, low], 1), t_pair[...])
            second = second + dot(high, t_pair_both[2 * size :, :])
            scaled = []
            for pair in range(GROUP // 2):
                block = second[pair * 2 * size : (pair + 1) * 2 * size]
                real = block[:size, : 2 * size] + block[size:, 2 * size :]
                imag = block[size:, : 2 * size] - block[:size, 2 * size :]
                member = begin + 2 * pair
                seen = [
                    observed[slot, pl.ds(pl.multiple_of((member + m) * half, half), half), :]
                    for m in range(2)
                ]
                seen = jnp.concatenate(
                    [
                        jnp.concatenate([seen[0][:, :size], seen[1][:, :size]], 1),
                        jnp.concatenate([seen[0][:, size:], seen[1][:, size:]], 1),
                    ],
                    0,
                )
                residual = real * real + imag * imag - seen
                live = member + jnp.where(lane >= size, 1, 0) < count
                residual = jnp.where(live, residual, 0.0)
                scaled += [residual * real, residual * imag]
            scaled = jnp.concatenate(scaled, 0).astype(BF16)
            third = dot(jnp.concatenate([scaled, scaled], 1), t_pair_both[...])
            turned = []
            for pair in range(GROUP // 2):
                block = third[pair * 2 * size : (pair + 1) * 2 * size]
                real = block[:size, : 2 * size] - block[size:, 2 * size :]
                imag = block[size:, : 2 * size] + block[:size, 2 * size :]
                turned.append(jnp.concatenate([real, imag], 0).T)
            high, low = halves(jnp.concatenate(turned, 0))
            back = dot(jnp.concatenate([high, low], 1), t_back[...])
            gradient = exit_wave * (back[:, : 2 * size] + back[:, 2 * size :])
            for member in range(GROUP):
                span = pl.ds(at[member], size)
                total[span, :] = total[span, :] + gradient[member * size : (member + 1) * size]

        for part in range(width // tile):
            flat = total[part * tile : (part + 1) * tile, :].T
            staged[pl.ds(slot * (width // tile) + part, size, rows), :] = flat[:size] + flat[size:]

    out[...] = staged[...].astype(BF16)


def ptycho(image, probe_wave, observed, counts, starts):
    slots = observed.shape[0]
    size = probe_wave.shape[1]
    height, tile = image.shape
    width = height // size // slots * tile
    tables = [jnp.asarray(table) for table in transform_tables(size)]
    vector = pl.BlockSpec(memory_space=pltpu.VMEM)
    return pl.pallas_call(
        ptycho_kernel,
        out_shape=jax.ShapeDtypeStruct((height, tile), BF16),
        in_specs=[pl.BlockSpec(memory_space=pltpu.SMEM), pl.BlockSpec(memory_space=pl.ANY)]
        + [vector] * 6
        + [pl.BlockSpec(memory_space=pl.ANY)],
        out_specs=vector,
        scratch_shapes=[
            pltpu.VMEM((width, 2 * size), F32),
            pltpu.VMEM((width, 2 * size), F32),
            pltpu.VMEM((height, tile), F32),
            pltpu.VMEM((size, 2 * size), F32),
            pltpu.VMEM((size, 2 * size), F32),
            pltpu.VMEM(observed.shape, F32),
            pltpu.SMEM((8, starts.shape[1]), jnp.int32),
            pltpu.SemaphoreType.DMA,
            pltpu.SemaphoreType.DMA((slots,)),
        ],
        compiler_params=pltpu.CompilerParams(vmem_limit_bytes=56 * 2**20),
    )(counts, starts, image, probe_wave, *tables, observed)


def collect_kernel(
    grads, pattern, out, mine, held, twin, counts, index, total, flat,
    slab_send, slab_recv, chip_send, chip_recv, pair_send, pair_recv,
    low_send, low_recv, high_send, high_recv,
):
    slab, column = lax.axis_index("slab"), lax.axis_index("col")
    chip, core = lax.div(column, 2), lax.rem(column, 2)
    sibling = (slab, 2 * chip + 1 - core)
    steps = steps_over()
    slabs, slab_rows, share, tile = grads.shape
    tile_rows, spread, angles = pattern.shape
    group, _, _ = out.shape
    tiles = out.shape[1] // slab_rows
    columns = angles * tile_rows // (slabs * share)
    greet_near(slab, chip, core)
    greeted(12)

    order = [1, 3, 4, 2, 5, 7, 6]
    slabs_, chips, pairs = {}, {}, {}
    for d in order:
        other = moved(slab, steps[d])
        slabs_[d] = remote(
            grads.at[other], mine.at[slab], slab_send.at[d], slab_recv.at[d], (other, column)
        )
        slabs_[d].start()
    mine[slab] = grads[slab]

    turned = jnp.concatenate(
        [
            pattern[:, :, base : base + tile].reshape(-1, tile).T
            for base in range(0, angles, tile)
        ],
        0,
    )
    turned = segment_of(turned, group, tiles)
    for d in range(tile_rows):
        index[pl.ds(d, angles, tile_rows), :spread] = turned[:, d * spread : (d + 1) * spread]

    for d in order:
        slabs_[d].wait_recv()
    low, high = slice(0, slab_rows // 2), slice(slab_rows // 2, slab_rows)
    across = (slab, 2 * moved(chip, (1, 0)) + core)
    along = {dy: (slab, 2 * moved(chip, (0, dy)) + core) for dy in range(1, 4)}
    for d in order[:4]:
        chips[d] = remote(
            mine, held.at[d], chip_send.at[d], chip_recv.at[d], across if d == 4 else along[d]
        )
        chips[d].start()
    lows, highs = {}, {}
    for dy in range(1, 4):
        lows[dy] = remote(
            held.at[dy, :, low], held.at[4 + dy, :, low], low_send.at[dy], low_recv.at[dy], across
        )
        highs[dy] = remote(
            held.at[4, :, high], held.at[4 + dy, :, high], high_send.at[dy], high_recv.at[dy],
            along[dy],
        )
    pairs[0] = remote(mine, twin.at[0], pair_send.at[0], pair_recv.at[0], sibling)
    pairs[0].start()

    row = lax.broadcasted_iota(jnp.int32, (tiles, 2 * slabs * share), 0).astype(I16)
    one, zero = jnp.ones(row.shape, BF16), jnp.zeros(row.shape, BF16)

    @pl.loop(0, columns // 2)
    def _(origin):
        wanted = jnp.concatenate(
            [
                index[pl.ds(pl.multiple_of((s * columns + 2 * origin + c) * share, share), share), :]
                for c in range(2)
                for s in range(slabs)
            ],
            0,
        ).T
        wide = [
            jnp.broadcast_to(wanted[member : member + 1, :], row.shape).astype(I16)
            for member in range(spread)
        ]
        for k in range(group):
            held_here = zero
            for member in range(spread):
                held_here = held_here + jnp.where(wide[member] == row + I16(k * tiles), one, zero)
            counts[origin, k * tiles : (k + 1) * tiles, :] = held_here

    def add(d, near, far):
        if d:
            origin = moved(chip, ((2 - steps[d][0]) % 2, (4 - steps[d][1]) % 4))
        else:
            origin = chip
        swapped = core == 1
        for z in range(0, slab_rows, 2):
            parts = []
            for more in range(2):
                a = near[:, z + more].reshape(slabs * share, tile)
                b = far[:, z + more].reshape(slabs * share, tile)
                parts.append(
                    jnp.concatenate([jnp.where(swapped, b, a), jnp.where(swapped, a, b)], 0)
                )
            right = jnp.concatenate(parts, 1)
            for base in range(0, group * tiles, 256):
                result = dot(counts[origin, base : base + 256, :], right)
                span = slice(base, base + 256)
                lanes = slice(z * tile, (z + 2) * tile)
                if d:
                    result = result + total[span, lanes]
                total[span, lanes] = result

    pending = 0
    for d in order + [None]:
        if d is not None:
            if d < 5:
                chips[d].wait_recv()
            else:
                lows[d - 4].wait_recv()
                highs[d - 4].wait_recv()
            if d < 4:
                lows[d].start()
            elif d == 4:
                for dy in range(1, 4):
                    highs[dy].start()
            pairs[d] = remote(held.at[d], twin.at[d], pair_send.at[d], pair_recv.at[d], sibling)
            pairs[d].start()
        pairs[pending].wait_recv()
        add(pending, held.at[pending] if pending else mine, twin.at[pending])
        pending = d

    for k in range(group):
        for z in range(slab_rows):
            block = total[k * tiles : (k + 1) * tiles, z * tile : (z + 1) * tile]
            flat[pl.ds(z, tiles, slab_rows), :] = block
        out[k] = flat[...].astype(BF16)

    for d in order:
        slabs_[d].wait_send()
    for d in order[:4]:
        chips[d].wait_send()
    for dy in range(1, 4):
        lows[dy].wait_send()
        highs[dy].wait_send()
    for d in [0] + order:
        pairs[d].wait_send()


def collect(grads, pattern, templates, tiles):
    slabs, slab_rows, share, tile = grads.shape
    group, tile_cells, _ = templates.shape
    tile_rows, spread, angles = pattern.shape
    columns = angles * tile_rows // (slabs * share)
    vector = pl.BlockSpec(memory_space=pltpu.VMEM)
    sem = pltpu.SemaphoreType.DMA((8,))
    return pl.pallas_call(
        collect_kernel,
        out_shape=jax.ShapeDtypeStruct((group, tiles * slab_rows, tile), BF16),
        in_specs=[vector, vector],
        out_specs=vector,
        scratch_shapes=[
            pltpu.VMEM(grads.shape, BF16),
            pltpu.VMEM((8,) + grads.shape, BF16),
            pltpu.VMEM((8,) + grads.shape, BF16),
            pltpu.VMEM((columns // 2, group * tiles, 2 * slabs * share), BF16),
            pltpu.VMEM((angles * tile_rows, tile), jnp.int32),
            pltpu.VMEM((group * tiles, slab_rows * tile), F32),
            pltpu.VMEM((tiles * slab_rows, tile), F32),
        ]
        + [sem] * 10,
        compiler_params=pltpu.CompilerParams(
            collective_id=2, has_side_effects=True, vmem_limit_bytes=56 * 2**20
        ),
    )(grads, pattern)


def update_kernel(sums, templates, volume, consensus, out):
    group, size, tile = sums.shape
    tile_cells = templates.shape[1]
    slab_rows = volume.shape[0]
    left = jnp.concatenate([sums[k] for k in range(group)], 1)
    for part in range(0, tile_cells, 256):
        total = jnp.zeros((size, 256), F32)
        for k in range(0, group, 2):
            right = jnp.concatenate(
                [templates[k, part : part + 256, :], templates[k + 1, part : part + 256, :]], 1
            )
            total = total + lax.dot_general(
                left[:, k * tile : (k + 2) * tile],
                right,
                (((1,), (1,)), ((), ())),
                preferred_element_type=F32,
            )
        for t in range(size // slab_rows):
            span = slice(t * tile_cells + part, t * tile_cells + part + 256)
            own_volume = volume[:, span].astype(F32)
            wanted = consensus[:, span].astype(F32)
            moved_by = total[t * slab_rows : (t + 1) * slab_rows]
            out[:, span] = own_volume - step_size * (moved_by + penalty * (own_volume - wanted))


def update(sums, templates, volume, consensus):
    slab_rows, cells = volume.shape
    group, height, tile = sums.shape
    steps = 4
    block = pl.BlockSpec((slab_rows, cells // steps), lambda i: (0, i))
    return pl.pallas_call(
        update_kernel,
        grid=(steps,),
        out_shape=jax.ShapeDtypeStruct((slab_rows, cells), F32),
        in_specs=[
            pl.BlockSpec((group, height // steps, tile), lambda i: (0, i, 0)),
            pl.BlockSpec(templates.shape, lambda i: (0, 0, 0)),
            block,
            block,
        ],
        out_specs=block,
        compiler_params=pltpu.CompilerParams(vmem_limit_bytes=56 * 2**20),
    )(sums, templates, volume, consensus)


def on_device(
    volume, consensus, templates, pattern, probe_wave, measured, scan_counts, scan_positions
):
    slab_rows = volume.shape[0]
    tile = templates.shape[2]
    slab_count = lax.axis_size("slab")
    column_count = lax.axis_size("col")
    angle_count, tile_rows, spread = pattern.shape[1:]
    per_owner = angle_count // (slab_count * column_count)
    own = per_owner * tile_rows
    rows = angle_count * tile_rows

    image, observed = forward(
        volume,
        templates,
        pattern[0].transpose(1, 2, 0),
        measured.transpose(0, 2, 3, 1),
        column_count,
        slab_count,
    )
    image = image.reshape(slab_count * slab_rows * own, tile)
    gradients = ptycho(image, probe_wave, observed, scan_counts, scan_positions)
    sums = collect(
        gradients.reshape(slab_count, slab_rows, own, tile),
        pattern[0].transpose(1, 2, 0),
        templates,
        volume.shape[1] // templates.shape[1],
    )
    return update(sums, templates, volume, consensus)


def solution(mesh):
    return jax.shard_map(
        on_device,
        mesh=mesh,
        in_specs=(
            P("slab", "col"),
            P("slab", "col"),
            P("col", None, None),
            P("col", None, None, None),
            P(),
            P(("slab", "col"), None, None, None),
            P(),
            P(),
        ),
        out_specs=P("slab", "col"),
        check_vma=False,
    )
```

```python
import functools
import math

import jax
import jax.numpy as jnp
import numpy as np
from jax import lax
from jax.experimental import pallas as pl
from jax.experimental.pallas import tpu as pltpu
from jax.sharding import PartitionSpec as P

BF16 = jnp.bfloat16
F32 = jnp.float32
GROUP = 64
step_size = 0.1
penalty = 1.0
I16 = jnp.int16
TURN = 65536 / (2 * math.pi)

def dot(left, right):
    return jnp.dot(left, right, preferred_element_type=F32)


def steps_over():
    return [(dx, dy) for dx in range(2) for dy in range(4)]


def moved(index, step):
    high, low = lax.div(index, 4), lax.rem(index, 4)
    return lax.rem(high + step[0], 2) * 4 + lax.rem(low + step[1], 4)


def greet_near(slab, chip, core):
    barrier = pltpu.get_barrier_semaphore()
    column = 2 * chip + core
    others = [(slab, 2 * chip + 1 - core)]
    others += [(slab, 2 * moved(chip, step) + core) for step in ((0, 1), (0, 3), (1, 0))]
    others += [(moved(slab, step), column) for step in steps_over()[1:]]
    for other in others:
        pl.semaphore_signal(barrier, inc=1, device_id=other, device_id_type=pl.DeviceIdType.MESH)


def greeted(number):
    pl.semaphore_wait(pltpu.get_barrier_semaphore(), number)


def remote(source, target, send, receive, device):
    return pltpu.make_async_remote_copy(
        src_ref=source,
        dst_ref=target,
        send_sem=send,
        recv_sem=receive,
        device_id=device,
        device_id_type=pl.DeviceIdType.MESH,
    )


def segment_of(entry, group, tiles):
    return (entry & (group - 1)) * tiles + lax.div(entry, group)


def forward_kernel(
    volume_in, templates_in, pattern, measured_in, image, observed,
    volume, templates, measured, turned_over, flat, table, counts, index, own, outgoing, pair, from_y, from_x, total,
    load_sem, pair_send, pair_recv, x_send, x_recv, y_send, y_recv, slab_send, slab_recv,
):
    slab, column = lax.axis_index("slab"), lax.axis_index("col")
    chip, core = lax.div(column, 2), lax.rem(column, 2)
    slabs, slab_rows, share, tile = image.shape
    columns = 2 * own.shape[0]
    group, tile_cells, _ = templates.shape
    tiles = table.shape[0] // group
    tile_rows, spread, angles = pattern.shape
    half = measured.shape[1] // 2
    limit = measured.shape[3]
    quarter = volume.shape[1] // 4
    greet_near(slab, chip, core)

    loads = [pltpu.make_async_copy(templates_in, templates, load_sem.at[0])]
    for part in range(4):
        span = pl.ds(part * quarter, quarter)
        loads.append(
            pltpu.make_async_copy(volume_in.at[:, span], volume.at[:, span], load_sem.at[1 + part])
        )
    loads.append(pltpu.make_async_copy(measured_in, measured, load_sem.at[5]))
    for load in loads:
        load.start()

    turned = jnp.concatenate(
        [
            pattern[:, :, base : base + tile].reshape(-1, tile).T
            for base in range(0, angles, tile)
        ],
        0,
    )
    turned = segment_of(turned, group, tiles)
    for d in range(tile_rows):
        index[pl.ds(d, angles, tile_rows), :spread] = turned[:, d * spread : (d + 1) * spread]

    loads[0].wait()
    step = tiles // 4
    for part in range(4):
        loads[1 + part].wait()
        left = jnp.concatenate(
            [
                volume[:, t * tile_cells : (t + 1) * tile_cells].astype(F32)
                for t in range(part * step, (part + 1) * step)
            ],
            0,
        ).astype(BF16)
        span = slice(part * step * slab_rows, (part + 1) * step * slab_rows)
        for k in range(0, group, 2):
            result = dot(left, jnp.concatenate([templates[k], templates[k + 1]], 1))
            flat[k, span, :] = result[:, :tile]
            flat[k + 1, span, :] = result[:, tile:]
    for k in range(group):
        for z in range(slab_rows):
            block = flat[k, pl.ds(z, tiles, slab_rows), :]
            table[k * tiles : (k + 1) * tiles, z * tile : (z + 1) * tile] = block.astype(BF16)

    greeted(11)
    lane = lax.broadcasted_iota(jnp.int32, (2 * slabs * share, tiles), 1).astype(I16)
    one, zero = jnp.ones(lane.shape, BF16), jnp.zeros(lane.shape, BF16)

    quarter_rows = slab_rows // 4
    low, high = slice(0, slab_rows // 2), slice(slab_rows // 2, slab_rows)
    across = (slab, 2 * moved(chip, (1, 0)) + core)

    def along(dy):
        return (slab, 2 * (4 * lax.div(chip, 4) + lax.rem(chip + dy, 4)) + core)

    def to_pair(d):
        return remote(
            outgoing.at[d], pair.at[d], pair_send.at[d], pair_recv.at[d],
            (slab, 2 * chip + 1 - core),
        )

    def low_across(dy):
        return remote(
            own.at[4 + dy, low], from_x.at[dy, low], x_send.at[dy], x_recv.at[dy], across
        )

    def low_along(dy):
        return remote(own.at[dy, low], from_y.at[dy, low], y_send.at[dy], y_recv.at[dy], along(dy))

    def high_along(d, dy):
        return remote(
            own.at[d, high], from_y.at[d, high], y_send.at[8 + d], y_recv.at[8 + d], along(dy)
        )

    def relay(d, side, dy):
        begin = side * (slab_rows // 2) + (dy // 2) * quarter_rows
        rows = slice(begin, begin + quarter_rows)
        number = 16 + 4 * lax.div(d, 4) + 2 * side + dy // 2
        return remote(
            own.at[d, rows], from_y.at[d, rows], y_send.at[number], y_recv.at[number], along(dy)
        )

    def take(d, side, dy):
        middle = d - dy + 2
        relay(middle, side, dy).wait_recv()
        begin = side * (slab_rows // 2) + (dy // 2) * quarter_rows

        @pl.loop(begin, begin + quarter_rows)
        def _(z):
            own[d, z] = own[d, z] + from_y[middle, z]

    def high_across():
        return remote(own.at[4, high], from_x.at[0, high], x_send.at[4], x_recv.at[4], across)

    def compute(d):
        ahead = lax.rem(lax.div(chip, 4) + lax.div(d, 4), 2)
        target = 4 * ahead + lax.rem(chip + d, 4)
        wanted = jnp.concatenate(
            [
                index[pl.ds(pl.multiple_of((s * columns + 2 * target + c) * share, share), share), :]
                for c in (core, 1 - core)
                for s in range(slabs)
            ],
            0,
        )
        wide = [
            jnp.broadcast_to(wanted[:, member : member + 1], lane.shape).astype(I16)
            for member in range(spread)
        ]
        for k in range(group):
            held = zero
            for member in range(spread):
                held = held + jnp.where(wide[member] == lane + I16(k * tiles), one, zero)
            counts[:, k * tiles : (k + 1) * tiles] = held
        for z in range(0, slab_rows, 2):
            result = dot(counts[...], table[:, z * tile : (z + 2) * tile])
            result = jnp.floor(result * TURN + 0.5).astype(jnp.int32).astype(I16)
            for more in range(2):
                part = result[:, more * tile : (more + 1) * tile]
                own[d, z + more] = part[: slabs * share].reshape(slabs, share, tile)
                outgoing[d, z + more] = part[slabs * share :].reshape(slabs, share, tile)
        to_pair(d).start()

    def add_pair(d):
        to_pair(d).wait_recv()

        @pl.loop(0, slab_rows)
        def _(z):
            own[d, z] = own[d, z] + pair[d, z]

    def add_low(dy):
        low_across(dy).wait_recv()

        @pl.loop(0, slab_rows // 2)
        def _(z):
            own[dy, z] = own[dy, z] + from_x[dy, z]

    def send_relays(d, side):
        for way in (1, 3):
            relay(d, side, way).start()

    def finish_high(d, way):
        take(d, 1, way)
        high_along(d, way).start()

    def finish_low(way):
        add_low(way)
        take(way, 0, way)
        low_along(way).start()

    def turn_corner():
        for dy in (1, 3):
            high_along(4 + dy, dy).wait_recv()

        @pl.loop(slab_rows // 2, slab_rows)
        def _(z):
            own[4, z] = own[4, z] + from_y[5, z] + from_y[7, z]

        high_across().start()

    plan = {
        1: [lambda: low_across(2).start(), lambda: send_relays(6, 1)],
        2: [lambda: send_relays(2, 1)],
        3: [lambda: low_across(1).start(), lambda: finish_high(5, 1)],
        4: [
            lambda: low_across(3).start(),
            lambda: finish_high(7, 3),
            lambda: add_low(2),
            lambda: send_relays(2, 0),
        ],
        5: [lambda: low_across(0).start()],
        6: [lambda: finish_high(1, 1), lambda: finish_low(1)],
        7: [lambda: finish_high(3, 3), lambda: finish_low(3), turn_corner],
        8: [lambda: add_low(0)],
    }
    sequence = (6, 2, 5, 7, 4, 1, 3, 0)

    def work(i, carry):
        rest, previous = carry
        d = lax.rem(rest, 8)

        @pl.when(i < 8)
        def _():
            compute(d)

        @pl.when(i > 0)
        def _():
            add_pair(previous)

        for number, actions in plan.items():

            @pl.when(i == number)
            def _():
                for action in actions:
                    action()

        return lax.div(rest, 8), d

    lax.fori_loop(0, 9, work, (sum(d * 8**n for n, d in enumerate(sequence)), 0))

    loads[5].wait()
    stores = []
    for slot in range(measured.shape[0]):

        @pl.loop(0, half, unroll=4)
        def _(row):
            both = jnp.concatenate([measured[slot, row], measured[slot, row + half]], 0)
            turned_over[slot, pl.ds(row, limit, half), :] = both.T

        stores.append(
            pltpu.make_async_copy(turned_over.at[slot], observed.at[slot], load_sem.at[6 + slot])
        )
        stores[-1].start()

    def to_slab(d, part):
        other = moved(slab, steps_over()[d])
        side = (low, high)[part]
        number = 8 * part + d
        return remote(
            total.at[other, side], image.at[slab, side], slab_send.at[number], slab_recv.at[number],
            (other, column),
        )

    for part in range(2):
        for dy in (1, 3):
            if part:
                high_along(dy, dy).wait_recv()
            else:
                low_along(dy).wait_recv()
        if part:
            high_across().wait_recv()

        @pl.loop(part * slab_rows // 2, (part + 1) * slab_rows // 2)
        def _(z):
            value = own[0, z] + from_y[1, z] + from_y[3, z]
            if part:
                value = value + from_x[0, z]
            total[:, z] = value

        for d in range(1, 8):
            to_slab(d, part).start()

    image[slab] = total[slab]
    for d in range(8):
        to_pair(d).wait_send()
    for dy in range(4):
        low_across(dy).wait_send()
    for dy in (1, 3):
        low_along(dy).wait_send()
        high_along(dy, dy).wait_send()
        high_along(4 + dy, dy).wait_send()
        relay(2, 0, dy).wait_send()
        relay(2, 1, dy).wait_send()
        relay(6, 1, dy).wait_send()
    high_across().wait_send()
    for part in range(2):
        for d in range(1, 8):
            to_slab(d, part).wait()
    for copy in stores:
        copy.wait()


def forward(volume, templates, pattern, measured, columns, slabs):
    slab_rows, cells = volume.shape
    group, tile_cells, tile = templates.shape
    tiles = cells // tile_cells
    tile_rows, spread, angles = pattern.shape
    slots, size, _, limit = measured.shape
    rows = angles * tile_rows
    share = rows // (columns * slabs)
    block = (columns // 2, slab_rows, slabs, share, tile)
    vector = pl.BlockSpec(memory_space=pltpu.VMEM)
    anywhere = pl.BlockSpec(memory_space=pl.ANY)
    sem = pltpu.SemaphoreType.DMA((8,))
    return pl.pallas_call(
        forward_kernel,
        out_shape=(
            jax.ShapeDtypeStruct((slabs, slab_rows, share, tile), I16),
            jax.ShapeDtypeStruct((slots, limit * size // 2, 2 * size), F32),
        ),
        in_specs=[anywhere, anywhere, vector, anywhere],
        out_specs=(vector, anywhere),
        scratch_shapes=[
            pltpu.VMEM(volume.shape, BF16),
            pltpu.VMEM(templates.shape, BF16),
            pltpu.VMEM(measured.shape, F32),
            pltpu.VMEM((slots, limit * size // 2, 2 * size), F32),
            pltpu.VMEM((group, tiles * slab_rows, tile), F32),
            pltpu.VMEM((group * tiles, slab_rows * tile), BF16),
            pltpu.VMEM((2 * slabs * share, group * tiles), BF16),
            pltpu.VMEM((rows, tile), jnp.int32),
        ]
        + [pltpu.VMEM(block, I16)] * 4
        + [pltpu.VMEM((4,) + block[1:], I16)]
        + [pltpu.VMEM((slabs, slab_rows, share, tile), I16)]
        + [sem] * 5
        + [pltpu.SemaphoreType.DMA((24,))] * 4,
        compiler_params=pltpu.CompilerParams(
            collective_id=1, has_side_effects=True, vmem_limit_bytes=56 * 2**20
        ),
    )(volume, templates, pattern, measured)


def trig_coefficients():
    grid = (np.cos(np.pi * (np.arange(400) + 0.5) / 400) + 1.0) * (np.pi * np.pi * 0.5005)
    root = np.sqrt(grid)
    sine = np.polynomial.Polynomial.fit(grid, np.sin(root) / root, 6).convert().coef
    cosine = np.polynomial.Polynomial.fit(grid, np.cos(root), 7).convert().coef
    return [float(v) for v in sine], [float(v) for v in cosine]


def sine_cosine(angle):
    sine, cosine = trig_coefficients()
    square = angle * angle
    sine_value = jnp.full_like(square, sine[-1])
    for value in sine[-2::-1]:
        sine_value = sine_value * square + value
    cosine_value = jnp.full_like(square, cosine[-1])
    for value in cosine[-2::-1]:
        cosine_value = cosine_value * square + value
    return sine_value * angle, cosine_value


def split_bf16(table):
    high = table.astype(np.float32).astype(BF16)
    low = (table - high.astype(np.float64)).astype(np.float32).astype(BF16)
    return high, low


def transform_tables(size):
    index = np.arange(size)
    radians = 2.0 * np.pi / size * (index[:, None] * index[None, :] % size)
    cosine = np.cos(radians) / math.sqrt(size)
    sine = np.sin(radians) / math.sqrt(size)
    zero = np.zeros_like(cosine)
    forward = np.block([[cosine, -sine], [sine, cosine]])
    pair = np.block([[cosine, zero, sine, zero], [zero, cosine, zero, sine]])
    back = np.block([[2 * sine, -2 * cosine], [2 * cosine, 2 * sine]])
    f_high, f_low = split_bf16(forward)
    p_high, p_low = split_bf16(pair)
    b_high, b_low = split_bf16(back)
    lanes = np.concatenate([f_high, f_low], 1)
    back = np.concatenate([b_high, b_low], 1)
    return (
        np.concatenate([lanes, lanes], 0),
        np.concatenate([p_high, p_high], 0),
        np.concatenate([p_high, p_low], 0),
        np.concatenate([back, back], 0),
    )


def halves(value):
    high = value.astype(BF16)
    low = (value - high.astype(F32)).astype(BF16)
    return high, low


def ptycho_kernel(
    counts, starts_in, image, probe_wave, t_first, t_pair, t_pair_both, t_back, observed_in,
    out, waves, total, staged, probe_a, probe_b, observed, starts, landed, here,
):
    slots = observed.shape[0]
    size = probe_wave.shape[1]
    limit = starts.shape[1]
    owner = lax.axis_index("slab") * lax.axis_size("col") + lax.axis_index("col")
    first_angle = owner * slots
    first_row = lax.div(first_angle, 8) * 8
    load = pltpu.make_async_copy(starts_in.at[pl.ds(pl.multiple_of(first_row, 8), 8)], starts, landed)
    load.start()
    fetches = [
        pltpu.make_async_copy(observed_in.at[slot], observed.at[slot], here.at[slot])
        for slot in range(slots)
    ]
    for fetch in fetches:
        fetch.start()
    both = jnp.concatenate([probe_wave[0], probe_wave[0]], 0)
    probe_a[...] = both.T
    both = jnp.concatenate([-probe_wave[1], probe_wave[1]], 0)
    probe_b[...] = both.T
    width = waves.shape[0]
    tile = image.shape[1]
    rows = width // tile * slots
    chunk_count = limit // GROUP

    def used_chunks(slot):
        return jnp.clip(lax.div(counts[first_angle + slot] + (GROUP - 1), GROUP), 0, chunk_count)

    half = size // 2

    staged[...] = image[...].astype(jnp.int32).astype(F32) * (2 * math.pi / 65536)
    load.wait()
    lane = lax.broadcasted_iota(jnp.int32, (size, 2 * size), 1)

    @pl.loop(0, slots)
    def _(slot):
        pltpu.make_async_copy(observed_in.at[slot], observed.at[slot], here.at[slot]).wait()
        for part in range(width // tile):
            sine, cosine = sine_cosine(staged[pl.ds(slot * (width // tile) + part, size, rows), :])
            waves[part * tile : (part + 1) * tile, :] = jnp.concatenate([cosine, sine], 0).T
        total[...] = jnp.zeros_like(total)
        count = counts[first_angle + slot]

        @pl.loop(0, used_chunks(slot))
        def _(chunk):
            begin = chunk * GROUP
            at = [starts[first_angle - first_row + slot, begin + member] for member in range(GROUP)]
            exits = []
            for member in range(GROUP):
                patch = waves[pl.ds(at[member], size), :]
                exits.append(probe_a[...] * patch + probe_b[...] * pltpu.roll(patch, size, 1))
            exit_wave = jnp.concatenate(exits, 0)
            high, low = halves(exit_wave)
            first = dot(jnp.concatenate([high, low], 1), t_first[...])
            first = first[:, : 2 * size] + first[:, 2 * size :]
            turned = jnp.concatenate(
                [first[pair * 2 * size : (pair + 1) * 2 * size].T for pair in range(GROUP // 2)], 0
            )
            high, low = halves(turned)
            second = dot(jnp.concatenate([high, low], 1), t_pair[...])
            second = second + dot(high, t_pair_both[2 * size :, :])
            scaled = []
            for pair in range(GROUP // 2):
                block = second[pair * 2 * size : (pair + 1) * 2 * size]
                real = block[:size, : 2 * size] + block[size:, 2 * size :]
                imag = block[size:, : 2 * size] - block[:size, 2 * size :]
                member = begin + 2 * pair
                seen = [
                    observed[slot, pl.ds(pl.multiple_of((member + m) * half, half), half), :]
                    for m in range(2)
                ]
                seen = jnp.concatenate(
                    [
                        jnp.concatenate([seen[0][:, :size], seen[1][:, :size]], 1),
                        jnp.concatenate([seen[0][:, size:], seen[1][:, size:]], 1),
                    ],
                    0,
                )
                residual = real * real + imag * imag - seen
                live = member + jnp.where(lane >= size, 1, 0) < count
                residual = jnp.where(live, residual, 0.0)
                scaled += [residual * real, residual * imag]
            scaled = jnp.concatenate(scaled, 0).astype(BF16)
            third = dot(jnp.concatenate([scaled, scaled], 1), t_pair_both[...])
            turned = []
            for pair in range(GROUP // 2):
                block = third[pair * 2 * size : (pair + 1) * 2 * size]
                real = block[:size, : 2 * size] - block[size:, 2 * size :]
                imag = block[size:, : 2 * size] + block[:size, 2 * size :]
                turned.append(jnp.concatenate([real, imag], 0).T)
            high, low = halves(jnp.concatenate(turned, 0))
            back = dot(jnp.concatenate([high, low], 1), t_back[...])
            gradient = exit_wave * (back[:, : 2 * size] + back[:, 2 * size :])
            for member in range(GROUP):
                span = pl.ds(at[member], size)
                total[span, :] = total[span, :] + gradient[member * size : (member + 1) * size]

        for part in range(width // tile):
            flat = total[part * tile : (part + 1) * tile, :].T
            staged[pl.ds(slot * (width // tile) + part, size, rows), :] = flat[:size] + flat[size:]

    out[...] = staged[...].astype(BF16)


def ptycho(image, probe_wave, observed, counts, starts):
    slots = observed.shape[0]
    size = probe_wave.shape[1]
    height, tile = image.shape
    width = height // size // slots * tile
    tables = [jnp.asarray(table) for table in transform_tables(size)]
    vector = pl.BlockSpec(memory_space=pltpu.VMEM)
    return pl.pallas_call(
        ptycho_kernel,
        out_shape=jax.ShapeDtypeStruct((height, tile), BF16),
        in_specs=[pl.BlockSpec(memory_space=pltpu.SMEM), pl.BlockSpec(memory_space=pl.ANY)]
        + [vector] * 6
        + [pl.BlockSpec(memory_space=pl.ANY)],
        out_specs=vector,
        scratch_shapes=[
            pltpu.VMEM((width, 2 * size), F32),
            pltpu.VMEM((width, 2 * size), F32),
            pltpu.VMEM((height, tile), F32),
            pltpu.VMEM((size, 2 * size), F32),
            pltpu.VMEM((size, 2 * size), F32),
            pltpu.VMEM(observed.shape, F32),
            pltpu.SMEM((8, starts.shape[1]), jnp.int32),
            pltpu.SemaphoreType.DMA,
            pltpu.SemaphoreType.DMA((slots,)),
        ],
        compiler_params=pltpu.CompilerParams(vmem_limit_bytes=56 * 2**20),
    )(counts, starts, image, probe_wave, *tables, observed)


def collect_kernel(
    grads, pattern, out, mine, held, twin, counts, index, total, flat,
    slab_send, slab_recv, chip_send, chip_recv, pair_send, pair_recv,
):
    slab, column = lax.axis_index("slab"), lax.axis_index("col")
    chip, core = lax.div(column, 2), lax.rem(column, 2)
    sibling = (slab, 2 * chip + 1 - core)
    steps = steps_over()
    slabs, slab_rows, share, tile = grads.shape
    tile_rows, spread, angles = pattern.shape
    group, _, _ = out.shape
    tiles = out.shape[1] // slab_rows
    columns = angles * tile_rows // (slabs * share)
    greet_near(slab, chip, core)
    greeted(11)

    order = [1, 3, 4, 2, 5, 7, 6]
    slabs_, chips, pairs = {}, {}, {}
    for d in order:
        other = moved(slab, steps[d])
        slabs_[d] = remote(
            grads.at[other], mine.at[slab], slab_send.at[d], slab_recv.at[d], (other, column)
        )
        slabs_[d].start()
    mine[slab] = grads[slab]

    turned = jnp.concatenate(
        [
            pattern[:, :, base : base + tile].reshape(-1, tile).T
            for base in range(0, angles, tile)
        ],
        0,
    )
    turned = segment_of(turned, group, tiles)
    for d in range(tile_rows):
        index[pl.ds(d, angles, tile_rows), :spread] = turned[:, d * spread : (d + 1) * spread]

    for d in order:
        slabs_[d].wait_recv()
    half, quarter = slab_rows // 2, slab_rows // 4
    low, high = slice(0, half), slice(half, slab_rows)
    upper, lower = slice(half, half + quarter), slice(half + quarter, slab_rows)
    across = (slab, 2 * moved(chip, (1, 0)) + core)
    up = (slab, 2 * moved(chip, (0, 1)) + core)
    down = (slab, 2 * moved(chip, (0, 3)) + core)

    def pass_on(number, source, target, rows, device):
        chips[number] = remote(
            (mine if source == 0 else held.at[source]).at[:, rows], held.at[target, :, rows],
            chip_send.at[number], chip_recv.at[number], device,
        )
        chips[number].start()

    whole = slice(0, slab_rows)
    pass_on(0, 0, 1, whole, up)
    pass_on(1, 0, 3, whole, down)
    pass_on(2, 0, 4, whole, across)
    pairs[0] = remote(mine, twin.at[0], pair_send.at[0], pair_recv.at[0], sibling)
    pairs[0].start()

    row = lax.broadcasted_iota(jnp.int32, (tiles, 2 * slabs * share), 0).astype(I16)
    one, zero = jnp.ones(row.shape, BF16), jnp.zeros(row.shape, BF16)

    @pl.loop(0, columns // 2)
    def _(origin):
        wanted = jnp.concatenate(
            [
                index[pl.ds(pl.multiple_of((s * columns + 2 * origin + c) * share, share), share), :]
                for c in range(2)
                for s in range(slabs)
            ],
            0,
        ).T
        wide = [
            jnp.broadcast_to(wanted[member : member + 1, :], row.shape).astype(I16)
            for member in range(spread)
        ]
        for k in range(group):
            held_here = zero
            for member in range(spread):
                held_here = held_here + jnp.where(wide[member] == row + I16(k * tiles), one, zero)
            counts[origin, k * tiles : (k + 1) * tiles, :] = held_here

    def add(d, near, far):
        if d:
            origin = moved(chip, ((2 - steps[d][0]) % 2, (4 - steps[d][1]) % 4))
        else:
            origin = chip
        swapped = core == 1
        for z in range(0, slab_rows, 2):
            parts = []
            for more in range(2):
                a = near[:, z + more].reshape(slabs * share, tile)
                b = far[:, z + more].reshape(slabs * share, tile)
                parts.append(
                    jnp.concatenate([jnp.where(swapped, b, a), jnp.where(swapped, a, b)], 0)
                )
            right = jnp.concatenate(parts, 1)
            for base in range(0, group * tiles, 256):
                result = dot(counts[origin, base : base + 256, :], right)
                span = slice(base, base + 256)
                lanes = slice(z * tile, (z + 2) * tile)
                if d:
                    result = result + total[span, lanes]
                total[span, lanes] = result

    def arrived(*numbers):
        for number in numbers:
            chips[number].wait_recv()

    def to_sibling(d):
        pairs[d] = remote(held.at[d], twin.at[d], pair_send.at[d], pair_recv.at[d], sibling)
        pairs[d].start()

    def use(d):
        pairs[d].wait_recv()
        add(d, held.at[d] if d else mine, twin.at[d])

    arrived(0)
    pass_on(3, 1, 2, low, up)
    pass_on(4, 1, 5, low, across)
    to_sibling(1)
    arrived(1)
    pass_on(5, 3, 2, high, down)
    pass_on(6, 3, 7, low, across)
    to_sibling(3)
    arrived(2)
    pass_on(7, 4, 5, high, up)
    pass_on(8, 4, 7, high, down)
    to_sibling(4)
    use(0)
    arrived(3)
    pass_on(9, 2, 6, low, across)
    use(1)
    arrived(7)
    pass_on(10, 5, 6, upper, up)
    arrived(8)
    pass_on(11, 7, 6, lower, down)
    use(3)
    arrived(5)
    to_sibling(2)
    use(4)
    arrived(4)
    to_sibling(5)
    use(2)
    arrived(6)
    to_sibling(7)
    use(5)
    arrived(9, 10, 11)
    to_sibling(6)
    use(7)
    use(6)

    for k in range(group):
        for z in range(slab_rows):
            block = total[k * tiles : (k + 1) * tiles, z * tile : (z + 1) * tile]
            flat[pl.ds(z, tiles, slab_rows), :] = block
        out[k] = flat[...].astype(BF16)

    for d in order:
        slabs_[d].wait_send()
    for number in range(12):
        chips[number].wait_send()
    for d in [0] + order:
        pairs[d].wait_send()


def collect(grads, pattern, templates, tiles):
    slabs, slab_rows, share, tile = grads.shape
    group, tile_cells, _ = templates.shape
    tile_rows, spread, angles = pattern.shape
    columns = angles * tile_rows // (slabs * share)
    vector = pl.BlockSpec(memory_space=pltpu.VMEM)
    sem = pltpu.SemaphoreType.DMA((8,))
    return pl.pallas_call(
        collect_kernel,
        out_shape=jax.ShapeDtypeStruct((group, tiles * slab_rows, tile), BF16),
        in_specs=[vector, vector],
        out_specs=vector,
        scratch_shapes=[
            pltpu.VMEM(grads.shape, BF16),
            pltpu.VMEM((8,) + grads.shape, BF16),
            pltpu.VMEM((8,) + grads.shape, BF16),
            pltpu.VMEM((columns // 2, group * tiles, 2 * slabs * share), BF16),
            pltpu.VMEM((angles * tile_rows, tile), jnp.int32),
            pltpu.VMEM((group * tiles, slab_rows * tile), F32),
            pltpu.VMEM((tiles * slab_rows, tile), F32),
        ]
        + [sem, sem, pltpu.SemaphoreType.DMA((12,)), pltpu.SemaphoreType.DMA((12,)), sem, sem],
        compiler_params=pltpu.CompilerParams(
            collective_id=2, has_side_effects=True, vmem_limit_bytes=32 * 2**20
        ),
    )(grads, pattern)


def update_kernel(sums, templates, volume, consensus, out):
    group, size, tile = sums.shape
    tile_cells = templates.shape[1]
    slab_rows = volume.shape[0]
    left = jnp.concatenate([sums[k] for k in range(group)], 1)
    for part in range(0, tile_cells, 256):
        total = jnp.zeros((size, 256), F32)
        for k in range(0, group, 2):
            right = jnp.concatenate(
                [templates[k, part : part + 256, :], templates[k + 1, part : part + 256, :]], 1
            )
            total = total + lax.dot_general(
                left[:, k * tile : (k + 2) * tile],
                right,
                (((1,), (1,)), ((), ())),
                preferred_element_type=F32,
            )
        for t in range(size // slab_rows):
            span = slice(t * tile_cells + part, t * tile_cells + part + 256)
            own_volume = volume[:, span].astype(F32)
            wanted = consensus[:, span].astype(F32)
            moved_by = total[t * slab_rows : (t + 1) * slab_rows]
            out[:, span] = own_volume - step_size * (moved_by + penalty * (own_volume - wanted))


def update(sums, templates, volume, consensus):
    slab_rows, cells = volume.shape
    group, height, tile = sums.shape
    steps = 4
    block = pl.BlockSpec((slab_rows, cells // steps), lambda i: (0, i))
    return pl.pallas_call(
        update_kernel,
        grid=(steps,),
        out_shape=jax.ShapeDtypeStruct((slab_rows, cells), F32),
        in_specs=[
            pl.BlockSpec((group, height // steps, tile), lambda i: (0, i, 0)),
            pl.BlockSpec(templates.shape, lambda i: (0, 0, 0)),
            block,
            block,
        ],
        out_specs=block,
        compiler_params=pltpu.CompilerParams(vmem_limit_bytes=20 * 2**20),
    )(sums, templates, volume, consensus)


def on_device(
    volume, consensus, templates, pattern, probe_wave, measured, scan_counts, scan_positions
):
    slab_rows = volume.shape[0]
    tile = templates.shape[2]
    slab_count = lax.axis_size("slab")
    column_count = lax.axis_size("col")
    angle_count, tile_rows, spread = pattern.shape[1:]
    per_owner = angle_count // (slab_count * column_count)
    own = per_owner * tile_rows
    rows = angle_count * tile_rows

    image, observed = forward(
        volume,
        templates,
        pattern[0].transpose(1, 2, 0),
        measured.transpose(0, 2, 3, 1),
        column_count,
        slab_count,
    )
    image = image.reshape(slab_count * slab_rows * own, tile)
    gradients = ptycho(image, probe_wave, observed, scan_counts, scan_positions)
    sums = collect(
        gradients.reshape(slab_count, slab_rows, own, tile),
        pattern[0].transpose(1, 2, 0),
        templates,
        volume.shape[1] // templates.shape[1],
    )
    return update(sums, templates, volume, consensus)


def solution(mesh):
    return jax.shard_map(
        on_device,
        mesh=mesh,
        in_specs=(
            P("slab", "col"),
            P("slab", "col"),
            P("col", None, None),
            P("col", None, None, None),
            P(),
            P(("slab", "col"), None, None, None),
            P(),
            P(),
        ),
        out_specs=P("slab", "col"),
        check_vma=False,
    )
```

```python
import functools
import math

import jax
import jax.numpy as jnp
import numpy as np
from jax import lax
from jax.experimental import pallas as pl
from jax.experimental.pallas import tpu as pltpu
from jax.sharding import PartitionSpec as P

BF16 = jnp.bfloat16
F32 = jnp.float32
GROUP = 128
step_size = 0.1
penalty = 1.0
I16 = jnp.int16
TURN = 65536 / (2 * math.pi)

def dot(left, right):
    return jnp.dot(left, right, preferred_element_type=F32)


def steps_over():
    return [(dx, dy) for dx in range(2) for dy in range(4)]


def moved(index, step):
    high, low = lax.div(index, 4), lax.rem(index, 4)
    return lax.rem(high + step[0], 2) * 4 + lax.rem(low + step[1], 4)


def greet_near(slab, chip, core):
    barrier = pltpu.get_barrier_semaphore()
    column = 2 * chip + core
    others = [(slab, 2 * chip + 1 - core)]
    others += [(slab, 2 * moved(chip, step) + core) for step in ((0, 1), (0, 3), (1, 0))]
    others += [(moved(slab, step), column) for step in steps_over()[1:]]
    for other in others:
        pl.semaphore_signal(barrier, inc=1, device_id=other, device_id_type=pl.DeviceIdType.MESH)


def greeted(number):
    pl.semaphore_wait(pltpu.get_barrier_semaphore(), number)


def remote(source, target, send, receive, device):
    return pltpu.make_async_remote_copy(
        src_ref=source,
        dst_ref=target,
        send_sem=send,
        recv_sem=receive,
        device_id=device,
        device_id_type=pl.DeviceIdType.MESH,
    )


def segment_of(entry, group, tiles):
    return (entry & (group - 1)) * tiles + lax.div(entry, group)


def forward_kernel(
    volume_in, templates_in, pattern, measured_in, image, observed,
    volume, templates, measured, turned_over, flat, table, counts, index, own, outgoing, pair, from_y, from_x, total,
    load_sem, pair_send, pair_recv, x_send, x_recv, y_send, y_recv, slab_send, slab_recv,
):
    slab, column = lax.axis_index("slab"), lax.axis_index("col")
    chip, core = lax.div(column, 2), lax.rem(column, 2)
    slabs, slab_rows, share, tile = image.shape
    columns = 2 * own.shape[0]
    group, tile_cells, _ = templates.shape
    tiles = table.shape[0] // group
    tile_rows, spread, angles = pattern.shape
    half = measured.shape[1] // 2
    limit = measured.shape[3]
    quarter = volume.shape[1] // 4
    greet_near(slab, chip, core)

    loads = [pltpu.make_async_copy(templates_in, templates, load_sem.at[0])]
    for part in range(4):
        span = pl.ds(part * quarter, quarter)
        loads.append(
            pltpu.make_async_copy(volume_in.at[:, span], volume.at[:, span], load_sem.at[1 + part])
        )
    loads.append(pltpu.make_async_copy(measured_in, measured, load_sem.at[5]))
    for load in loads:
        load.start()

    turned = jnp.concatenate(
        [
            pattern[:, :, base : base + tile].reshape(-1, tile).T
            for base in range(0, angles, tile)
        ],
        0,
    )
    turned = segment_of(turned, group, tiles)
    for d in range(tile_rows):
        index[pl.ds(d, angles, tile_rows), :spread] = turned[:, d * spread : (d + 1) * spread]

    loads[0].wait()
    step = tiles // 4
    for part in range(4):
        loads[1 + part].wait()
        left = jnp.concatenate(
            [
                volume[:, t * tile_cells : (t + 1) * tile_cells].astype(F32)
                for t in range(part * step, (part + 1) * step)
            ],
            0,
        ).astype(BF16)
        span = slice(part * step * slab_rows, (part + 1) * step * slab_rows)
        for k in range(0, group, 2):
            result = dot(left, jnp.concatenate([templates[k], templates[k + 1]], 1))
            flat[k, span, :] = result[:, :tile]
            flat[k + 1, span, :] = result[:, tile:]
    for k in range(group):
        for z in range(slab_rows):
            block = flat[k, pl.ds(z, tiles, slab_rows), :]
            table[k * tiles : (k + 1) * tiles, z * tile : (z + 1) * tile] = block.astype(BF16)

    greeted(11)
    lane = lax.broadcasted_iota(jnp.int32, (2 * slabs * share, tiles), 1).astype(I16)
    one, zero = jnp.ones(lane.shape, BF16), jnp.zeros(lane.shape, BF16)

    quarter_rows = slab_rows // 4
    low, high = slice(0, slab_rows // 2), slice(slab_rows // 2, slab_rows)
    across = (slab, 2 * moved(chip, (1, 0)) + core)

    def along(dy):
        return (slab, 2 * (4 * lax.div(chip, 4) + lax.rem(chip + dy, 4)) + core)

    def to_pair(d):
        return remote(
            outgoing.at[d], pair.at[d], pair_send.at[d], pair_recv.at[d],
            (slab, 2 * chip + 1 - core),
        )

    def low_across(dy):
        return remote(
            own.at[4 + dy, low], from_x.at[dy, low], x_send.at[dy], x_recv.at[dy], across
        )

    def low_along(dy):
        return remote(own.at[dy, low], from_y.at[dy, low], y_send.at[dy], y_recv.at[dy], along(dy))

    def high_along(d, dy):
        return remote(
            own.at[d, high], from_y.at[d, high], y_send.at[8 + d], y_recv.at[8 + d], along(dy)
        )

    def relay(d, side, dy):
        begin = side * (slab_rows // 2) + (dy // 2) * quarter_rows
        rows = slice(begin, begin + quarter_rows)
        number = 16 + 4 * lax.div(d, 4) + 2 * side + dy // 2
        return remote(
            own.at[d, rows], from_y.at[d, rows], y_send.at[number], y_recv.at[number], along(dy)
        )

    def take(d, side, dy):
        middle = d - dy + 2
        relay(middle, side, dy).wait_recv()
        begin = side * (slab_rows // 2) + (dy // 2) * quarter_rows

        @pl.loop(begin, begin + quarter_rows)
        def _(z):
            own[d, z] = own[d, z] + from_y[middle, z]

    def high_across():
        return remote(own.at[4, high], from_x.at[0, high], x_send.at[4], x_recv.at[4], across)

    def compute(d):
        ahead = lax.rem(lax.div(chip, 4) + lax.div(d, 4), 2)
        target = 4 * ahead + lax.rem(chip + d, 4)
        wanted = jnp.concatenate(
            [
                index[pl.ds(pl.multiple_of((s * columns + 2 * target + c) * share, share), share), :]
                for c in (core, 1 - core)
                for s in range(slabs)
            ],
            0,
        )
        wide = [
            jnp.broadcast_to(wanted[:, member : member + 1], lane.shape).astype(I16)
            for member in range(spread)
        ]
        for k in range(group):
            held = zero
            for member in range(spread):
                held = held + jnp.where(wide[member] == lane + I16(k * tiles), one, zero)
            counts[:, k * tiles : (k + 1) * tiles] = held
        for z in range(0, slab_rows, 2):
            result = dot(counts[...], table[:, z * tile : (z + 2) * tile])
            result = jnp.floor(result * TURN + 0.5).astype(jnp.int32).astype(I16)
            for more in range(2):
                part = result[:, more * tile : (more + 1) * tile]
                own[d, z + more] = part[: slabs * share].reshape(slabs, share, tile)
                outgoing[d, z + more] = part[slabs * share :].reshape(slabs, share, tile)
        to_pair(d).start()

    def add_pair(d):
        to_pair(d).wait_recv()

        @pl.loop(0, slab_rows)
        def _(z):
            own[d, z] = own[d, z] + pair[d, z]

    def add_low(dy):
        low_across(dy).wait_recv()

        @pl.loop(0, slab_rows // 2)
        def _(z):
            own[dy, z] = own[dy, z] + from_x[dy, z]

    def send_relays(d, side):
        for way in (1, 3):
            relay(d, side, way).start()

    def finish_high(d, way):
        take(d, 1, way)
        high_along(d, way).start()

    def finish_low(way):
        add_low(way)
        take(way, 0, way)
        low_along(way).start()

    def turn_corner():
        for dy in (1, 3):
            high_along(4 + dy, dy).wait_recv()

        @pl.loop(slab_rows // 2, slab_rows)
        def _(z):
            own[4, z] = own[4, z] + from_y[5, z] + from_y[7, z]

        high_across().start()

    plan = {
        1: [lambda: low_across(2).start(), lambda: send_relays(6, 1)],
        2: [lambda: send_relays(2, 1)],
        3: [lambda: low_across(1).start(), lambda: finish_high(5, 1)],
        4: [
            lambda: low_across(3).start(),
            lambda: finish_high(7, 3),
            lambda: add_low(2),
            lambda: send_relays(2, 0),
        ],
        5: [lambda: low_across(0).start()],
        6: [lambda: finish_high(1, 1), lambda: finish_low(1)],
        7: [lambda: finish_high(3, 3), lambda: finish_low(3), turn_corner],
        8: [lambda: add_low(0)],
    }
    sequence = (6, 2, 5, 7, 4, 1, 3, 0)

    def work(i, carry):
        rest, previous = carry
        d = lax.rem(rest, 8)

        @pl.when(i < 8)
        def _():
            compute(d)

        @pl.when(i > 0)
        def _():
            add_pair(previous)

        for number, actions in plan.items():

            @pl.when(i == number)
            def _():
                for action in actions:
                    action()

        return lax.div(rest, 8), d

    lax.fori_loop(0, 9, work, (sum(d * 8**n for n, d in enumerate(sequence)), 0))

    loads[5].wait()
    stores = []
    for slot in range(measured.shape[0]):

        @pl.loop(0, half, unroll=4)
        def _(row):
            both = jnp.concatenate([measured[slot, row], measured[slot, row + half]], 0)
            turned_over[slot, pl.ds(row, limit, half), :] = both.T

        stores.append(
            pltpu.make_async_copy(turned_over.at[slot], observed.at[slot], load_sem.at[6 + slot])
        )
        stores[-1].start()

    def to_slab(d, part):
        other = moved(slab, steps_over()[d])
        side = (low, high)[part]
        number = 8 * part + d
        return remote(
            total.at[other, side], image.at[slab, side], slab_send.at[number], slab_recv.at[number],
            (other, column),
        )

    for part in range(2):
        for dy in (1, 3):
            if part:
                high_along(dy, dy).wait_recv()
            else:
                low_along(dy).wait_recv()
        if part:
            high_across().wait_recv()

        @pl.loop(part * slab_rows // 2, (part + 1) * slab_rows // 2)
        def _(z):
            value = own[0, z] + from_y[1, z] + from_y[3, z]
            if part:
                value = value + from_x[0, z]
            total[:, z] = value

        for d in range(1, 8):
            to_slab(d, part).start()

    image[slab] = total[slab]
    for d in range(8):
        to_pair(d).wait_send()
    for dy in range(4):
        low_across(dy).wait_send()
    for dy in (1, 3):
        low_along(dy).wait_send()
        high_along(dy, dy).wait_send()
        high_along(4 + dy, dy).wait_send()
        relay(2, 0, dy).wait_send()
        relay(2, 1, dy).wait_send()
        relay(6, 1, dy).wait_send()
    high_across().wait_send()
    for part in range(2):
        for d in range(1, 8):
            to_slab(d, part).wait()
    for copy in stores:
        copy.wait()


def forward(volume, templates, pattern, measured, columns, slabs):
    slab_rows, cells = volume.shape
    group, tile_cells, tile = templates.shape
    tiles = cells // tile_cells
    tile_rows, spread, angles = pattern.shape
    slots, size, _, limit = measured.shape
    rows = angles * tile_rows
    share = rows // (columns * slabs)
    block = (columns // 2, slab_rows, slabs, share, tile)
    vector = pl.BlockSpec(memory_space=pltpu.VMEM)
    anywhere = pl.BlockSpec(memory_space=pl.ANY)
    sem = pltpu.SemaphoreType.DMA((8,))
    return pl.pallas_call(
        forward_kernel,
        out_shape=(
            jax.ShapeDtypeStruct((slabs, slab_rows, share, tile), I16),
            jax.ShapeDtypeStruct((slots, limit * size // 2, 2 * size), F32),
        ),
        in_specs=[anywhere, anywhere, vector, anywhere],
        out_specs=(vector, anywhere),
        scratch_shapes=[
            pltpu.VMEM(volume.shape, BF16),
            pltpu.VMEM(templates.shape, BF16),
            pltpu.VMEM(measured.shape, F32),
            pltpu.VMEM((slots, limit * size // 2, 2 * size), F32),
            pltpu.VMEM((group, tiles * slab_rows, tile), F32),
            pltpu.VMEM((group * tiles, slab_rows * tile), BF16),
            pltpu.VMEM((2 * slabs * share, group * tiles), BF16),
            pltpu.VMEM((rows, tile), jnp.int32),
        ]
        + [pltpu.VMEM(block, I16)] * 4
        + [pltpu.VMEM((4,) + block[1:], I16)]
        + [pltpu.VMEM((slabs, slab_rows, share, tile), I16)]
        + [sem] * 5
        + [pltpu.SemaphoreType.DMA((24,))] * 4,
        compiler_params=pltpu.CompilerParams(
            collective_id=1, has_side_effects=True, vmem_limit_bytes=56 * 2**20
        ),
    )(volume, templates, pattern, measured)


def trig_coefficients():
    grid = (np.cos(np.pi * (np.arange(400) + 0.5) / 400) + 1.0) * (np.pi * np.pi * 0.5005)
    root = np.sqrt(grid)
    sine = np.polynomial.Polynomial.fit(grid, np.sin(root) / root, 6).convert().coef
    cosine = np.polynomial.Polynomial.fit(grid, np.cos(root), 7).convert().coef
    return [float(v) for v in sine], [float(v) for v in cosine]


def sine_cosine(angle):
    sine, cosine = trig_coefficients()
    square = angle * angle
    sine_value = jnp.full_like(square, sine[-1])
    for value in sine[-2::-1]:
        sine_value = sine_value * square + value
    cosine_value = jnp.full_like(square, cosine[-1])
    for value in cosine[-2::-1]:
        cosine_value = cosine_value * square + value
    return sine_value * angle, cosine_value


def split_bf16(table):
    high = table.astype(np.float32).astype(BF16)
    low = (table - high.astype(np.float64)).astype(np.float32).astype(BF16)
    return high, low


def transform_tables(size):
    index = np.arange(size)
    radians = 2.0 * np.pi / size * (index[:, None] * index[None, :] % size)
    cosine = np.cos(radians) / math.sqrt(size)
    sine = np.sin(radians) / math.sqrt(size)
    zero = np.zeros_like(cosine)
    forward = np.block([[cosine, -sine], [sine, cosine]])
    pair = np.block([[cosine, zero, sine, zero], [zero, cosine, zero, sine]])
    back = np.block([[2 * sine, -2 * cosine], [2 * cosine, 2 * sine]])
    f_high, f_low = split_bf16(forward)
    p_high, p_low = split_bf16(pair)
    b_high, b_low = split_bf16(back)
    lanes = np.concatenate([f_high, f_low], 1)
    back = np.concatenate([b_high, b_low], 1)
    return (
        np.concatenate([lanes, lanes], 0),
        np.concatenate([p_high, p_high], 0),
        np.concatenate([p_high, p_low], 0),
        np.concatenate([back, back], 0),
    )


def halves(value):
    high = value.astype(BF16)
    low = (value - high.astype(F32)).astype(BF16)
    return high, low


def ptycho_kernel(
    counts, starts_in, image, probe_wave, t_first, t_pair, t_pair_both, t_back, observed_in,
    out, waves, swapped, total, staged, probe_a, probe_b, observed, starts, landed, here,
):
    slots = observed.shape[0]
    size = probe_wave.shape[1]
    limit = starts.shape[1]
    owner = lax.axis_index("slab") * lax.axis_size("col") + lax.axis_index("col")
    first_angle = owner * slots
    first_row = lax.div(first_angle, 8) * 8
    load = pltpu.make_async_copy(starts_in.at[pl.ds(pl.multiple_of(first_row, 8), 8)], starts, landed)
    load.start()
    fetches = [
        pltpu.make_async_copy(observed_in.at[slot], observed.at[slot], here.at[slot])
        for slot in range(slots)
    ]
    for fetch in fetches:
        fetch.start()
    both = jnp.concatenate([probe_wave[0], probe_wave[0]], 0)
    probe_a[...] = both.T
    both = jnp.concatenate([-probe_wave[1], probe_wave[1]], 0)
    probe_b[...] = both.T
    width = waves.shape[0]
    tile = image.shape[1]
    rows = width // tile * slots
    chunk_count = limit // GROUP

    def used_chunks(slot):
        return jnp.clip(lax.div(counts[first_angle + slot] + (GROUP - 1), GROUP), 0, chunk_count)

    half = size // 2

    staged[...] = image[...].astype(jnp.int32).astype(F32) * (2 * math.pi / 65536)
    load.wait()
    lane = lax.broadcasted_iota(jnp.int32, (size, 2 * size), 1)

    @pl.loop(0, slots)
    def _(slot):
        pltpu.make_async_copy(observed_in.at[slot], observed.at[slot], here.at[slot]).wait()
        for part in range(width // tile):
            sine, cosine = sine_cosine(staged[pl.ds(slot * (width // tile) + part, size, rows), :])
            waves[part * tile : (part + 1) * tile, :] = jnp.concatenate([cosine, sine], 0).T
            swapped[part * tile : (part + 1) * tile, :] = jnp.concatenate([sine, cosine], 0).T
        total[...] = jnp.zeros_like(total)
        count = counts[first_angle + slot]

        @pl.loop(0, used_chunks(slot))
        def _(chunk):
            begin = chunk * GROUP
            at = [starts[first_angle - first_row + slot, begin + member] for member in range(GROUP)]
            exits = []
            for member in range(GROUP):
                patch = waves[pl.ds(at[member], size), :]
                exits.append(probe_a[...] * patch + probe_b[...] * swapped[pl.ds(at[member], size), :])
            exit_wave = jnp.concatenate(exits, 0)
            high, low = halves(exit_wave)
            first = dot(jnp.concatenate([high, low], 1), t_first[...])
            first = first[:, : 2 * size] + first[:, 2 * size :]
            turned = jnp.concatenate(
                [first[pair * 2 * size : (pair + 1) * 2 * size].T for pair in range(GROUP // 2)], 0
            )
            high, low = halves(turned)
            second = dot(jnp.concatenate([high, low], 1), t_pair[...])
            second = second + dot(high, t_pair_both[2 * size :, :])
            scaled = []
            for pair in range(GROUP // 2):
                block = second[pair * 2 * size : (pair + 1) * 2 * size]
                real = block[:size, : 2 * size] + block[size:, 2 * size :]
                imag = block[size:, : 2 * size] - block[:size, 2 * size :]
                member = begin + 2 * pair
                seen = [
                    observed[slot, pl.ds(pl.multiple_of((member + m) * half, half), half), :]
                    for m in range(2)
                ]
                seen = jnp.concatenate(
                    [
                        jnp.concatenate([seen[0][:, :size], seen[1][:, :size]], 1),
                        jnp.concatenate([seen[0][:, size:], seen[1][:, size:]], 1),
                    ],
                    0,
                )
                residual = real * real + imag * imag - seen
                live = member + jnp.where(lane >= size, 1, 0) < count
                residual = jnp.where(live, residual, 0.0)
                scaled += [residual * real, residual * imag]
            scaled = jnp.concatenate(scaled, 0).astype(BF16)
            third = dot(jnp.concatenate([scaled, scaled], 1), t_pair_both[...])
            turned = []
            for pair in range(GROUP // 2):
                block = third[pair * 2 * size : (pair + 1) * 2 * size]
                real = block[:size, : 2 * size] - block[size:, 2 * size :]
                imag = block[size:, : 2 * size] + block[:size, 2 * size :]
                turned.append(jnp.concatenate([real, imag], 0).T)
            high, low = halves(jnp.concatenate(turned, 0))
            back = dot(jnp.concatenate([high, low], 1), t_back[...])
            gradient = exit_wave * (back[:, : 2 * size] + back[:, 2 * size :])
            for member in range(GROUP):
                span = pl.ds(at[member], size)
                total[span, :] = total[span, :] + gradient[member * size : (member + 1) * size]

        for part in range(width // tile):
            flat = total[part * tile : (part + 1) * tile, :].T
            staged[pl.ds(slot * (width // tile) + part, size, rows), :] = flat[:size] + flat[size:]

    out[...] = staged[...].astype(BF16)


def ptycho(image, probe_wave, observed, counts, starts):
    slots = observed.shape[0]
    size = probe_wave.shape[1]
    height, tile = image.shape
    width = height // size // slots * tile
    tables = [jnp.asarray(table) for table in transform_tables(size)]
    vector = pl.BlockSpec(memory_space=pltpu.VMEM)
    return pl.pallas_call(
        ptycho_kernel,
        out_shape=jax.ShapeDtypeStruct((height, tile), BF16),
        in_specs=[pl.BlockSpec(memory_space=pltpu.SMEM), pl.BlockSpec(memory_space=pl.ANY)]
        + [vector] * 6
        + [pl.BlockSpec(memory_space=pl.ANY)],
        out_specs=vector,
        scratch_shapes=[
            pltpu.VMEM((width, 2 * size), F32),
            pltpu.VMEM((width, 2 * size), F32),
            pltpu.VMEM((width, 2 * size), F32),
            pltpu.VMEM((height, tile), F32),
            pltpu.VMEM((size, 2 * size), F32),
            pltpu.VMEM((size, 2 * size), F32),
            pltpu.VMEM(observed.shape, F32),
            pltpu.SMEM((8, starts.shape[1]), jnp.int32),
            pltpu.SemaphoreType.DMA,
            pltpu.SemaphoreType.DMA((slots,)),
        ],
        compiler_params=pltpu.CompilerParams(vmem_limit_bytes=56 * 2**20),
    )(counts, starts, image, probe_wave, *tables, observed)


def collect_kernel(
    grads, pattern, out, mine, held, twin, counts, index, total, flat,
    slab_send, slab_recv, chip_send, chip_recv, pair_send, pair_recv,
):
    slab, column = lax.axis_index("slab"), lax.axis_index("col")
    chip, core = lax.div(column, 2), lax.rem(column, 2)
    sibling = (slab, 2 * chip + 1 - core)
    steps = steps_over()
    slabs, slab_rows, share, tile = grads.shape
    tile_rows, spread, angles = pattern.shape
    group, _, _ = out.shape
    tiles = out.shape[1] // slab_rows
    columns = angles * tile_rows // (slabs * share)
    greet_near(slab, chip, core)
    greeted(11)

    order = [1, 3, 4, 2, 5, 7, 6]
    slabs_, chips, pairs = {}, {}, {}
    for d in order:
        other = moved(slab, steps[d])
        slabs_[d] = remote(
            grads.at[other], mine.at[slab], slab_send.at[d], slab_recv.at[d], (other, column)
        )
        slabs_[d].start()
    mine[slab] = grads[slab]

    turned = jnp.concatenate(
        [
            pattern[:, :, base : base + tile].reshape(-1, tile).T
            for base in range(0, angles, tile)
        ],
        0,
    )
    turned = segment_of(turned, group, tiles)
    for d in range(tile_rows):
        index[pl.ds(d, angles, tile_rows), :spread] = turned[:, d * spread : (d + 1) * spread]

    for d in order:
        slabs_[d].wait_recv()
    half, quarter = slab_rows // 2, slab_rows // 4
    low, high = slice(0, half), slice(half, slab_rows)
    upper, lower = slice(half, half + quarter), slice(half + quarter, slab_rows)
    across = (slab, 2 * moved(chip, (1, 0)) + core)
    up = (slab, 2 * moved(chip, (0, 1)) + core)
    down = (slab, 2 * moved(chip, (0, 3)) + core)

    def pass_on(number, source, target, rows, device):
        chips[number] = remote(
            (mine if source == 0 else held.at[source]).at[:, rows], held.at[target, :, rows],
            chip_send.at[number], chip_recv.at[number], device,
        )
        chips[number].start()

    whole = slice(0, slab_rows)
    pass_on(0, 0, 1, whole, up)
    pass_on(1, 0, 3, whole, down)
    pass_on(2, 0, 4, whole, across)
    pairs[0] = remote(mine, twin.at[0], pair_send.at[0], pair_recv.at[0], sibling)
    pairs[0].start()

    row = lax.broadcasted_iota(jnp.int32, (tiles, 2 * slabs * share), 0).astype(I16)
    one, zero = jnp.ones(row.shape, BF16), jnp.zeros(row.shape, BF16)

    @pl.loop(0, columns // 2)
    def _(origin):
        wanted = jnp.concatenate(
            [
                index[pl.ds(pl.multiple_of((s * columns + 2 * origin + c) * share, share), share), :]
                for c in range(2)
                for s in range(slabs)
            ],
            0,
        ).T
        wide = [
            jnp.broadcast_to(wanted[member : member + 1, :], row.shape).astype(I16)
            for member in range(spread)
        ]
        for k in range(group):
            held_here = zero
            for member in range(spread):
                held_here = held_here + jnp.where(wide[member] == row + I16(k * tiles), one, zero)
            counts[origin, k * tiles : (k + 1) * tiles, :] = held_here

    def add(d, near, far):
        if d:
            origin = moved(chip, ((2 - steps[d][0]) % 2, (4 - steps[d][1]) % 4))
        else:
            origin = chip
        swapped = core == 1
        for z in range(0, slab_rows, 2):
            parts = []
            for more in range(2):
                a = near[:, z + more].reshape(slabs * share, tile)
                b = far[:, z + more].reshape(slabs * share, tile)
                parts.append(
                    jnp.concatenate([jnp.where(swapped, b, a), jnp.where(swapped, a, b)], 0)
                )
            right = jnp.concatenate(parts, 1)
            for base in range(0, group * tiles, 256):
                result = dot(counts[origin, base : base + 256, :], right)
                span = slice(base, base + 256)
                lanes = slice(z * tile, (z + 2) * tile)
                if d:
                    result = result + total[span, lanes]
                total[span, lanes] = result

    def arrived(*numbers):
        for number in numbers:
            chips[number].wait_recv()

    def to_sibling(d):
        pairs[d] = remote(held.at[d], twin.at[d], pair_send.at[d], pair_recv.at[d], sibling)
        pairs[d].start()

    def use(d):
        pairs[d].wait_recv()
        add(d, held.at[d] if d else mine, twin.at[d])

    arrived(0)
    pass_on(3, 1, 2, low, up)
    pass_on(4, 1, 5, low, across)
    to_sibling(1)
    arrived(1)
    pass_on(5, 3, 2, high, down)
    pass_on(6, 3, 7, low, across)
    to_sibling(3)
    arrived(2)
    pass_on(7, 4, 5, high, up)
    pass_on(8, 4, 7, high, down)
    to_sibling(4)
    use(0)
    arrived(3)
    pass_on(9, 2, 6, low, across)
    use(1)
    arrived(7)
    pass_on(10, 5, 6, upper, up)
    arrived(8)
    pass_on(11, 7, 6, lower, down)
    use(3)
    arrived(5)
    to_sibling(2)
    use(4)
    arrived(4)
    to_sibling(5)
    use(2)
    arrived(6)
    to_sibling(7)
    use(5)
    arrived(9, 10, 11)
    to_sibling(6)
    use(7)
    use(6)

    for k in range(group):
        for z in range(slab_rows):
            block = total[k * tiles : (k + 1) * tiles, z * tile : (z + 1) * tile]
            flat[pl.ds(z, tiles, slab_rows), :] = block
        out[k] = flat[...].astype(BF16)

    for d in order:
        slabs_[d].wait_send()
    for number in range(12):
        chips[number].wait_send()
    for d in [0] + order:
        pairs[d].wait_send()


def collect(grads, pattern, templates, tiles):
    slabs, slab_rows, share, tile = grads.shape
    group, tile_cells, _ = templates.shape
    tile_rows, spread, angles = pattern.shape
    columns = angles * tile_rows // (slabs * share)
    vector = pl.BlockSpec(memory_space=pltpu.VMEM)
    sem = pltpu.SemaphoreType.DMA((8,))
    return pl.pallas_call(
        collect_kernel,
        out_shape=jax.ShapeDtypeStruct((group, tiles * slab_rows, tile), BF16),
        in_specs=[vector, vector],
        out_specs=vector,
        scratch_shapes=[
            pltpu.VMEM(grads.shape, BF16),
            pltpu.VMEM((8,) + grads.shape, BF16),
            pltpu.VMEM((8,) + grads.shape, BF16),
            pltpu.VMEM((columns // 2, group * tiles, 2 * slabs * share), BF16),
            pltpu.VMEM((angles * tile_rows, tile), jnp.int32),
            pltpu.VMEM((group * tiles, slab_rows * tile), F32),
            pltpu.VMEM((tiles * slab_rows, tile), F32),
        ]
        + [sem, sem, pltpu.SemaphoreType.DMA((12,)), pltpu.SemaphoreType.DMA((12,)), sem, sem],
        compiler_params=pltpu.CompilerParams(
            collective_id=2, has_side_effects=True, vmem_limit_bytes=32 * 2**20
        ),
    )(grads, pattern)


def update_kernel(sums, templates, volume, consensus, out):
    group, size, tile = sums.shape
    tile_cells = templates.shape[1]
    slab_rows = volume.shape[0]
    left = jnp.concatenate([sums[k] for k in range(group)], 1)
    for part in range(0, tile_cells, 256):
        total = jnp.zeros((size, 256), F32)
        for k in range(0, group, 2):
            right = jnp.concatenate(
                [templates[k, part : part + 256, :], templates[k + 1, part : part + 256, :]], 1
            )
            total = total + lax.dot_general(
                left[:, k * tile : (k + 2) * tile],
                right,
                (((1,), (1,)), ((), ())),
                preferred_element_type=F32,
            )
        for t in range(size // slab_rows):
            span = slice(t * tile_cells + part, t * tile_cells + part + 256)
            own_volume = volume[:, span].astype(F32)
            wanted = consensus[:, span].astype(F32)
            moved_by = total[t * slab_rows : (t + 1) * slab_rows]
            out[:, span] = own_volume - step_size * (moved_by + penalty * (own_volume - wanted))


def update(sums, templates, volume, consensus):
    slab_rows, cells = volume.shape
    group, height, tile = sums.shape
    steps = 4
    block = pl.BlockSpec((slab_rows, cells // steps), lambda i: (0, i))
    return pl.pallas_call(
        update_kernel,
        grid=(steps,),
        out_shape=jax.ShapeDtypeStruct((slab_rows, cells), F32),
        in_specs=[
            pl.BlockSpec((group, height // steps, tile), lambda i: (0, i, 0)),
            pl.BlockSpec(templates.shape, lambda i: (0, 0, 0)),
            block,
            block,
        ],
        out_specs=block,
        compiler_params=pltpu.CompilerParams(vmem_limit_bytes=20 * 2**20),
    )(sums, templates, volume, consensus)


def on_device(
    volume, consensus, templates, pattern, probe_wave, measured, scan_counts, scan_positions
):
    slab_rows = volume.shape[0]
    tile = templates.shape[2]
    slab_count = lax.axis_size("slab")
    column_count = lax.axis_size("col")
    angle_count, tile_rows, spread = pattern.shape[1:]
    per_owner = angle_count // (slab_count * column_count)
    own = per_owner * tile_rows
    rows = angle_count * tile_rows

    image, observed = forward(
        volume,
        templates,
        pattern[0].transpose(1, 2, 0),
        measured.transpose(0, 2, 3, 1),
        column_count,
        slab_count,
    )
    image = image.reshape(slab_count * slab_rows * own, tile)
    gradients = ptycho(image, probe_wave, observed, scan_counts, scan_positions)
    sums = collect(
        gradients.reshape(slab_count, slab_rows, own, tile),
        pattern[0].transpose(1, 2, 0),
        templates,
        volume.shape[1] // templates.shape[1],
    )
    return update(sums, templates, volume, consensus)


def solution(mesh):
    return jax.shard_map(
        on_device,
        mesh=mesh,
        in_specs=(
            P("slab", "col"),
            P("slab", "col"),
            P("col", None, None),
            P("col", None, None, None),
            P(),
            P(("slab", "col"), None, None, None),
            P(),
            P(),
        ),
        out_specs=P("slab", "col"),
        check_vma=False,
    )
```

```python
import functools
import math

import jax
import jax.numpy as jnp
import numpy as np
from jax import lax
from jax.experimental import pallas as pl
from jax.experimental.pallas import tpu as pltpu
from jax.sharding import PartitionSpec as P

BF16 = jnp.bfloat16
F32 = jnp.float32
GROUP = 64
step_size = 0.1
penalty = 1.0
I16 = jnp.int16
TURN = 65536 / (2 * math.pi)

def dot(left, right):
    return jnp.dot(left, right, preferred_element_type=F32)


def steps_over():
    return [(dx, dy) for dx in range(2) for dy in range(4)]


def moved(index, step):
    high, low = lax.div(index, 4), lax.rem(index, 4)
    return lax.rem(high + step[0], 2) * 4 + lax.rem(low + step[1], 4)


def greet_near(slab, chip, core):
    barrier = pltpu.get_barrier_semaphore()
    column = 2 * chip + core
    others = [(slab, 2 * chip + 1 - core)]
    others += [(slab, 2 * moved(chip, step) + core) for step in ((0, 1), (0, 3), (1, 0))]
    others += [(moved(slab, step), column) for step in steps_over()[1:]]
    for other in others:
        pl.semaphore_signal(barrier, inc=1, device_id=other, device_id_type=pl.DeviceIdType.MESH)


def greeted(number):
    pl.semaphore_wait(pltpu.get_barrier_semaphore(), number)


def remote(source, target, send, receive, device):
    return pltpu.make_async_remote_copy(
        src_ref=source,
        dst_ref=target,
        send_sem=send,
        recv_sem=receive,
        device_id=device,
        device_id_type=pl.DeviceIdType.MESH,
    )


def segment_of(entry, group, tiles):
    return (entry & (group - 1)) * tiles + lax.div(entry, group)


def forward_kernel(
    volume_in, templates_in, pattern, measured_in, image, observed,
    volume, templates, measured, turned_over, flat, table, counts, index, own, outgoing, pair, from_y, from_x, total,
    load_sem, pair_send, pair_recv, x_send, x_recv, y_send, y_recv, slab_send, slab_recv,
):
    slab, column = lax.axis_index("slab"), lax.axis_index("col")
    chip, core = lax.div(column, 2), lax.rem(column, 2)
    slabs, slab_rows, share, tile = image.shape
    columns = 2 * own.shape[0]
    group, tile_cells, _ = templates.shape
    tiles = table.shape[0] // group
    tile_rows, spread, angles = pattern.shape
    half = measured.shape[1] // 2
    limit = measured.shape[3]
    quarter = volume.shape[1] // 4
    greet_near(slab, chip, core)

    loads = [pltpu.make_async_copy(templates_in, templates, load_sem.at[0])]
    for part in range(4):
        span = pl.ds(part * quarter, quarter)
        loads.append(
            pltpu.make_async_copy(volume_in.at[:, span], volume.at[:, span], load_sem.at[1 + part])
        )
    loads.append(pltpu.make_async_copy(measured_in, measured, load_sem.at[5]))
    for load in loads:
        load.start()

    turned = jnp.concatenate(
        [
            pattern[:, :, base : base + tile].reshape(-1, tile).T
            for base in range(0, angles, tile)
        ],
        0,
    )
    turned = segment_of(turned, group, tiles)
    for d in range(tile_rows):
        index[pl.ds(d, angles, tile_rows), :spread] = turned[:, d * spread : (d + 1) * spread]

    loads[0].wait()
    step = tiles // 4
    for part in range(4):
        loads[1 + part].wait()
        left = jnp.concatenate(
            [
                volume[:, t * tile_cells : (t + 1) * tile_cells].astype(F32)
                for t in range(part * step, (part + 1) * step)
            ],
            0,
        ).astype(BF16)
        span = slice(part * step * slab_rows, (part + 1) * step * slab_rows)
        for k in range(0, group, 2):
            result = dot(left, jnp.concatenate([templates[k], templates[k + 1]], 1))
            flat[k, span, :] = result[:, :tile]
            flat[k + 1, span, :] = result[:, tile:]
    for k in range(group):
        for z in range(slab_rows):
            block = flat[k, pl.ds(z, tiles, slab_rows), :]
            table[k * tiles : (k + 1) * tiles, z * tile : (z + 1) * tile] = block.astype(BF16)

    greeted(11)
    lane = lax.broadcasted_iota(jnp.int32, (2 * slabs * share, tiles), 1).astype(I16)
    one, zero = jnp.ones(lane.shape, BF16), jnp.zeros(lane.shape, BF16)

    quarter_rows = slab_rows // 4
    low, high = slice(0, slab_rows // 2), slice(slab_rows // 2, slab_rows)
    across = (slab, 2 * moved(chip, (1, 0)) + core)

    def along(dy):
        return (slab, 2 * (4 * lax.div(chip, 4) + lax.rem(chip + dy, 4)) + core)

    def to_pair(d):
        return remote(
            outgoing.at[d], pair.at[d], pair_send.at[d], pair_recv.at[d],
            (slab, 2 * chip + 1 - core),
        )

    def low_across(dy):
        return remote(
            own.at[4 + dy, low], from_x.at[dy, low], x_send.at[dy], x_recv.at[dy], across
        )

    def low_along(dy):
        return remote(own.at[dy, low], from_y.at[dy, low], y_send.at[dy], y_recv.at[dy], along(dy))

    def high_along(d, dy):
        return remote(
            own.at[d, high], from_y.at[d, high], y_send.at[8 + d], y_recv.at[8 + d], along(dy)
        )

    def relay(d, side, dy):
        begin = side * (slab_rows // 2) + (dy // 2) * quarter_rows
        rows = slice(begin, begin + quarter_rows)
        number = 16 + 4 * lax.div(d, 4) + 2 * side + dy // 2
        return remote(
            own.at[d, rows], from_y.at[d, rows], y_send.at[number], y_recv.at[number], along(dy)
        )

    def take(d, side, dy):
        middle = d - dy + 2
        relay(middle, side, dy).wait_recv()
        begin = side * (slab_rows // 2) + (dy // 2) * quarter_rows

        @pl.loop(begin, begin + quarter_rows)
        def _(z):
            own[d, z] = own[d, z] + from_y[middle, z]

    def high_across():
        return remote(own.at[4, high], from_x.at[0, high], x_send.at[4], x_recv.at[4], across)

    def compute(d):
        ahead = lax.rem(lax.div(chip, 4) + lax.div(d, 4), 2)
        target = 4 * ahead + lax.rem(chip + d, 4)
        wanted = jnp.concatenate(
            [
                index[pl.ds(pl.multiple_of((s * columns + 2 * target + c) * share, share), share), :]
                for c in (core, 1 - core)
                for s in range(slabs)
            ],
            0,
        )
        wide = [
            jnp.broadcast_to(wanted[:, member : member + 1], lane.shape).astype(I16)
            for member in range(spread)
        ]
        for k in range(group):
            held = zero
            for member in range(spread):
                held = held + jnp.where(wide[member] == lane + I16(k * tiles), one, zero)
            counts[:, k * tiles : (k + 1) * tiles] = held
        for z in range(0, slab_rows, 2):
            result = dot(counts[...], table[:, z * tile : (z + 2) * tile])
            result = jnp.floor(result * TURN + 0.5).astype(jnp.int32).astype(I16)
            for more in range(2):
                part = result[:, more * tile : (more + 1) * tile]
                own[d, z + more] = part[: slabs * share].reshape(slabs, share, tile)
                outgoing[d, z + more] = part[slabs * share :].reshape(slabs, share, tile)
        to_pair(d).start()

    def add_pair(d):
        to_pair(d).wait_recv()

        @pl.loop(0, slab_rows)
        def _(z):
            own[d, z] = own[d, z] + pair[d, z]

    def add_low(dy):
        low_across(dy).wait_recv()

        @pl.loop(0, slab_rows // 2)
        def _(z):
            own[dy, z] = own[dy, z] + from_x[dy, z]

    def send_relays(d, side):
        for way in (1, 3):
            relay(d, side, way).start()

    def finish_high(d, way):
        take(d, 1, way)
        high_along(d, way).start()

    def finish_low(way):
        add_low(way)
        take(way, 0, way)
        low_along(way).start()

    def turn_corner():
        for dy in (1, 3):
            high_along(4 + dy, dy).wait_recv()

        @pl.loop(slab_rows // 2, slab_rows)
        def _(z):
            own[4, z] = own[4, z] + from_y[5, z] + from_y[7, z]

        high_across().start()

    plan = {
        1: [lambda: low_across(2).start(), lambda: send_relays(6, 1)],
        2: [lambda: send_relays(2, 1)],
        3: [lambda: low_across(1).start(), lambda: finish_high(5, 1)],
        4: [
            lambda: low_across(3).start(),
            lambda: finish_high(7, 3),
            lambda: add_low(2),
            lambda: send_relays(2, 0),
        ],
        5: [lambda: low_across(0).start()],
        6: [lambda: finish_high(1, 1), lambda: finish_low(1)],
        7: [lambda: finish_high(3, 3), lambda: finish_low(3), turn_corner],
        8: [lambda: add_low(0)],
    }
    sequence = (6, 2, 5, 7, 4, 1, 3, 0)

    def work(i, carry):
        rest, previous = carry
        d = lax.rem(rest, 8)

        @pl.when(i < 8)
        def _():
            compute(d)

        @pl.when(i > 0)
        def _():
            add_pair(previous)

        for number, actions in plan.items():

            @pl.when(i == number)
            def _():
                for action in actions:
                    action()

        return lax.div(rest, 8), d

    lax.fori_loop(0, 9, work, (sum(d * 8**n for n, d in enumerate(sequence)), 0))

    loads[5].wait()
    stores = []
    for slot in range(measured.shape[0]):

        @pl.loop(0, half, unroll=4)
        def _(row):
            both = jnp.concatenate([measured[slot, row], measured[slot, row + half]], 0)
            turned_over[slot, pl.ds(row, limit, half), :] = both.T

        stores.append(
            pltpu.make_async_copy(turned_over.at[slot], observed.at[slot], load_sem.at[6 + slot])
        )
        stores[-1].start()

    def to_slab(d, part):
        other = moved(slab, steps_over()[d])
        side = (low, high)[part]
        number = 8 * part + d
        return remote(
            total.at[other, side], image.at[slab, side], slab_send.at[number], slab_recv.at[number],
            (other, column),
        )

    for part in range(2):
        for dy in (1, 3):
            if part:
                high_along(dy, dy).wait_recv()
            else:
                low_along(dy).wait_recv()
        if part:
            high_across().wait_recv()

        @pl.loop(part * slab_rows // 2, (part + 1) * slab_rows // 2)
        def _(z):
            value = own[0, z] + from_y[1, z] + from_y[3, z]
            if part:
                value = value + from_x[0, z]
            total[:, z] = value

        for d in range(1, 8):
            to_slab(d, part).start()

    image[slab] = total[slab]
    for d in range(8):
        to_pair(d).wait_send()
    for dy in range(4):
        low_across(dy).wait_send()
    for dy in (1, 3):
        low_along(dy).wait_send()
        high_along(dy, dy).wait_send()
        high_along(4 + dy, dy).wait_send()
        relay(2, 0, dy).wait_send()
        relay(2, 1, dy).wait_send()
        relay(6, 1, dy).wait_send()
    high_across().wait_send()
    for part in range(2):
        for d in range(1, 8):
            to_slab(d, part).wait()
    for copy in stores:
        copy.wait()


def forward(volume, templates, pattern, measured, columns, slabs):
    slab_rows, cells = volume.shape
    group, tile_cells, tile = templates.shape
    tiles = cells // tile_cells
    tile_rows, spread, angles = pattern.shape
    slots, size, _, limit = measured.shape
    rows = angles * tile_rows
    share = rows // (columns * slabs)
    block = (columns // 2, slab_rows, slabs, share, tile)
    vector = pl.BlockSpec(memory_space=pltpu.VMEM)
    anywhere = pl.BlockSpec(memory_space=pl.ANY)
    sem = pltpu.SemaphoreType.DMA((8,))
    return pl.pallas_call(
        forward_kernel,
        out_shape=(
            jax.ShapeDtypeStruct((slabs, slab_rows, share, tile), I16),
            jax.ShapeDtypeStruct((slots, limit * size // 2, 2 * size), F32),
        ),
        in_specs=[anywhere, anywhere, vector, anywhere],
        out_specs=(vector, anywhere),
        scratch_shapes=[
            pltpu.VMEM(volume.shape, BF16),
            pltpu.VMEM(templates.shape, BF16),
            pltpu.VMEM(measured.shape, F32),
            pltpu.VMEM((slots, limit * size // 2, 2 * size), F32),
            pltpu.VMEM((group, tiles * slab_rows, tile), F32),
            pltpu.VMEM((group * tiles, slab_rows * tile), BF16),
            pltpu.VMEM((2 * slabs * share, group * tiles), BF16),
            pltpu.VMEM((rows, tile), jnp.int32),
        ]
        + [pltpu.VMEM(block, I16)] * 4
        + [pltpu.VMEM((4,) + block[1:], I16)]
        + [pltpu.VMEM((slabs, slab_rows, share, tile), I16)]
        + [sem] * 5
        + [pltpu.SemaphoreType.DMA((24,))] * 4,
        compiler_params=pltpu.CompilerParams(
            collective_id=1, has_side_effects=True, vmem_limit_bytes=56 * 2**20
        ),
    )(volume, templates, pattern, measured)


def trig_coefficients():
    grid = (np.cos(np.pi * (np.arange(400) + 0.5) / 400) + 1.0) * (np.pi * np.pi * 0.5005)
    root = np.sqrt(grid)
    sine = np.polynomial.Polynomial.fit(grid, np.sin(root) / root, 6).convert().coef
    cosine = np.polynomial.Polynomial.fit(grid, np.cos(root), 7).convert().coef
    return [float(v) for v in sine], [float(v) for v in cosine]


def sine_cosine(angle):
    sine, cosine = trig_coefficients()
    square = angle * angle
    sine_value = jnp.full_like(square, sine[-1])
    for value in sine[-2::-1]:
        sine_value = sine_value * square + value
    cosine_value = jnp.full_like(square, cosine[-1])
    for value in cosine[-2::-1]:
        cosine_value = cosine_value * square + value
    return sine_value * angle, cosine_value


def split_bf16(table):
    high = table.astype(np.float32).astype(BF16)
    low = (table - high.astype(np.float64)).astype(np.float32).astype(BF16)
    return high, low


def transform_tables(size):
    index = np.arange(size)
    radians = 2.0 * np.pi / size * (index[:, None] * index[None, :] % size)
    cosine = np.cos(radians) / math.sqrt(size)
    sine = np.sin(radians) / math.sqrt(size)
    zero = np.zeros_like(cosine)
    forward = np.block([[cosine, -sine], [sine, cosine]])
    pair = np.block([[cosine, zero, sine, zero], [zero, cosine, zero, sine]])
    back = np.block([[2 * sine, -2 * cosine], [2 * cosine, 2 * sine]])
    f_high, f_low = split_bf16(forward)
    p_high, p_low = split_bf16(pair)
    b_high, b_low = split_bf16(back)
    lanes = np.concatenate([f_high, f_low], 1)
    back = np.concatenate([b_high, b_low], 1)
    return (
        np.concatenate([lanes, lanes], 0),
        np.concatenate([p_high, p_high], 0),
        np.concatenate([p_high, p_low], 0),
        np.concatenate([back, back], 0),
    )


def halves(value):
    high = value.astype(BF16)
    low = (value - high.astype(F32)).astype(BF16)
    return high, low


def ptycho_kernel(
    counts, starts_in, image, probe_wave, t_first, t_pair, t_pair_both, t_back, observed_in,
    out, waves, swapped, total, staged, probe_a, probe_b, observed, starts, landed, here,
):
    slots = observed.shape[0]
    size = probe_wave.shape[1]
    limit = starts.shape[1]
    owner = lax.axis_index("slab") * lax.axis_size("col") + lax.axis_index("col")
    first_angle = owner * slots
    first_row = lax.div(first_angle, 8) * 8
    load = pltpu.make_async_copy(starts_in.at[pl.ds(pl.multiple_of(first_row, 8), 8)], starts, landed)
    load.start()
    fetches = [
        pltpu.make_async_copy(observed_in.at[slot], observed.at[slot], here.at[slot])
        for slot in range(slots)
    ]
    for fetch in fetches:
        fetch.start()
    both = jnp.concatenate([probe_wave[0], probe_wave[0]], 0)
    probe_a[...] = both.T
    both = jnp.concatenate([-probe_wave[1], probe_wave[1]], 0)
    probe_b[...] = both.T
    width = waves.shape[0]
    tile = image.shape[1]
    rows = width // tile * slots
    chunk_count = limit // GROUP

    def used_chunks(slot):
        return jnp.clip(lax.div(counts[first_angle + slot] + (GROUP - 1), GROUP), 0, chunk_count)

    half = size // 2

    staged[...] = image[...].astype(jnp.int32).astype(F32) * (2 * math.pi / 65536)
    load.wait()
    lane = lax.broadcasted_iota(jnp.int32, (size, 2 * size), 1)

    @pl.loop(0, slots)
    def _(slot):
        pltpu.make_async_copy(observed_in.at[slot], observed.at[slot], here.at[slot]).wait()
        for part in range(width // tile):
            sine, cosine = sine_cosine(staged[pl.ds(slot * (width // tile) + part, size, rows), :])
            waves[part * tile : (part + 1) * tile, :] = jnp.concatenate([cosine, sine], 0).T
            swapped[part * tile : (part + 1) * tile, :] = jnp.concatenate([sine, cosine], 0).T
        total[...] = jnp.zeros_like(total)
        count = counts[first_angle + slot]

        @pl.loop(0, used_chunks(slot))
        def _(chunk):
            begin = chunk * GROUP
            at = [starts[first_angle - first_row + slot, begin + member] for member in range(GROUP)]
            exits = []
            for member in range(GROUP):
                patch = waves[pl.ds(at[member], size), :]
                exits.append(probe_a[...] * patch + probe_b[...] * swapped[pl.ds(at[member], size), :])
            exit_wave = jnp.concatenate(exits, 0)
            high, low = halves(exit_wave)
            first = dot(jnp.concatenate([high, low], 1), t_first[...])
            first = first[:, : 2 * size] + first[:, 2 * size :]
            turned = jnp.concatenate(
                [first[pair * 2 * size : (pair + 1) * 2 * size].T for pair in range(GROUP // 2)], 0
            )
            high, low = halves(turned)
            second = dot(jnp.concatenate([high, low], 1), t_pair[...])
            second = second + dot(high, t_pair_both[2 * size :, :])
            scaled = []
            for pair in range(GROUP // 2):
                block = second[pair * 2 * size : (pair + 1) * 2 * size]
                real = block[:size, : 2 * size] + block[size:, 2 * size :]
                imag = block[size:, : 2 * size] - block[:size, 2 * size :]
                member = begin + 2 * pair
                seen = [
                    observed[slot, pl.ds(pl.multiple_of((member + m) * half, half), half), :]
                    for m in range(2)
                ]
                seen = jnp.concatenate(
                    [
                        jnp.concatenate([seen[0][:, :size], seen[1][:, :size]], 1),
                        jnp.concatenate([seen[0][:, size:], seen[1][:, size:]], 1),
                    ],
                    0,
                )
                residual = real * real + imag * imag - seen
                live = member + jnp.where(lane >= size, 1, 0) < count
                residual = jnp.where(live, residual, 0.0)
                scaled += [residual * real, residual * imag]
            scaled = jnp.concatenate(scaled, 0).astype(BF16)
            third = dot(jnp.concatenate([scaled, scaled], 1), t_pair_both[...])
            turned = []
            for pair in range(GROUP // 2):
                block = third[pair * 2 * size : (pair + 1) * 2 * size]
                real = block[:size, : 2 * size] - block[size:, 2 * size :]
                imag = block[size:, : 2 * size] + block[:size, 2 * size :]
                turned.append(jnp.concatenate([real, imag], 0).T)
            high, low = halves(jnp.concatenate(turned, 0))
            back = dot(jnp.concatenate([high, low], 1), t_back[...])
            gradient = exit_wave * (back[:, : 2 * size] + back[:, 2 * size :])
            for member in range(GROUP):
                span = pl.ds(at[member], size)
                total[span, :] = total[span, :] + gradient[member * size : (member + 1) * size]

        for part in range(width // tile):
            flat = total[part * tile : (part + 1) * tile, :].T
            staged[pl.ds(slot * (width // tile) + part, size, rows), :] = flat[:size] + flat[size:]

    out[...] = staged[...].astype(BF16)


def ptycho(image, probe_wave, observed, counts, starts):
    slots = observed.shape[0]
    size = probe_wave.shape[1]
    height, tile = image.shape
    width = height // size // slots * tile
    tables = [jnp.asarray(table) for table in transform_tables(size)]
    vector = pl.BlockSpec(memory_space=pltpu.VMEM)
    return pl.pallas_call(
        ptycho_kernel,
        out_shape=jax.ShapeDtypeStruct((height, tile), BF16),
        in_specs=[pl.BlockSpec(memory_space=pltpu.SMEM), pl.BlockSpec(memory_space=pl.ANY)]
        + [vector] * 6
        + [pl.BlockSpec(memory_space=pl.ANY)],
        out_specs=vector,
        scratch_shapes=[
            pltpu.VMEM((width, 2 * size), F32),
            pltpu.VMEM((width, 2 * size), F32),
            pltpu.VMEM((width, 2 * size), F32),
            pltpu.VMEM((height, tile), F32),
            pltpu.VMEM((size, 2 * size), F32),
            pltpu.VMEM((size, 2 * size), F32),
            pltpu.VMEM(observed.shape, F32),
            pltpu.SMEM((8, starts.shape[1]), jnp.int32),
            pltpu.SemaphoreType.DMA,
            pltpu.SemaphoreType.DMA((slots,)),
        ],
        compiler_params=pltpu.CompilerParams(vmem_limit_bytes=56 * 2**20),
    )(counts, starts, image, probe_wave, *tables, observed)


def collect_kernel(
    grads, pattern, out, mine, held, twin, counts, index, total, flat,
    slab_send, slab_recv, chip_send, chip_recv, pair_send, pair_recv,
):
    slab, column = lax.axis_index("slab"), lax.axis_index("col")
    chip, core = lax.div(column, 2), lax.rem(column, 2)
    sibling = (slab, 2 * chip + 1 - core)
    steps = steps_over()
    slabs, slab_rows, share, tile = grads.shape
    tile_rows, spread, angles = pattern.shape
    group, _, _ = out.shape
    tiles = out.shape[1] // slab_rows
    columns = angles * tile_rows // (slabs * share)
    greet_near(slab, chip, core)
    greeted(11)

    order = [1, 3, 4, 2, 5, 7, 6]
    slabs_, chips, pairs = {}, {}, {}
    for d in order:
        other = moved(slab, steps[d])
        slabs_[d] = remote(
            grads.at[other], mine.at[slab], slab_send.at[d], slab_recv.at[d], (other, column)
        )
        slabs_[d].start()
    mine[slab] = grads[slab]

    turned = jnp.concatenate(
        [
            pattern[:, :, base : base + tile].reshape(-1, tile).T
            for base in range(0, angles, tile)
        ],
        0,
    )
    turned = segment_of(turned, group, tiles)
    for d in range(tile_rows):
        index[pl.ds(d, angles, tile_rows), :spread] = turned[:, d * spread : (d + 1) * spread]

    for d in order:
        slabs_[d].wait_recv()
    half, quarter = slab_rows // 2, slab_rows // 4
    low, high = slice(0, half), slice(half, slab_rows)
    upper, lower = slice(half, half + quarter), slice(half + quarter, slab_rows)
    across = (slab, 2 * moved(chip, (1, 0)) + core)
    up = (slab, 2 * moved(chip, (0, 1)) + core)
    down = (slab, 2 * moved(chip, (0, 3)) + core)

    def pass_on(number, source, target, rows, device):
        chips[number] = remote(
            (mine if source == 0 else held.at[source]).at[:, rows], held.at[target, :, rows],
            chip_send.at[number], chip_recv.at[number], device,
        )
        chips[number].start()

    whole = slice(0, slab_rows)
    pass_on(0, 0, 1, whole, up)
    pass_on(1, 0, 3, whole, down)
    pass_on(2, 0, 4, whole, across)
    pairs[0] = remote(mine, twin.at[0], pair_send.at[0], pair_recv.at[0], sibling)
    pairs[0].start()

    row = lax.broadcasted_iota(jnp.int32, (tiles, 2 * slabs * share), 0).astype(I16)
    one, zero = jnp.ones(row.shape, BF16), jnp.zeros(row.shape, BF16)

    @pl.loop(0, columns // 2)
    def _(origin):
        wanted = jnp.concatenate(
            [
                index[pl.ds(pl.multiple_of((s * columns + 2 * origin + c) * share, share), share), :]
                for c in range(2)
                for s in range(slabs)
            ],
            0,
        ).T
        wide = [
            jnp.broadcast_to(wanted[member : member + 1, :], row.shape).astype(I16)
            for member in range(spread)
        ]
        for k in range(group):
            held_here = zero
            for member in range(spread):
                held_here = held_here + jnp.where(wide[member] == row + I16(k * tiles), one, zero)
            counts[origin, k * tiles : (k + 1) * tiles, :] = held_here

    def add(d, near, far):
        if d:
            origin = moved(chip, ((2 - steps[d][0]) % 2, (4 - steps[d][1]) % 4))
        else:
            origin = chip
        swapped = core == 1
        for z in range(0, slab_rows, 2):
            parts = []
            for more in range(2):
                a = near[:, z + more].reshape(slabs * share, tile)
                b = far[:, z + more].reshape(slabs * share, tile)
                parts.append(
                    jnp.concatenate([jnp.where(swapped, b, a), jnp.where(swapped, a, b)], 0)
                )
            right = jnp.concatenate(parts, 1)
            for base in range(0, group * tiles, 256):
                result = dot(counts[origin, base : base + 256, :], right)
                span = slice(base, base + 256)
                lanes = slice(z * tile, (z + 2) * tile)
                if d:
                    result = result + total[span, lanes]
                total[span, lanes] = result

    def arrived(*numbers):
        for number in numbers:
            chips[number].wait_recv()

    def to_sibling(d):
        pairs[d] = remote(held.at[d], twin.at[d], pair_send.at[d], pair_recv.at[d], sibling)
        pairs[d].start()

    def use(d):
        pairs[d].wait_recv()
        add(d, held.at[d] if d else mine, twin.at[d])

    arrived(0)
    pass_on(3, 1, 2, low, up)
    pass_on(4, 1, 5, low, across)
    to_sibling(1)
    arrived(1)
    pass_on(5, 3, 2, high, down)
    pass_on(6, 3, 7, low, across)
    to_sibling(3)
    arrived(2)
    pass_on(7, 4, 5, high, up)
    pass_on(8, 4, 7, high, down)
    to_sibling(4)
    use(0)
    arrived(3)
    pass_on(9, 2, 6, low, across)
    use(1)
    arrived(7)
    pass_on(10, 5, 6, upper, up)
    arrived(8)
    pass_on(11, 7, 6, lower, down)
    use(3)
    arrived(5)
    to_sibling(2)
    use(4)
    arrived(4)
    to_sibling(5)
    use(2)
    arrived(6)
    to_sibling(7)
    use(5)
    arrived(9, 10, 11)
    to_sibling(6)
    use(7)
    use(6)

    for k in range(group):
        for z in range(slab_rows):
            block = total[k * tiles : (k + 1) * tiles, z * tile : (z + 1) * tile]
            flat[pl.ds(z, tiles, slab_rows), :] = block
        out[k] = flat[...].astype(BF16)

    for d in order:
        slabs_[d].wait_send()
    for number in range(12):
        chips[number].wait_send()
    for d in [0] + order:
        pairs[d].wait_send()


def collect(grads, pattern, templates, tiles):
    slabs, slab_rows, share, tile = grads.shape
    group, tile_cells, _ = templates.shape
    tile_rows, spread, angles = pattern.shape
    columns = angles * tile_rows // (slabs * share)
    vector = pl.BlockSpec(memory_space=pltpu.VMEM)
    sem = pltpu.SemaphoreType.DMA((8,))
    return pl.pallas_call(
        collect_kernel,
        out_shape=jax.ShapeDtypeStruct((group, tiles * slab_rows, tile), BF16),
        in_specs=[vector, vector],
        out_specs=vector,
        scratch_shapes=[
            pltpu.VMEM(grads.shape, BF16),
            pltpu.VMEM((8,) + grads.shape, BF16),
            pltpu.VMEM((8,) + grads.shape, BF16),
            pltpu.VMEM((columns // 2, group * tiles, 2 * slabs * share), BF16),
            pltpu.VMEM((angles * tile_rows, tile), jnp.int32),
            pltpu.VMEM((group * tiles, slab_rows * tile), F32),
            pltpu.VMEM((tiles * slab_rows, tile), F32),
        ]
        + [sem, sem, pltpu.SemaphoreType.DMA((12,)), pltpu.SemaphoreType.DMA((12,)), sem, sem],
        compiler_params=pltpu.CompilerParams(
            collective_id=2, has_side_effects=True, vmem_limit_bytes=32 * 2**20
        ),
    )(grads, pattern)


def update_kernel(sums, templates, volume, consensus, out):
    group, size, tile = sums.shape
    tile_cells = templates.shape[1]
    slab_rows = volume.shape[0]
    left = jnp.concatenate([sums[k] for k in range(group)], 1)
    for part in range(0, tile_cells, 256):
        total = jnp.zeros((size, 256), F32)
        for k in range(0, group, 2):
            right = jnp.concatenate(
                [templates[k, part : part + 256, :], templates[k + 1, part : part + 256, :]], 1
            )
            total = total + lax.dot_general(
                left[:, k * tile : (k + 2) * tile],
                right,
                (((1,), (1,)), ((), ())),
                preferred_element_type=F32,
            )
        for t in range(size // slab_rows):
            span = slice(t * tile_cells + part, t * tile_cells + part + 256)
            own_volume = volume[:, span].astype(F32)
            wanted = consensus[:, span].astype(F32)
            moved_by = total[t * slab_rows : (t + 1) * slab_rows]
            out[:, span] = own_volume - step_size * (moved_by + penalty * (own_volume - wanted))


def update(sums, templates, volume, consensus):
    slab_rows, cells = volume.shape
    group, height, tile = sums.shape
    steps = 2
    block = pl.BlockSpec((slab_rows, cells // steps), lambda i: (0, i))
    return pl.pallas_call(
        update_kernel,
        grid=(steps,),
        out_shape=jax.ShapeDtypeStruct((slab_rows, cells), F32),
        in_specs=[
            pl.BlockSpec((group, height // steps, tile), lambda i: (0, i, 0)),
            pl.BlockSpec(templates.shape, lambda i: (0, 0, 0)),
            block,
            block,
        ],
        out_specs=block,
        compiler_params=pltpu.CompilerParams(vmem_limit_bytes=20 * 2**20),
    )(sums, templates, volume, consensus)


def on_device(
    volume, consensus, templates, pattern, probe_wave, measured, scan_counts, scan_positions
):
    slab_rows = volume.shape[0]
    tile = templates.shape[2]
    slab_count = lax.axis_size("slab")
    column_count = lax.axis_size("col")
    angle_count, tile_rows, spread = pattern.shape[1:]
    per_owner = angle_count // (slab_count * column_count)
    own = per_owner * tile_rows
    rows = angle_count * tile_rows

    image, observed = forward(
        volume,
        templates,
        pattern[0].transpose(1, 2, 0),
        measured.transpose(0, 2, 3, 1),
        column_count,
        slab_count,
    )
    image = image.reshape(slab_count * slab_rows * own, tile)
    gradients = ptycho(image, probe_wave, observed, scan_counts, scan_positions)
    sums = collect(
        gradients.reshape(slab_count, slab_rows, own, tile),
        pattern[0].transpose(1, 2, 0),
        templates,
        volume.shape[1] // templates.shape[1],
    )
    return update(sums, templates, volume, consensus)


def solution(mesh):
    return jax.shard_map(
        on_device,
        mesh=mesh,
        in_specs=(
            P("slab", "col"),
            P("slab", "col"),
            P("col", None, None),
            P("col", None, None, None),
            P(),
            P(("slab", "col"), None, None, None),
            P(),
            P(),
        ),
        out_specs=P("slab", "col"),
        check_vma=False,
    )
```

```python
import functools
import math

import jax
import jax.numpy as jnp
import numpy as np
from jax import lax
from jax.experimental import pallas as pl
from jax.experimental.pallas import tpu as pltpu
from jax.sharding import PartitionSpec as P

BF16 = jnp.bfloat16
F32 = jnp.float32
GROUP = 64
step_size = 0.1
penalty = 1.0
I16 = jnp.int16
TURN = 65536 / (2 * math.pi)

def dot(left, right):
    return jnp.dot(left, right, preferred_element_type=F32)


def steps_over():
    return [(dx, dy) for dx in range(2) for dy in range(4)]


def moved(index, step):
    high, low = lax.div(index, 4), lax.rem(index, 4)
    return lax.rem(high + step[0], 2) * 4 + lax.rem(low + step[1], 4)


def greet_near(slab, chip, core):
    barrier = pltpu.get_barrier_semaphore()
    column = 2 * chip + core
    others = [(slab, 2 * chip + 1 - core)]
    others += [(slab, 2 * moved(chip, step) + core) for step in ((0, 1), (0, 3), (1, 0))]
    others += [(moved(slab, step), column) for step in steps_over()[1:]]
    for other in others:
        pl.semaphore_signal(barrier, inc=1, device_id=other, device_id_type=pl.DeviceIdType.MESH)


def greeted(number):
    pl.semaphore_wait(pltpu.get_barrier_semaphore(), number)


def remote(source, target, send, receive, device):
    return pltpu.make_async_remote_copy(
        src_ref=source,
        dst_ref=target,
        send_sem=send,
        recv_sem=receive,
        device_id=device,
        device_id_type=pl.DeviceIdType.MESH,
    )


def segment_of(entry, group, tiles):
    return (entry & (group - 1)) * tiles + lax.div(entry, group)


def forward_kernel(
    volume_in, templates_in, pattern, measured_in, image, observed,
    volume, templates, measured, turned_over, flat, table, counts, index, own, outgoing, pair, from_y, from_x, total,
    load_sem, pair_send, pair_recv, x_send, x_recv, y_send, y_recv, slab_send, slab_recv,
):
    slab, column = lax.axis_index("slab"), lax.axis_index("col")
    chip, core = lax.div(column, 2), lax.rem(column, 2)
    slabs, slab_rows, share, tile = image.shape
    columns = 2 * own.shape[0]
    group, tile_cells, _ = templates.shape
    tiles = table.shape[0] // group
    tile_rows, spread, angles = pattern.shape
    half = measured.shape[1] // 2
    limit = measured.shape[3]
    quarter = volume.shape[1] // 4
    greet_near(slab, chip, core)

    loads = [pltpu.make_async_copy(templates_in, templates, load_sem.at[0])]
    for part in range(4):
        span = pl.ds(part * quarter, quarter)
        loads.append(
            pltpu.make_async_copy(volume_in.at[:, span], volume.at[:, span], load_sem.at[1 + part])
        )
    loads.append(pltpu.make_async_copy(measured_in, measured, load_sem.at[5]))
    for load in loads:
        load.start()

    turned = jnp.concatenate(
        [
            pattern[:, :, base : base + tile].reshape(-1, tile).T
            for base in range(0, angles, tile)
        ],
        0,
    )
    turned = segment_of(turned, group, tiles)
    for d in range(tile_rows):
        index[pl.ds(d, angles, tile_rows), :spread] = turned[:, d * spread : (d + 1) * spread]

    loads[0].wait()
    step = tiles // 4
    for part in range(4):
        loads[1 + part].wait()
        left = jnp.concatenate(
            [
                volume[:, t * tile_cells : (t + 1) * tile_cells].astype(F32)
                for t in range(part * step, (part + 1) * step)
            ],
            0,
        ).astype(BF16)
        span = slice(part * step * slab_rows, (part + 1) * step * slab_rows)
        for k in range(0, group, 2):
            result = dot(left, jnp.concatenate([templates[k], templates[k + 1]], 1))
            flat[k, span, :] = result[:, :tile]
            flat[k + 1, span, :] = result[:, tile:]
    for k in range(group):
        for z in range(slab_rows):
            block = flat[k, pl.ds(z, tiles, slab_rows), :]
            table[k * tiles : (k + 1) * tiles, z * tile : (z + 1) * tile] = block.astype(BF16)

    greeted(11)
    lane = lax.broadcasted_iota(jnp.int32, (2 * slabs * share, tiles), 1).astype(I16)
    one, zero = jnp.ones(lane.shape, BF16), jnp.zeros(lane.shape, BF16)

    quarter_rows = slab_rows // 4
    low, high = slice(0, slab_rows // 2), slice(slab_rows // 2, slab_rows)
    across = (slab, 2 * moved(chip, (1, 0)) + core)

    def along(dy):
        return (slab, 2 * (4 * lax.div(chip, 4) + lax.rem(chip + dy, 4)) + core)

    def to_pair(d):
        return remote(
            outgoing.at[d], pair.at[d], pair_send.at[d], pair_recv.at[d],
            (slab, 2 * chip + 1 - core),
        )

    def low_across(dy):
        return remote(
            own.at[4 + dy, low], from_x.at[dy, low], x_send.at[dy], x_recv.at[dy], across
        )

    def low_along(dy):
        return remote(own.at[dy, low], from_y.at[dy, low], y_send.at[dy], y_recv.at[dy], along(dy))

    def high_along(d, dy):
        return remote(
            own.at[d, high], from_y.at[d, high], y_send.at[8 + d], y_recv.at[8 + d], along(dy)
        )

    def relay(d, side, dy):
        begin = side * (slab_rows // 2) + (dy // 2) * quarter_rows
        rows = slice(begin, begin + quarter_rows)
        number = 16 + 4 * lax.div(d, 4) + 2 * side + dy // 2
        return remote(
            own.at[d, rows], from_y.at[d, rows], y_send.at[number], y_recv.at[number], along(dy)
        )

    def take(d, side, dy):
        middle = d - dy + 2
        relay(middle, side, dy).wait_recv()
        begin = side * (slab_rows // 2) + (dy // 2) * quarter_rows

        @pl.loop(begin, begin + quarter_rows, unroll=True)
        def _(z):
            own[d, z] = own[d, z] + from_y[middle, z]

    def high_across():
        return remote(own.at[4, high], from_x.at[0, high], x_send.at[4], x_recv.at[4], across)

    def compute(d):
        ahead = lax.rem(lax.div(chip, 4) + lax.div(d, 4), 2)
        target = 4 * ahead + lax.rem(chip + d, 4)
        wanted = jnp.concatenate(
            [
                index[pl.ds(pl.multiple_of((s * columns + 2 * target + c) * share, share), share), :]
                for c in (core, 1 - core)
                for s in range(slabs)
            ],
            0,
        )
        wide = [
            jnp.broadcast_to(wanted[:, member : member + 1], lane.shape).astype(I16)
            for member in range(spread)
        ]
        for k in range(group):
            held = zero
            for member in range(spread):
                held = held + jnp.where(wide[member] == lane + I16(k * tiles), one, zero)
            counts[:, k * tiles : (k + 1) * tiles] = held
        for z in range(0, slab_rows, 2):
            result = dot(counts[...], table[:, z * tile : (z + 2) * tile])
            result = jnp.floor(result * TURN + 0.5).astype(jnp.int32).astype(I16)
            for more in range(2):
                part = result[:, more * tile : (more + 1) * tile]
                own[d, z + more] = part[: slabs * share].reshape(slabs, share, tile)
                outgoing[d, z + more] = part[slabs * share :].reshape(slabs, share, tile)
        to_pair(d).start()

    def add_pair(d):
        to_pair(d).wait_recv()

        @pl.loop(0, slab_rows, unroll=True)
        def _(z):
            own[d, z] = own[d, z] + pair[d, z]

    def add_low(dy):
        low_across(dy).wait_recv()

        @pl.loop(0, slab_rows // 2, unroll=True)
        def _(z):
            own[dy, z] = own[dy, z] + from_x[dy, z]

    def send_relays(d, side):
        for way in (1, 3):
            relay(d, side, way).start()

    def finish_high(d, way):
        take(d, 1, way)
        high_along(d, way).start()

    def finish_low(way):
        add_low(way)
        take(way, 0, way)
        low_along(way).start()

    def turn_corner():
        for dy in (1, 3):
            high_along(4 + dy, dy).wait_recv()

        @pl.loop(slab_rows // 2, slab_rows, unroll=True)
        def _(z):
            own[4, z] = own[4, z] + from_y[5, z] + from_y[7, z]

        high_across().start()

    plan = {
        1: [lambda: low_across(2).start(), lambda: send_relays(6, 1)],
        2: [lambda: send_relays(2, 1)],
        3: [lambda: low_across(1).start(), lambda: finish_high(5, 1)],
        4: [
            lambda: low_across(3).start(),
            lambda: finish_high(7, 3),
            lambda: add_low(2),
            lambda: send_relays(2, 0),
        ],
        5: [lambda: low_across(0).start()],
        6: [lambda: finish_high(1, 1), lambda: finish_low(1)],
        7: [lambda: finish_high(3, 3), lambda: finish_low(3), turn_corner],
        8: [lambda: add_low(0)],
    }
    sequence = (6, 2, 5, 7, 4, 1, 3, 0)

    def work(i, carry):
        rest, previous = carry
        d = lax.rem(rest, 8)

        @pl.when(i < 8)
        def _():
            compute(d)

        @pl.when(i > 0)
        def _():
            add_pair(previous)

        for number, actions in plan.items():

            @pl.when(i == number)
            def _():
                for action in actions:
                    action()

        return lax.div(rest, 8), d

    lax.fori_loop(0, 9, work, (sum(d * 8**n for n, d in enumerate(sequence)), 0))

    loads[5].wait()
    stores = []
    for slot in range(measured.shape[0]):

        @pl.loop(0, half, unroll=4)
        def _(row):
            both = jnp.concatenate([measured[slot, row], measured[slot, row + half]], 0)
            turned_over[slot, pl.ds(row, limit, half), :] = both.T

        stores.append(
            pltpu.make_async_copy(turned_over.at[slot], observed.at[slot], load_sem.at[6 + slot])
        )
        stores[-1].start()

    def to_slab(d, part):
        other = moved(slab, steps_over()[d])
        side = (low, high)[part]
        number = 8 * part + d
        return remote(
            total.at[other, side], image.at[slab, side], slab_send.at[number], slab_recv.at[number],
            (other, column),
        )

    for part in range(2):
        for dy in (1, 3):
            if part:
                high_along(dy, dy).wait_recv()
            else:
                low_along(dy).wait_recv()
        if part:
            high_across().wait_recv()

        @pl.loop(part * slab_rows // 2, (part + 1) * slab_rows // 2, unroll=True)
        def _(z):
            value = own[0, z] + from_y[1, z] + from_y[3, z]
            if part:
                value = value + from_x[0, z]
            total[:, z] = value

        for d in range(1, 8):
            to_slab(d, part).start()

    image[slab] = total[slab]
    for d in range(8):
        to_pair(d).wait_send()
    for dy in range(4):
        low_across(dy).wait_send()
    for dy in (1, 3):
        low_along(dy).wait_send()
        high_along(dy, dy).wait_send()
        high_along(4 + dy, dy).wait_send()
        relay(2, 0, dy).wait_send()
        relay(2, 1, dy).wait_send()
        relay(6, 1, dy).wait_send()
    high_across().wait_send()
    for part in range(2):
        for d in range(1, 8):
            to_slab(d, part).wait()
    for copy in stores:
        copy.wait()


def forward(volume, templates, pattern, measured, columns, slabs):
    slab_rows, cells = volume.shape
    group, tile_cells, tile = templates.shape
    tiles = cells // tile_cells
    tile_rows, spread, angles = pattern.shape
    slots, size, _, limit = measured.shape
    rows = angles * tile_rows
    share = rows // (columns * slabs)
    block = (columns // 2, slab_rows, slabs, share, tile)
    vector = pl.BlockSpec(memory_space=pltpu.VMEM)
    anywhere = pl.BlockSpec(memory_space=pl.ANY)
    sem = pltpu.SemaphoreType.DMA((8,))
    return pl.pallas_call(
        forward_kernel,
        out_shape=(
            jax.ShapeDtypeStruct((slabs, slab_rows, share, tile), I16),
            jax.ShapeDtypeStruct((slots, limit * size // 2, 2 * size), F32),
        ),
        in_specs=[anywhere, anywhere, vector, anywhere],
        out_specs=(vector, anywhere),
        scratch_shapes=[
            pltpu.VMEM(volume.shape, BF16),
            pltpu.VMEM(templates.shape, BF16),
            pltpu.VMEM(measured.shape, F32),
            pltpu.VMEM((slots, limit * size // 2, 2 * size), F32),
            pltpu.VMEM((group, tiles * slab_rows, tile), F32),
            pltpu.VMEM((group * tiles, slab_rows * tile), BF16),
            pltpu.VMEM((2 * slabs * share, group * tiles), BF16),
            pltpu.VMEM((rows, tile), jnp.int32),
        ]
        + [pltpu.VMEM(block, I16)] * 4
        + [pltpu.VMEM((4,) + block[1:], I16)]
        + [pltpu.VMEM((slabs, slab_rows, share, tile), I16)]
        + [sem] * 5
        + [pltpu.SemaphoreType.DMA((24,))] * 4,
        compiler_params=pltpu.CompilerParams(
            collective_id=1, has_side_effects=True, vmem_limit_bytes=56 * 2**20
        ),
    )(volume, templates, pattern, measured)


def trig_coefficients():
    grid = (np.cos(np.pi * (np.arange(400) + 0.5) / 400) + 1.0) * (np.pi * np.pi * 0.5005)
    root = np.sqrt(grid)
    sine = np.polynomial.Polynomial.fit(grid, np.sin(root) / root, 6).convert().coef
    cosine = np.polynomial.Polynomial.fit(grid, np.cos(root), 7).convert().coef
    return [float(v) for v in sine], [float(v) for v in cosine]


def sine_cosine(angle):
    sine, cosine = trig_coefficients()
    square = angle * angle
    sine_value = jnp.full_like(square, sine[-1])
    for value in sine[-2::-1]:
        sine_value = sine_value * square + value
    cosine_value = jnp.full_like(square, cosine[-1])
    for value in cosine[-2::-1]:
        cosine_value = cosine_value * square + value
    return sine_value * angle, cosine_value


def split_bf16(table):
    high = table.astype(np.float32).astype(BF16)
    low = (table - high.astype(np.float64)).astype(np.float32).astype(BF16)
    return high, low


def transform_tables(size):
    index = np.arange(size)
    radians = 2.0 * np.pi / size * (index[:, None] * index[None, :] % size)
    cosine = np.cos(radians) / math.sqrt(size)
    sine = np.sin(radians) / math.sqrt(size)
    zero = np.zeros_like(cosine)
    forward = np.block([[cosine, -sine], [sine, cosine]])
    pair = np.block([[cosine, zero, sine, zero], [zero, cosine, zero, sine]])
    back = np.block([[2 * sine, -2 * cosine], [2 * cosine, 2 * sine]])
    f_high, f_low = split_bf16(forward)
    p_high, p_low = split_bf16(pair)
    b_high, b_low = split_bf16(back)
    lanes = np.concatenate([f_high, f_low], 1)
    back = np.concatenate([b_high, b_low], 1)
    return (
        np.concatenate([lanes, lanes], 0),
        np.concatenate([p_high, p_high], 0),
        np.concatenate([p_high, p_low], 0),
        np.concatenate([back, back], 0),
    )


def halves(value):
    high = value.astype(BF16)
    low = (value - high.astype(F32)).astype(BF16)
    return high, low


def ptycho_kernel(
    counts, starts_in, image, probe_wave, t_first, t_pair, t_pair_both, t_back, observed_in,
    out, waves, swapped, total, staged, probe_a, probe_b, observed, starts, landed, here,
):
    slots = observed.shape[0]
    size = probe_wave.shape[1]
    limit = starts.shape[1]
    owner = lax.axis_index("slab") * lax.axis_size("col") + lax.axis_index("col")
    first_angle = owner * slots
    first_row = lax.div(first_angle, 8) * 8
    load = pltpu.make_async_copy(starts_in.at[pl.ds(pl.multiple_of(first_row, 8), 8)], starts, landed)
    load.start()
    fetches = [
        pltpu.make_async_copy(observed_in.at[slot], observed.at[slot], here.at[slot])
        for slot in range(slots)
    ]
    for fetch in fetches:
        fetch.start()
    both = jnp.concatenate([probe_wave[0], probe_wave[0]], 0)
    probe_a[...] = both.T
    both = jnp.concatenate([-probe_wave[1], probe_wave[1]], 0)
    probe_b[...] = both.T
    width = waves.shape[0]
    tile = image.shape[1]
    rows = width // tile * slots
    chunk_count = limit // GROUP

    def used_chunks(slot):
        return jnp.clip(lax.div(counts[first_angle + slot] + (GROUP - 1), GROUP), 0, chunk_count)

    half = size // 2

    staged[...] = image[...].astype(jnp.int32).astype(F32) * (2 * math.pi / 65536)
    load.wait()
    lane = lax.broadcasted_iota(jnp.int32, (size, 2 * size), 1)

    @pl.loop(0, slots)
    def _(slot):
        pltpu.make_async_copy(observed_in.at[slot], observed.at[slot], here.at[slot]).wait()
        for part in range(width // tile):
            sine, cosine = sine_cosine(staged[pl.ds(slot * (width // tile) + part, size, rows), :])
            waves[part * tile : (part + 1) * tile, :] = jnp.concatenate([cosine, sine], 0).T
            swapped[part * tile : (part + 1) * tile, :] = jnp.concatenate([sine, cosine], 0).T
        total[...] = jnp.zeros_like(total)
        count = counts[first_angle + slot]

        @pl.loop(0, used_chunks(slot))
        def _(chunk):
            begin = chunk * GROUP
            at = [starts[first_angle - first_row + slot, begin + member] for member in range(GROUP)]
            exits = []
            for member in range(GROUP):
                patch = waves[pl.ds(at[member], size), :]
                exits.append(probe_a[...] * patch + probe_b[...] * swapped[pl.ds(at[member], size), :])
            exit_wave = jnp.concatenate(exits, 0)
            high, low = halves(exit_wave)
            first = dot(jnp.concatenate([high, low], 1), t_first[...])
            first = first[:, : 2 * size] + first[:, 2 * size :]
            turned = jnp.concatenate(
                [first[pair * 2 * size : (pair + 1) * 2 * size].T for pair in range(GROUP // 2)], 0
            )
            high, low = halves(turned)
            second = dot(jnp.concatenate([high, low], 1), t_pair[...])
            second = second + dot(high, t_pair_both[2 * size :, :])
            scaled = []
            for pair in range(GROUP // 2):
                block = second[pair * 2 * size : (pair + 1) * 2 * size]
                real = block[:size, : 2 * size] + block[size:, 2 * size :]
                imag = block[size:, : 2 * size] - block[:size, 2 * size :]
                member = begin + 2 * pair
                seen = [
                    observed[slot, pl.ds(pl.multiple_of((member + m) * half, half), half), :]
                    for m in range(2)
                ]
                seen = jnp.concatenate(
                    [
                        jnp.concatenate([seen[0][:, :size], seen[1][:, :size]], 1),
                        jnp.concatenate([seen[0][:, size:], seen[1][:, size:]], 1),
                    ],
                    0,
                )
                residual = real * real + imag * imag - seen
                live = member + jnp.where(lane >= size, 1, 0) < count
                residual = jnp.where(live, residual, 0.0)
                scaled += [residual * real, residual * imag]
            scaled = jnp.concatenate(scaled, 0).astype(BF16)
            third = dot(jnp.concatenate([scaled, scaled], 1), t_pair_both[...])
            turned = []
            for pair in range(GROUP // 2):
                block = third[pair * 2 * size : (pair + 1) * 2 * size]
                real = block[:size, : 2 * size] - block[size:, 2 * size :]
                imag = block[size:, : 2 * size] + block[:size, 2 * size :]
                turned.append(jnp.concatenate([real, imag], 0).T)
            high, low = halves(jnp.concatenate(turned, 0))
            back = dot(jnp.concatenate([high, low], 1), t_back[...])
            gradient = exit_wave * (back[:, : 2 * size] + back[:, 2 * size :])
            for member in range(GROUP):
                span = pl.ds(at[member], size)
                total[span, :] = total[span, :] + gradient[member * size : (member + 1) * size]

        for part in range(width // tile):
            flat = total[part * tile : (part + 1) * tile, :].T
            staged[pl.ds(slot * (width // tile) + part, size, rows), :] = flat[:size] + flat[size:]

    out[...] = staged[...].astype(BF16)


def ptycho(image, probe_wave, observed, counts, starts):
    slots = observed.shape[0]
    size = probe_wave.shape[1]
    height, tile = image.shape
    width = height // size // slots * tile
    tables = [jnp.asarray(table) for table in transform_tables(size)]
    vector = pl.BlockSpec(memory_space=pltpu.VMEM)
    return pl.pallas_call(
        ptycho_kernel,
        out_shape=jax.ShapeDtypeStruct((height, tile), BF16),
        in_specs=[pl.BlockSpec(memory_space=pltpu.SMEM), pl.BlockSpec(memory_space=pl.ANY)]
        + [vector] * 6
        + [pl.BlockSpec(memory_space=pl.ANY)],
        out_specs=vector,
        scratch_shapes=[
            pltpu.VMEM((width, 2 * size), F32),
            pltpu.VMEM((width, 2 * size), F32),
            pltpu.VMEM((width, 2 * size), F32),
            pltpu.VMEM((height, tile), F32),
            pltpu.VMEM((size, 2 * size), F32),
            pltpu.VMEM((size, 2 * size), F32),
            pltpu.VMEM(observed.shape, F32),
            pltpu.SMEM((8, starts.shape[1]), jnp.int32),
            pltpu.SemaphoreType.DMA,
            pltpu.SemaphoreType.DMA((slots,)),
        ],
        compiler_params=pltpu.CompilerParams(vmem_limit_bytes=56 * 2**20),
    )(counts, starts, image, probe_wave, *tables, observed)


def collect_kernel(
    grads, pattern, out, mine, held, twin, counts, index, total, flat,
    slab_send, slab_recv, chip_send, chip_recv, pair_send, pair_recv,
):
    slab, column = lax.axis_index("slab"), lax.axis_index("col")
    chip, core = lax.div(column, 2), lax.rem(column, 2)
    sibling = (slab, 2 * chip + 1 - core)
    steps = steps_over()
    slabs, slab_rows, share, tile = grads.shape
    tile_rows, spread, angles = pattern.shape
    group, _, _ = out.shape
    tiles = out.shape[1] // slab_rows
    columns = angles * tile_rows // (slabs * share)
    greet_near(slab, chip, core)
    greeted(11)

    order = [1, 3, 4, 2, 5, 7, 6]
    slabs_, chips, pairs = {}, {}, {}
    for d in order:
        other = moved(slab, steps[d])
        slabs_[d] = remote(
            grads.at[other], mine.at[slab], slab_send.at[d], slab_recv.at[d], (other, column)
        )
        slabs_[d].start()
    mine[slab] = grads[slab]

    turned = jnp.concatenate(
        [
            pattern[:, :, base : base + tile].reshape(-1, tile).T
            for base in range(0, angles, tile)
        ],
        0,
    )
    turned = segment_of(turned, group, tiles)
    for d in range(tile_rows):
        index[pl.ds(d, angles, tile_rows), :spread] = turned[:, d * spread : (d + 1) * spread]

    for d in order:
        slabs_[d].wait_recv()
    half, quarter = slab_rows // 2, slab_rows // 4
    low, high = slice(0, half), slice(half, slab_rows)
    upper, lower = slice(half, half + quarter), slice(half + quarter, slab_rows)
    across = (slab, 2 * moved(chip, (1, 0)) + core)
    up = (slab, 2 * moved(chip, (0, 1)) + core)
    down = (slab, 2 * moved(chip, (0, 3)) + core)

    def pass_on(number, source, target, rows, device):
        chips[number] = remote(
            (mine if source == 0 else held.at[source]).at[:, rows], held.at[target, :, rows],
            chip_send.at[number], chip_recv.at[number], device,
        )
        chips[number].start()

    whole = slice(0, slab_rows)
    pass_on(0, 0, 1, whole, up)
    pass_on(1, 0, 3, whole, down)
    pass_on(2, 0, 4, whole, across)
    pairs[0] = remote(mine, twin.at[0], pair_send.at[0], pair_recv.at[0], sibling)
    pairs[0].start()

    row = lax.broadcasted_iota(jnp.int32, (tiles, 2 * slabs * share), 0).astype(I16)
    one, zero = jnp.ones(row.shape, BF16), jnp.zeros(row.shape, BF16)

    @pl.loop(0, columns // 2)
    def _(origin):
        wanted = jnp.concatenate(
            [
                index[pl.ds(pl.multiple_of((s * columns + 2 * origin + c) * share, share), share), :]
                for c in range(2)
                for s in range(slabs)
            ],
            0,
        ).T
        wide = [
            jnp.broadcast_to(wanted[member : member + 1, :], row.shape).astype(I16)
            for member in range(spread)
        ]
        for k in range(group):
            held_here = zero
            for member in range(spread):
                held_here = held_here + jnp.where(wide[member] == row + I16(k * tiles), one, zero)
            counts[origin, k * tiles : (k + 1) * tiles, :] = held_here

    def add(d, near, far):
        if d:
            origin = moved(chip, ((2 - steps[d][0]) % 2, (4 - steps[d][1]) % 4))
        else:
            origin = chip
        swapped = core == 1
        for z in range(0, slab_rows, 2):
            parts = []
            for more in range(2):
                a = near[:, z + more].reshape(slabs * share, tile)
                b = far[:, z + more].reshape(slabs * share, tile)
                parts.append(
                    jnp.concatenate([jnp.where(swapped, b, a), jnp.where(swapped, a, b)], 0)
                )
            right = jnp.concatenate(parts, 1)
            for base in range(0, group * tiles, 256):
                result = dot(counts[origin, base : base + 256, :], right)
                span = slice(base, base + 256)
                lanes = slice(z * tile, (z + 2) * tile)
                if d:
                    result = result + total[span, lanes]
                total[span, lanes] = result

    def arrived(*numbers):
        for number in numbers:
            chips[number].wait_recv()

    def to_sibling(d):
        pairs[d] = remote(held.at[d], twin.at[d], pair_send.at[d], pair_recv.at[d], sibling)
        pairs[d].start()

    def use(d):
        pairs[d].wait_recv()
        add(d, held.at[d] if d else mine, twin.at[d])

    arrived(0)
    pass_on(3, 1, 2, low, up)
    pass_on(4, 1, 5, low, across)
    to_sibling(1)
    arrived(1)
    pass_on(5, 3, 2, high, down)
    pass_on(6, 3, 7, low, across)
    to_sibling(3)
    arrived(2)
    pass_on(7, 4, 5, high, up)
    pass_on(8, 4, 7, high, down)
    to_sibling(4)
    use(0)
    arrived(3)
    pass_on(9, 2, 6, low, across)
    use(1)
    arrived(7)
    pass_on(10, 5, 6, upper, up)
    arrived(8)
    pass_on(11, 7, 6, lower, down)
    use(3)
    arrived(5)
    to_sibling(2)
    use(4)
    arrived(4)
    to_sibling(5)
    use(2)
    arrived(6)
    to_sibling(7)
    use(5)
    arrived(9, 10, 11)
    to_sibling(6)
    use(7)
    use(6)

    for k in range(group):
        for z in range(slab_rows):
            block = total[k * tiles : (k + 1) * tiles, z * tile : (z + 1) * tile]
            flat[pl.ds(z, tiles, slab_rows), :] = block
        out[k] = flat[...].astype(BF16)

    for d in order:
        slabs_[d].wait_send()
    for number in range(12):
        chips[number].wait_send()
    for d in [0] + order:
        pairs[d].wait_send()


def collect(grads, pattern, templates, tiles):
    slabs, slab_rows, share, tile = grads.shape
    group, tile_cells, _ = templates.shape
    tile_rows, spread, angles = pattern.shape
    columns = angles * tile_rows // (slabs * share)
    vector = pl.BlockSpec(memory_space=pltpu.VMEM)
    sem = pltpu.SemaphoreType.DMA((8,))
    return pl.pallas_call(
        collect_kernel,
        out_shape=jax.ShapeDtypeStruct((group, tiles * slab_rows, tile), BF16),
        in_specs=[vector, vector],
        out_specs=vector,
        scratch_shapes=[
            pltpu.VMEM(grads.shape, BF16),
            pltpu.VMEM((8,) + grads.shape, BF16),
            pltpu.VMEM((8,) + grads.shape, BF16),
            pltpu.VMEM((columns // 2, group * tiles, 2 * slabs * share), BF16),
            pltpu.VMEM((angles * tile_rows, tile), jnp.int32),
            pltpu.VMEM((group * tiles, slab_rows * tile), F32),
            pltpu.VMEM((tiles * slab_rows, tile), F32),
        ]
        + [sem, sem, pltpu.SemaphoreType.DMA((12,)), pltpu.SemaphoreType.DMA((12,)), sem, sem],
        compiler_params=pltpu.CompilerParams(
            collective_id=2, has_side_effects=True, vmem_limit_bytes=32 * 2**20
        ),
    )(grads, pattern)


def update_kernel(sums, templates, volume, consensus, out):
    group, size, tile = sums.shape
    tile_cells = templates.shape[1]
    slab_rows = volume.shape[0]
    left = jnp.concatenate([sums[k] for k in range(group)], 1)
    for part in range(0, tile_cells, 256):
        total = jnp.zeros((size, 256), F32)
        for k in range(0, group, 2):
            right = jnp.concatenate(
                [templates[k, part : part + 256, :], templates[k + 1, part : part + 256, :]], 1
            )
            total = total + lax.dot_general(
                left[:, k * tile : (k + 2) * tile],
                right,
                (((1,), (1,)), ((), ())),
                preferred_element_type=F32,
            )
        for t in range(size // slab_rows):
            span = slice(t * tile_cells + part, t * tile_cells + part + 256)
            own_volume = volume[:, span].astype(F32)
            wanted = consensus[:, span].astype(F32)
            moved_by = total[t * slab_rows : (t + 1) * slab_rows]
            out[:, span] = own_volume - step_size * (moved_by + penalty * (own_volume - wanted))


def update(sums, templates, volume, consensus):
    slab_rows, cells = volume.shape
    group, height, tile = sums.shape
    steps = 2
    block = pl.BlockSpec((slab_rows, cells // steps), lambda i: (0, i))
    return pl.pallas_call(
        update_kernel,
        grid=(steps,),
        out_shape=jax.ShapeDtypeStruct((slab_rows, cells), F32),
        in_specs=[
            pl.BlockSpec((group, height // steps, tile), lambda i: (0, i, 0)),
            pl.BlockSpec(templates.shape, lambda i: (0, 0, 0)),
            block,
            block,
        ],
        out_specs=block,
        compiler_params=pltpu.CompilerParams(vmem_limit_bytes=20 * 2**20),
    )(sums, templates, volume, consensus)


def on_device(
    volume, consensus, templates, pattern, probe_wave, measured, scan_counts, scan_positions
):
    slab_rows = volume.shape[0]
    tile = templates.shape[2]
    slab_count = lax.axis_size("slab")
    column_count = lax.axis_size("col")
    angle_count, tile_rows, spread = pattern.shape[1:]
    per_owner = angle_count // (slab_count * column_count)
    own = per_owner * tile_rows
    rows = angle_count * tile_rows

    image, observed = forward(
        volume,
        templates,
        pattern[0].transpose(1, 2, 0),
        measured.transpose(0, 2, 3, 1),
        column_count,
        slab_count,
    )
    image = image.reshape(slab_count * slab_rows * own, tile)
    gradients = ptycho(image, probe_wave, observed, scan_counts, scan_positions)
    sums = collect(
        gradients.reshape(slab_count, slab_rows, own, tile),
        pattern[0].transpose(1, 2, 0),
        templates,
        volume.shape[1] // templates.shape[1],
    )
    return update(sums, templates, volume, consensus)


def solution(mesh):
    return jax.shard_map(
        on_device,
        mesh=mesh,
        in_specs=(
            P("slab", "col"),
            P("slab", "col"),
            P("col", None, None),
            P("col", None, None, None),
            P(),
            P(("slab", "col"), None, None, None),
            P(),
            P(),
        ),
        out_specs=P("slab", "col"),
        check_vma=False,
    )
```
